32 devices in a mesh: nodes: 16 (over z, y, x), feat: 2 (over core).
Axes of the slice: x: 2, y: 2, z: 4, core: 2. Of those that a mesh axis runs over, the one named last changes fastest.
Arguments:
- grid_in: bfloat16 [4, 8192, 227], P(None, ('nodes', 'feat')), may hold values from -6 to 6
- targets: bfloat16 [4, 8192, 227], P(None, ('nodes', 'feat')), may hold values from -6 to 6
- area_weight: float32 [4, 8192], P(None, ('nodes', 'feat')), may hold values from 0.2 to 1
- grid_count: int32 [4, 16], P(None, 'nodes'), may hold values from 1 to 512, as said below
- g2m_edges: int32 [2, 32768], P(None, 'nodes'), may hold values from 0 to 1535, as said below
- mesh_edges: int32 [2, 81920], P(None, 'nodes'), may hold values from 0 to 1919, as said below
- m2g_edges: int32 [2, 49152], P(None, 'nodes'), may hold values from 0 to 1919, as said below
- edge_count: int32 [3, 16], P(None, 'nodes'), may hold values from 1024 to 5120, as said below
- embed_weight: float32 [227, 512], P(None, ('nodes', 'feat')), may hold values from -0.375 to 0.375
- embed_first: float32 [227, 512], P(None, ('nodes', 'feat')), may hold values from -0.0017089844 to 0.0017089844
- embed_second: float32 [227, 512], P(None, ('nodes', 'feat')), may hold values from 5.452073e-08 to 2.1487583e-07
- node_mats: float32 [11, 512, 512], P(None, ('nodes', 'feat')), may hold values from -0.25 to 0.25
- mats_first: float32 [11, 512, 512], P(None, ('nodes', 'feat')), may hold values from -0.0017089844 to 0.0017089844
- mats_second: float32 [11, 512, 512], P(None, ('nodes', 'feat')), may hold values from 5.452073e-08 to 2.1487583e-07
- head_weight: float32 [512, 227], P(('nodes', 'feat')), may hold values from -0.25 to 0.25
- head_first: float32 [512, 227], P(('nodes', 'feat')), may hold values from -0.0017089844 to 0.0017089844
- head_second: float32 [512, 227], P(('nodes', 'feat')), may hold values from 5.452073e-08 to 2.1487583e-07
- norm_gains: float32 [4, 512], P(None, ('nodes', 'feat'))
- gains_first: float32 [4, 512], P(None, ('nodes', 'feat')), may hold values from -0.0068359375 to 0.0068359375
- gains_second: float32 [4, 512], P(None, ('nodes', 'feat')), may hold values from 8.659175e-07 to 3.431599e-06
Outputs:
- loss_sum: float32 [], replicated
- weight_sum: float32 [], replicated
- grad_norm: float32 [], replicated
- embed_new: float32 [227, 512], P(None, ('nodes', 'feat'))
- embed_moment: float32 [227, 512], P(None, ('nodes', 'feat'))
- embed_square: float32 [227, 512], P(None, ('nodes', 'feat'))
- embed_copy: bfloat16 [227, 512], P(None, ('nodes', 'feat'))
- mats_new: float32 [11, 512, 512], P(None, ('nodes', 'feat'))
- mats_moment: float32 [11, 512, 512], P(None, ('nodes', 'feat'))
- mats_square: float32 [11, 512, 512], P(None, ('nodes', 'feat'))
- mats_copy: bfloat16 [11, 512, 512], P(None, ('nodes', 'feat'))
- head_new: float32 [512, 227], P(('nodes', 'feat'))
- head_moment: float32 [512, 227], P(('nodes', 'feat'))
- head_square: float32 [512, 227], P(('nodes', 'feat'))
- head_copy: bfloat16 [512, 227], P(('nodes', 'feat'))
- gains_new: float32 [4, 512], P(None, ('nodes', 'feat'))
- gains_moment: float32 [4, 512], P(None, ('nodes', 'feat'))
- gains_square: float32 [4, 512], P(None, ('nodes', 'feat'))
- gains_copy: bfloat16 [4, 512], P(None, ('nodes', 'feat'))
The draws below stay inside these ranges and needn't reach their ends.
Inputs may be any that keep to these rules, and one draw needn't show every extreme that they name: `grid_count`: each block's live cell slots are a prefix of its 512 slots; the last block has all of them live. `g2m_edges`: row 0 is a sender in rim coordinates: 0 to 511 the previous block (wrapping), 512 to 1023 the own block, then the next block; row 1 is a mesh node of the own block. `mesh_edges`: row 0 is a mesh sender in rim coordinates over the previous, own and next blocks of 640; row 1 a mesh node of the own block. `m2g_edges`: row 0 is a mesh sender in rim coordinates over the previous, own and next blocks of 640; row 1 a cell of the own block. `edge_count`: row 0 counts g2m slots (at most 2048), row 1 mesh slots (at most 5120), row 2 m2g slots (at most 3072); live slots are a prefix, at least half of a block's slots, and in each row some block has all slots live.
All inputs are finite; a program needn't handle non-finite values.
Results may differ from the reference program's by a relative error of at most 0.0044.
The reference program's roundings to bfloat16 on the way (of `agg`) count: a program that leaves them out, or rounds other values in their place, can miss the bound.
Values may be sent and summed in bfloat16 or wider, within the bound.
A program may use at most 256 MiB of HBM per device.

```python
import math
import jax
import jax.numpy as jnp
from jax import lax

D = 512
V = 227
G_DEV = 512
M_DEV = 640
EG_DEV = 2048
EM_DEV = 5120
ED_DEV = 3072
MICRO = 4
STEP = 5
NG = 8192
N_NODES = 16


def draw_grid_count(key, part):
    key = jax.random.fold_in(key, 11)
    place = jnp.arange(N_NODES, dtype=jnp.int32)
    base = G_DEV // 3 + (G_DEV - G_DEV // 3) * place // max(N_NODES - 1, 1)
    jitter = jax.random.randint(key, (MICRO, N_NODES), 0, max(G_DEV // 8, 1) + 1)
    count = jnp.maximum(base[None, :] - jitter, 1)
    count = jnp.where(place[None, :] == N_NODES - 1, G_DEV, count)
    return count.astype(jnp.int32)


def draw_edge_count(key, part):
    key = jax.random.fold_in(key, 12)
    most = jnp.array([EG_DEV, EM_DEV, ED_DEV], dtype=jnp.int32)[:, None]
    count = jax.random.randint(key, (3, N_NODES), most // 2, most + 1)
    pick = jax.random.randint(jax.random.fold_in(key, 1), (3, 1), 0, N_NODES)
    full = jnp.arange(N_NODES, dtype=jnp.int32)[None, :] == pick
    return jnp.where(full, most, count).astype(jnp.int32)


def edge_list(key, per, source_rows, target_rows):
    total = N_NODES * per
    side = jax.random.randint(key, (total,), 0, 4)
    region = jnp.where(side == 0, 0, jnp.where(side == 3, 2, 1))
    row = jax.random.randint(jax.random.fold_in(key, 1), (total,), 0, source_rows)
    target = jax.random.randint(jax.random.fold_in(key, 2), (total,), 0, target_rows)
    return jnp.stack([region * source_rows + row, target]).astype(jnp.int32)


def draw_g2m_edges(key, part):
    key = jax.random.fold_in(key, 21)
    return edge_list(key, EG_DEV, G_DEV, M_DEV)


def draw_mesh_edges(key, part):
    key = jax.random.fold_in(key, 22)
    return edge_list(key, EM_DEV, M_DEV, M_DEV)


def draw_m2g_edges(key, part):
    key = jax.random.fold_in(key, 23)
    return edge_list(key, ED_DEV, M_DEV, G_DEV)


def draw_norm_gains(key, part):
    key = jax.random.fold_in(key, 31)
    position = jnp.arange(D, dtype=jnp.float32) / D
    rise = 0.7 * (1.0 + 2.0 * position)
    noise = jnp.clip(1.0 + 0.2 * jax.random.normal(key, (4, D)), 0.4, 1.6)
    return (rise[None, :] * noise).astype(jnp.float32)


def levels(own_key, dims, pieces, least, largest):
    def one(dim, blocks):
        heights = jax.random.uniform(jax.random.fold_in(jax.random.fold_in(own_key, 6), dim), (blocks,), jnp.float32, least / len(pieces), largest / len(pieces))
        return jnp.repeat(jnp.exp(heights), dims[dim] // blocks).reshape((-1,) + (1,) * (len(dims) - dim - 1))

    level = one(*pieces[0])
    for cut in pieces[1:]:
        level = level * one(*cut)
    return level


def gaussian(rng, extent, scale, bound, shards=(), kind=jnp.bfloat16):
    factor_of = levels(rng, extent, shards, -0.22, 0.18) if shards else 1.0
    result = jax.random.normal(rng, extent, jnp.float32) * scale * factor_of
    return jnp.minimum(jnp.maximum(result, -bound), bound).astype(kind)


def setup_inputs(seed: int = 0) -> dict:
    seeds = jax.random.split(jax.random.key(seed), 21)
    return {
        "grid_in": gaussian(seeds[0], (MICRO, NG, V), 1.0, 6.0, ((1, 32),)),
        "targets": gaussian(seeds[1], (MICRO, NG, V), 1.0, 6.0, ((1, 32),)),
        "area_weight": jnp.clip(0.2 + 0.8 * jax.random.uniform(seeds[2], (MICRO, NG), jnp.float32) ** levels(seeds[2], (MICRO, NG), ((1, 32),), -0.2, 0.2), 0.2, 1.0),
        "grid_count": draw_grid_count(jax.random.fold_in(seeds[20], 71), 0),
        "g2m_edges": draw_g2m_edges(jax.random.fold_in(seeds[20], 71), 0),
        "mesh_edges": draw_mesh_edges(jax.random.fold_in(seeds[20], 71), 0),
        "m2g_edges": draw_m2g_edges(jax.random.fold_in(seeds[20], 71), 0),
        "edge_count": draw_edge_count(jax.random.fold_in(seeds[20], 71), 0),
        "embed_weight": gaussian(seeds[8], (V, D), V ** -0.5, 0.375, ((1, 32),), jnp.float32),
        "embed_first": gaussian(seeds[9], (V, D), (0.5 / (2 * V * D + 11 * D * D + 4 * D) ** 0.5), 0.0017089844, ((1, 32),), jnp.float32),
        "embed_second": jnp.clip(jnp.exp(math.log(2.1487582557710994e-07) - 1.3714793 * jax.random.uniform(seeds[10], (V, D), jnp.float32) ** levels(seeds[10], (V, D), ((1, 32),), -0.2, 0.2)), 5.45207292645955e-08, 2.1487582557710994e-07),
        "node_mats": gaussian(seeds[11], (11, D, D), D ** -0.5, 0.25, ((1, 32),), jnp.float32),
        "mats_first": gaussian(seeds[12], (11, D, D), (0.5 / (2 * V * D + 11 * D * D + 4 * D) ** 0.5), 0.0017089844, ((1, 32),), jnp.float32),
        "mats_second": jnp.clip(jnp.exp(math.log(2.1487582557710994e-07) - 1.3714793 * jax.random.uniform(seeds[13], (11, D, D), jnp.float32) ** levels(seeds[13], (11, D, D), ((1, 32),), -0.2, 0.2)), 5.45207292645955e-08, 2.1487582557710994e-07),
        "head_weight": gaussian(seeds[14], (D, V), D ** -0.5, 0.25, ((0, 32),), jnp.float32),
        "head_first": gaussian(seeds[15], (D, V), (0.5 / (2 * V * D + 11 * D * D + 4 * D) ** 0.5), 0.0017089844, ((0, 32),), jnp.float32),
        "head_second": jnp.clip(jnp.exp(math.log(2.1487582557710994e-07) - 1.3714793 * jax.random.uniform(seeds[16], (D, V), jnp.float32) ** levels(seeds[16], (D, V), ((0, 32),), -0.2, 0.2)), 5.45207292645955e-08, 2.1487582557710994e-07),
        "norm_gains": draw_norm_gains(jax.random.fold_in(seeds[20], 71), 0),
        "gains_first": gaussian(seeds[18], (4, D), (2.0 / (2 * V * D + 11 * D * D + 4 * D) ** 0.5), 0.0068359375, ((1, 32),), jnp.float32),
        "gains_second": jnp.clip(jnp.exp(math.log(3.4315989978495054e-06) - 1.376992 * jax.random.uniform(seeds[19], (4, D), jnp.float32) ** levels(seeds[19], (4, D), ((1, 32),), -0.2, 0.2)), 8.659175136926933e-07, 3.4315989978495054e-06),
    }


EPS_NORM = 1e-05
CLIP = 0.5
RATE = 0.04
GAIN_RATE = 0.4
BETA_ONE = 0.5
BETA_TWO = 0.6
EPS_ADAM = 1e-08
DECAY = 0.1

@jax.custom_vjp
def low(v):
    return lax.optimization_barrier(v.astype(jnp.bfloat16)).astype(jnp.float32)

@jax.custom_vjp
def low_back(v):
    return v

def low_keep(v):
    return (low(v), None)

def low_pass(kept, grad):
    return (grad,)

def back_keep(v):
    return (v, None)

def back_low(kept, grad):
    return (low(grad),)
low.defvjp(low_keep, low_pass)
low_back.defvjp(back_keep, back_low)

def matmul(a, b):
    return jnp.dot(a, b, precision=lax.Precision.HIGHEST, preferred_element_type=jnp.float32)

def norm_rows(z, gain):
    mean = lax.optimization_barrier(jnp.mean(z, axis=-1, keepdims=True))
    centred = z - mean
    spread = lax.optimization_barrier(jnp.mean(centred * centred, axis=-1, keepdims=True))
    return centred * lax.rsqrt(spread + EPS_NORM) * gain

def graph_of(edges, counts, source_rows, target_rows):
    per = edges.shape[1] // N_NODES
    slots = jnp.arange(edges.shape[1], dtype=jnp.int32)
    device = slots // per
    owner = (device + edges[0] // source_rows - 1 + N_NODES) % N_NODES
    source = (owner * source_rows + edges[0] % source_rows).astype(jnp.int32)
    target = (device * target_rows + edges[1]).astype(jnp.int32)
    live = (slots % per < counts[device]).astype(jnp.float32)
    return (source, target, live)

def spread(rows_low, graph, total):
    source, target, live = graph
    picked = low_back(rows_low)[source] * live[:, None]
    summed = jax.ops.segment_sum(picked, target, num_segments=total)
    return low_back(low(summed))

def update(index, base, agg, mats, gains):
    pre = matmul(agg, mats[index])
    if base is not None:
        pre = pre + matmul(base, mats[3 + index])
    pre = low_back(pre)
    inner = low_back(matmul(low(jax.nn.silu(pre)), mats[7 + index]))
    return norm_rows(inner, gains[index])

def batch_loss(weights, inputs, wanted, weight, encoder, processor, decoder):
    embed, mats, head, gains = weights
    mesh_total = M_DEV * N_NODES
    grid_total = G_DEV * N_NODES
    grid_hidden = low_back(matmul(inputs, embed))
    grid_low = low(grid_hidden)
    mesh = update(0, None, spread(grid_low, encoder, mesh_total), mats, gains)
    for index in (1, 2):
        mesh_low = low(mesh)
        mesh = mesh + update(index, mesh_low, spread(mesh_low, processor, mesh_total), mats, gains)
    mesh_low = low(mesh)
    grid_out = grid_hidden + update(3, grid_low, spread(mesh_low, decoder, grid_total), mats, gains)
    pred = low_back(matmul(low(grid_out), head))
    error = pred - wanted
    return jnp.sum(weight[:, None] * error * error)

def adamw(param, first, second, grad, scale, rate):
    clipped = grad * scale
    moment = BETA_ONE * first + (1.0 - BETA_ONE) * clipped
    square = BETA_TWO * second + (1.0 - BETA_TWO) * clipped * clipped
    fixed_one = moment / (1.0 - BETA_ONE ** STEP)
    fixed_two = square / (1.0 - BETA_TWO ** STEP)
    fresh = param - rate * (fixed_one / (jnp.sqrt(fixed_two) + EPS_ADAM) + DECAY * param)
    return (fresh, moment, square, fresh.astype(jnp.bfloat16))

def reference(grid_in, targets, area_weight, grid_count, g2m_edges, mesh_edges, m2g_edges, edge_count, embed_weight, embed_first, embed_second, node_mats, mats_first, mats_second, head_weight, head_first, head_second, norm_gains, gains_first, gains_second):
    encoder = graph_of(g2m_edges, edge_count[0], G_DEV, M_DEV)
    processor = graph_of(mesh_edges, edge_count[1], M_DEV, M_DEV)
    decoder = graph_of(m2g_edges, edge_count[2], M_DEV, G_DEV)
    cells = jnp.arange(G_DEV * N_NODES, dtype=jnp.int32)
    live = ((cells % G_DEV)[None, :] < grid_count[:, cells // G_DEV]).astype(jnp.float32)
    weight = area_weight * live
    inputs = grid_in.astype(jnp.float32)
    wanted = targets.astype(jnp.float32)
    step_fn = jax.checkpoint(batch_loss)

    def loss_of(params):
        weights = tuple((low(p) for p in params))

        def one(total, data):
            return (total + step_fn(weights, data[0], data[1], data[2], encoder, processor, decoder), None)
        total, _ = lax.scan(one, jnp.float32(0.0), (inputs, wanted, weight))
        return total
    params = (embed_weight, node_mats, head_weight, norm_gains)
    loss_sum, pull = jax.vjp(loss_of, params)
    grads = pull(jnp.float32(1.0))[0]
    weight_sum = jnp.sum(weight)
    grad_norm = jnp.sqrt(sum((jnp.sum(g * g) for g in grads)))
    scale = jnp.minimum(1.0, CLIP / (grad_norm + 1e-06))
    e_new, e_mom, e_sq, e_copy = adamw(embed_weight, embed_first, embed_second, grads[0], scale, RATE)
    m_new, m_mom, m_sq, m_copy = adamw(node_mats, mats_first, mats_second, grads[1], scale, RATE)
    h_new, h_mom, h_sq, h_copy = adamw(head_weight, head_first, head_second, grads[2], scale, RATE)
    g_new, g_mom, g_sq, g_copy = adamw(norm_gains, gains_first, gains_second, grads[3], scale, GAIN_RATE)
    return (loss_sum, weight_sum, grad_norm, e_new, e_mom, e_sq, e_copy, m_new, m_mom, m_sq, m_copy, h_new, h_mom, h_sq, h_copy, g_new, g_mom, g_sq, g_copy)
```

```python
import functools
import math

import jax
import jax.numpy as jnp
from jax import lax
from jax.experimental import pallas as pl
from jax.experimental.pallas import tpu as pltpu
from jax.sharding import PartitionSpec as P

M_DEV = 640
STEP = 5
MICRO = 4


EPS_NORM = 1e-05
CLIP = 0.5
RATE = 0.04
GAIN_RATE = 0.4
BETA_ONE = 0.5
BETA_TWO = 0.6
EPS_ADAM = 1e-08
DECAY = 0.1

BOTH = ("nodes", "feat")


class Plan:
    def __init__(self, nodes):
        self.nodes = nodes
        self.chips = nodes // MICRO
        self.bits = self.chips.bit_length() - 1
        width = math.isqrt(self.chips)
        self.width = width if width * width == self.chips else 0

    def device(self, m, j, c):
        return (m * self.chips + walk(j % self.chips, self.width)) * 2 + c

    def ring(self, step):
        pairs = []
        length = 2 * self.chips
        for m in range(MICRO):
            for q in range(length):
                to = (q + step) % length
                pairs.append((self.device(m, q // 2, q % 2), self.device(m, to // 2, to % 2)))
        return pairs


MESH = pl.DeviceIdType.MESH


def walk(value, width):
    if width == 0:
        return value
    row, col = value // width, value % width
    return row * width + col + (row % 2) * (width - 1 - 2 * col)


class Spot:
    def __init__(self, plan):
        me = lax.axis_index("nodes")
        self.plan = plan
        self.core = lax.axis_index("feat")
        self.z = me // plan.chips
        self.p = me % plan.chips

    def bit(self, b):
        return (self.p // (1 << b)) % 2

    def peer_z(self, d):
        return {"nodes": ((self.z + d) % MICRO) * self.plan.chips + self.p, "feat": self.core}

    def peer_bit(self, b):
        other = self.p + (1 - 2 * self.bit(b)) * (1 << b)
        return {"nodes": self.z * self.plan.chips + other, "feat": self.core}

    def in_plane(self, p, core):
        return {"nodes": self.z * self.plan.chips + p, "feat": core}

    def sibling(self):
        return self.in_plane(self.p, 1 - self.core)

    def partners(self):
        chips = self.plan.chips
        found = [self.peer_z(d) for d in range(1, MICRO)]
        for turn in range(chips):
            p = (self.p + turn) % chips
            if turn:
                found.append(self.in_plane(p, self.core))
            found.append(self.in_plane(p, 1 - self.core))
        return found

    def meet(self):
        barrier = pltpu.get_barrier_semaphore()
        found = self.partners()
        for other in found:
            pl.semaphore_signal(barrier, inc=1, device_id=other, device_id_type=MESH)
        pl.semaphore_wait(barrier, len(found))

    def held(self, done):
        bits = range(self.plan.bits - 1, -1, -1)
        return tuple(slice(None) if b in done else self.bit(b) for b in bits)


def remote(src, dst, send, recv, to):
    return pltpu.make_async_remote_copy(
        src_ref=src, dst_ref=dst, send_sem=send, recv_sem=recv, device_id=to, device_id_type=MESH
    )


def gather_kernel(
    plan,
    pack_ref,
    cells_ref,
    codes_ref,
    all_ref,
    main_ref,
    halo_ref,
    graph_ref,
    cell_hop,
    code_hop,
    own_sem,
    hop_send,
    hop_recv,
    plane_send,
    plane_recv,
    twin_send,
    twin_recv,
    move_send,
    move_recv,
):
    spot = Spot(plan)
    z, p, core = spot.z, spot.p, spot.core
    chips, bits = plan.chips, plan.bits
    groups = bits
    mats = pack_ref.shape[0] // groups
    code_rows = codes_ref.shape[0] // 2
    lanes = halo_ref.shape[-1]
    own = pltpu.make_async_copy(pack_ref, all_ref.at[(slice(None), z) + spot.held(()) + (core,)], own_sem)
    own.start()
    spot.meet()
    my_codes = codes_ref.at[pl.ds(pl.multiple_of(core * code_rows, 8), code_rows)]
    hops = []
    for d in range(1, MICRO):
        to = spot.peer_z(d)
        m = (z + d) % MICRO
        for n, (src, dst) in enumerate(
            (
                (my_codes, code_hop.at[d - 1]),
                (cells_ref.at[m], cell_hop.at[d - 1]),
                (pack_ref, all_ref.at[(slice(None), z) + spot.held(()) + (core,)]),
            )
        ):
            copy = remote(src, dst, hop_send.at[d - 1, n], hop_recv.at[d - 1, n], to)
            copy.start()
            hops.append(copy)
    quarter = p % 4
    bb, to_core = quarter % 2, quarter // 2
    slot = bb * 2 + core
    half_slot = (1 - bb) * 2 + core
    moves = []

    def move(d, n, src, dst, sem, chip, to_core):
        here = jnp.logical_and(chip == p, to_core == core)
        copy = remote(src, dst, move_send.at[d, n], sem, spot.in_plane(chip, to_core))

        @pl.when(here)
        def _():
            pltpu.make_async_copy(src, dst, sem).start()

        @pl.when(jnp.logical_not(here))
        def _():
            copy.start()

        moves.append((here, copy))

    def spread(d):
        block = ((z - d) % MICRO) * chips + p
        j = block // 4
        chip = walk(j, plan.width)
        q = (2 * j + to_core + 2 * bb - 1) % (2 * chips)
        near = walk(q // 2, plan.width)
        codes = my_codes if d == 0 else code_hop.at[d - 1]
        rows = pl.ds(pl.multiple_of(core * code_rows, 8), code_rows)
        move(d, 0, codes, graph_ref.at[bb, rows], move_recv.at[0, slot], chip, to_core)
        cells = cells_ref.at[z] if d == 0 else cell_hop.at[d - 1]
        move(
            d,
            1,
            cells.at[:, pl.ds(0, lanes)],
            halo_ref.at[1 - bb, core],
            move_recv.at[1, half_slot],
            near,
            q % 2,
        )
        move(d, 2, cells, main_ref.at[bb, core], move_recv.at[2, slot], chip, to_core)

    def region(d, done):
        return ((z - d) % MICRO,) + spot.held(done) + (core,)

    planes = {}

    def step(d, g, t):
        done = tuple((g + s) % bits for s in range(t))
        where = (pl.ds(g * mats, mats),) + region(d, done)
        copy = remote(
            all_ref.at[where],
            all_ref.at[where],
            plane_send.at[d, g, t],
            plane_recv.at[d, g, t],
            spot.peer_bit((g + t) % bits),
        )
        copy.start()
        planes[d, g, t] = copy

    twins = []
    for tick in range(MICRO + bits):
        for t in range(bits + 1):
            d = tick - t
            if d < 0 or d >= MICRO:
                continue
            if t == 0:
                if d == 0:
                    own.wait()
                else:
                    hops[3 * (d - 1)].wait_recv()
                    hops[3 * (d - 1) + 1].wait_recv()
                    hops[3 * (d - 1) + 2].wait_recv()
                spread(d)
            else:
                for g in range(groups):
                    planes[d, g, t - 1].wait_recv()
            if t < bits:
                for g in range(groups):
                    step(d, g, t)
            else:
                where = (slice(None),) + region(d, tuple(range(bits)))
                copy = remote(
                    all_ref.at[where], all_ref.at[where], twin_send.at[d], twin_recv.at[d], spot.sibling()
                )
                copy.start()
                twins.append(copy)
    for copy in hops + list(planes.values()):
        copy.wait_send()
    for copy in twins:
        copy.wait()
    for here, copy in moves:

        @pl.when(jnp.logical_not(here))
        def _():
            copy.wait_send()

    for n in range(4):
        half, side = n % 2, n // 2
        for kind, dst in enumerate(
            (
                graph_ref.at[side, pl.ds(half * code_rows, code_rows)],
                halo_ref.at[side, half],
                main_ref.at[side, half],
            )
        ):
            pltpu.make_async_copy(dst, dst, move_recv.at[kind, n]).wait()


def gather_all(plan, pack, cells, codes):
    mats, rows, width = pack.shape
    micro, half, lanes = cells.shape
    bits = plan.bits
    any_space = pl.BlockSpec(memory_space=pl.ANY)
    dma = pltpu.SemaphoreType.DMA
    return pl.pallas_call(
        functools.partial(gather_kernel, plan),
        out_shape=(
            jax.ShapeDtypeStruct((mats, MICRO) + (2,) * bits + (2, rows, width), pack.dtype),
            jax.ShapeDtypeStruct((2, 2, half, lanes), cells.dtype),
            jax.ShapeDtypeStruct((2, 2, half, lanes // 2), cells.dtype),
            jax.ShapeDtypeStruct((2,) + codes.shape, codes.dtype),
        ),
        in_specs=[any_space] * 3,
        out_specs=(any_space,) * 4,
        scratch_shapes=[
            pltpu.VMEM((MICRO - 1, half, lanes), cells.dtype),
            pltpu.VMEM((MICRO - 1, codes.shape[0] // 2, codes.shape[1]), codes.dtype),
            dma,
            dma((MICRO - 1, 3)),
            dma((MICRO - 1, 3)),
            dma((MICRO, bits, bits)),
            dma((MICRO, bits, bits)),
            dma((MICRO,)),
            dma((MICRO,)),
            dma((MICRO, 3)),
            dma((3, 4)),
        ],
        compiler_params=pltpu.CompilerParams(
            collective_id=0, has_side_effects=True, vmem_limit_bytes=48 << 20
        ),
        name="gather_all",
    )(pack, cells, codes)


def reduce_kernel(
    plan,
    grads_ref,
    low_ref,
    stats_ref,
    share_ref,
    total_ref,
    acc,
    twin_in,
    plane_out,
    plane_in,
    hop_out,
    hop_in,
    z_stats,
    plane_stats,
    twin_stats,
    own_sem,
    twin_send,
    twin_recv,
    plane_send,
    plane_recv,
    hop_send,
    hop_recv,
    stat_send,
    stat_recv,
):
    spot = Spot(plan)
    z, p, core = spot.z, spot.p, spot.core
    chips, bits = plan.chips, plan.bits
    groups = bits
    mats = grads_ref.shape[0]
    part = mats // groups
    every = (slice(None),) * bits
    order = [1, 2, 3, 0]
    owns = {}
    for d in order:
        item = (z + d) % MICRO
        owns[d] = pltpu.make_async_copy(
            grads_ref.at[(slice(None), item) + every + (core,)], acc.at[d], own_sem.at[d]
        )
        owns[d].start()
    spot.meet()
    twins = {}
    for d in order:
        item = (z + d) % MICRO
        twins[d] = remote(
            low_ref.at[(slice(None), item) + every + (1 - core,)],
            twin_in.at[d],
            twin_send.at[d],
            twin_recv.at[d],
            spot.sibling(),
        )
        twins[d].start()

    def starts(t):
        return sum(1 << (bits - 1 - s) for s in range(t))

    planes, hops = {}, []

    def send_step(d, g, t):
        done = tuple((g + s) % bits for s in range(t))
        b = (g + t) % bits
        count = 1 << (bits - 1 - t)
        at = starts(t)
        theirs = tuple(
            spot.bit(n) if n in done else (1 - spot.bit(n) if n == b else slice(None))
            for n in range(bits - 1, -1, -1)
        )

        def body(n, _):
            mat = g * part + n
            value = acc[(d, mat) + theirs]
            plane_out[d, mat, at : at + count] = value.reshape((count,) + value.shape[-2:]).astype(
                plane_out.dtype
            )
            return 0

        lax.fori_loop(0, part, body, 0)
        where = (d, pl.ds(g * part, part), pl.ds(at, count))
        planes[d, g, t] = remote(
            plane_out.at[where],
            plane_in.at[where],
            plane_send.at[d, g, t],
            plane_recv.at[d, g, t],
            spot.peer_bit(b),
        )
        planes[d, g, t].start()

    def add_step(d, g, t):
        planes[d, g, t].wait_recv()
        done = tuple((g + s) % bits for s in range(t + 1))
        count = 1 << (bits - 1 - t)
        at = starts(t)
        mine = tuple(spot.bit(n) if n in done else slice(None) for n in range(bits - 1, -1, -1))

        def body(n, _):
            mat = g * part + n
            where = (d, mat) + mine
            value = acc[where]
            came = plane_in[d, mat, at : at + count].astype(jnp.float32)
            acc[where] = value + came.reshape(value.shape)
            return 0

        lax.fori_loop(0, part, body, 0)

    for tick in range(MICRO + bits):
        for t in range(bits + 1):
            n = tick - t
            if n < 0 or n >= MICRO:
                continue
            d = order[n]
            if t == 0:
                owns[d].wait()
                twins[d].wait_recv()

                def body(mat, _):
                    acc[d, mat] = acc[d, mat] + twin_in[d, mat].astype(jnp.float32)
                    return 0

                lax.fori_loop(0, mats, body, 0)
            else:
                for g in range(groups):
                    add_step(d, g, t - 1)
            if t < bits:
                for g in range(groups):
                    send_step(d, g, t)
            elif d:

                def body(mat, _):
                    hop_out[d - 1, mat] = acc[(d, mat) + spot.held(())].astype(hop_out.dtype)
                    return 0

                lax.fori_loop(0, mats, body, 0)
                copy = remote(
                    hop_out.at[d - 1], hop_in.at[d - 1], hop_send.at[d - 1], hop_recv.at[d - 1], spot.peer_z(d)
                )
                copy.start()
                hops.append(copy)
    for copy in hops:
        copy.wait_recv()

    def body(mat, square):
        value = acc[(0, mat) + spot.held(())]
        for d in range(MICRO - 1):
            value = value + hop_in[d, mat].astype(jnp.float32)
        share_ref[mat] = value
        return square + value * value

    square = lax.fori_loop(0, mats, body, jnp.zeros(share_ref.shape[1:], jnp.float32))
    square = jnp.sum(square, axis=0, keepdims=True)
    lanes = total_ref.shape[1]
    square = sum(square[:, n : n + lanes] for n in range(0, square.shape[1], lanes))
    row = lax.broadcasted_iota(jnp.int32, total_ref.shape, 0)
    tile = jnp.where(row == 0, square, stats_ref[...])
    sends = []

    def exchange(buffer, index, targets, at):
        buffer[index] = tile
        copies = []
        for n, to in enumerate(targets):
            copy = remote(
                buffer.at[index], buffer.at[index], stat_send.at[at + n], stat_recv.at[at + n], to
            )
            copy.start()
            copies.append(copy)
        for copy in copies:
            copy.wait()
        total = buffer[0]
        for n in range(1, buffer.shape[0]):
            total = total + buffer[n]
        return total

    tile = exchange(z_stats, z, [spot.peer_z(d) for d in range(1, MICRO)], 0)
    tile = exchange(
        plane_stats, p, [spot.in_plane((p + d) % chips, core) for d in range(1, chips)], MICRO - 1
    )
    tile = exchange(twin_stats, core, [spot.sibling()], MICRO + chips - 2)
    total_ref[...] = tile
    for copy in list(twins.values()) + list(planes.values()) + hops:
        copy.wait_send()


def reduce_all(plan, grads, low, stats):
    mats, rows, width = grads.shape[0], grads.shape[-2], grads.shape[-1]
    bits, chips = plan.bits, plan.chips
    shards = (2,) * bits
    steps = chips - 1
    any_space = pl.BlockSpec(memory_space=pl.ANY)
    vmem = pl.BlockSpec(memory_space=pltpu.VMEM)
    dma = pltpu.SemaphoreType.DMA
    return pl.pallas_call(
        functools.partial(reduce_kernel, plan),
        out_shape=(
            jax.ShapeDtypeStruct((mats, rows, width), jnp.float32),
            jax.ShapeDtypeStruct(stats.shape, jnp.float32),
        ),
        in_specs=[any_space, any_space, vmem],
        out_specs=(vmem, vmem),
        scratch_shapes=[
            pltpu.VMEM((MICRO, mats) + shards + (rows, width), jnp.float32),
            pltpu.VMEM((MICRO, mats) + shards + (rows, width), low.dtype),
            pltpu.VMEM((MICRO, mats, steps, rows, width), jnp.bfloat16),
            pltpu.VMEM((MICRO, mats, steps, rows, width), jnp.bfloat16),
            pltpu.VMEM((MICRO - 1, mats, rows, width), jnp.bfloat16),
            pltpu.VMEM((MICRO - 1, mats, rows, width), jnp.bfloat16),
            pltpu.VMEM((MICRO,) + stats.shape, jnp.float32),
            pltpu.VMEM((chips,) + stats.shape, jnp.float32),
            pltpu.VMEM((2,) + stats.shape, jnp.float32),
            dma((MICRO,)),
            dma((MICRO,)),
            dma((MICRO,)),
            dma((MICRO, bits, bits)),
            dma((MICRO, bits, bits)),
            dma((MICRO - 1,)),
            dma((MICRO - 1,)),
            dma((MICRO + chips - 1,)),
            dma((MICRO + chips - 1,)),
        ],
        compiler_params=pltpu.CompilerParams(
            collective_id=1, has_side_effects=True, vmem_limit_bytes=56 << 20
        ),
        name="reduce_all",
    )(grads, low, stats)


def matmul(a, b):
    return jnp.dot(a, b, preferred_element_type=jnp.float32)


def left_dot(a, b):
    return lax.dot_general(a, b, (((0,), (0,)), ((), ())), preferred_element_type=jnp.float32)


def right_dot(a, b):
    return lax.dot_general(a, b, (((1,), (1,)), ((), ())), preferred_element_type=jnp.float32)


def norm_rows(z, gain):
    mean = jnp.mean(z, axis=-1, keepdims=True)
    centred = z - mean
    spread = jnp.mean(centred * centred, axis=-1, keepdims=True)
    return centred * lax.rsqrt(spread + EPS_NORM) * gain


def update_fwd(index, base, agg, mats, gains):
    pre = matmul(agg, mats[index])
    if base is not None:
        pre = pre + matmul(base, mats[3 + index])
    active = jax.nn.silu(pre).astype(jnp.bfloat16)
    inner = matmul(active, mats[7 + index])
    return (norm_rows(inner, gains[index]), (pre, active, inner))


def update_bwd(index, base, agg, mats, gains, kept, grad_out):
    pre, active, inner = kept
    _, pull = jax.vjp(norm_rows, inner, gains[index])
    grad_inner, grad_gain = pull(grad_out)
    inner_low = grad_inner.astype(jnp.bfloat16)
    grad_second = left_dot(active, inner_low)
    grad_active = right_dot(inner_low, mats[7 + index])
    sigma = jax.nn.sigmoid(pre)
    pre_low = (grad_active * sigma * (1.0 + pre * (1.0 - sigma))).astype(jnp.bfloat16)
    grad_first = left_dot(agg, pre_low)
    grad_agg = right_dot(pre_low, mats[index])
    grad_self = None
    grad_base = None
    if base is not None:
        grad_self = left_dot(base, pre_low)
        grad_base = right_dot(pre_low, mats[3 + index])
    return (grad_base, grad_agg, grad_first, grad_self, grad_second, grad_gain)


def adjacency(source, target, rows, columns):
    into = target[None, :] == jnp.arange(rows, dtype=jnp.int32)[:, None]
    out = source[:, None] == jnp.arange(columns, dtype=jnp.int32)[None, :]
    return matmul(into.astype(jnp.bfloat16), out.astype(jnp.bfloat16)).astype(jnp.bfloat16)


def adamw(param, first, second, grad, scale, rate):
    clipped = grad * scale
    moment = BETA_ONE * first + (1.0 - BETA_ONE) * clipped
    square = BETA_TWO * second + (1.0 - BETA_TWO) * clipped * clipped
    fixed_one = moment / (1.0 - BETA_ONE**STEP)
    fixed_two = square / (1.0 - BETA_TWO**STEP)
    fresh = param - rate * (fixed_one / (jnp.sqrt(fixed_two) + EPS_ADAM) + DECAY * param)
    return (fresh, moment, square, fresh.astype(jnp.bfloat16))


def on_device(
    plan,
    grid_in,
    targets,
    area_weight,
    grid_count,
    g2m_edges,
    mesh_edges,
    m2g_edges,
    edge_count,
    embed_weight,
    embed_first,
    embed_second,
    node_mats,
    mats_first,
    mats_second,
    head_weight,
    head_first,
    head_second,
    norm_gains,
    gains_first,
    gains_second,
):
    half, variables = grid_in.shape[1:]
    grid_rows = 2 * half
    mesh_rows = M_DEV
    lanes = -(-variables // 128) * 128
    core = lax.axis_index("feat")

    position = core * half + jnp.arange(half, dtype=jnp.int32)
    weights = jnp.where(position[None, :] < grid_count, area_weight, 0.0)
    pieces = []
    rest = weights
    for _ in range(3):
        piece = lax.reduce_precision(rest, 8, 7)
        pieces.append(piece.astype(jnp.bfloat16))
        rest = rest - piece
    cells = jnp.concatenate(
        [
            jnp.pad(grid_in, ((0, 0), (0, 0), (0, lanes - variables))),
            targets,
            jnp.pad(jnp.stack(pieces, axis=-1), ((0, 0), (0, 0), (0, lanes - variables - 3))),
        ],
        axis=-1,
    )
    last = jnp.concatenate(
        [
            jnp.pad(embed_weight.T, ((0, 0), (0, lanes - variables))),
            head_weight,
            jnp.pad(norm_gains.T, ((0, 0), (0, lanes - variables - 4))),
        ],
        axis=-1,
    )
    pack = jnp.concatenate([node_mats, last[None]]).astype(jnp.bfloat16)
    shapes = ((g2m_edges, grid_rows, mesh_rows), (mesh_edges, mesh_rows, mesh_rows), (m2g_edges, mesh_rows, grid_rows))
    codes = []
    for n, (edges, columns, _) in enumerate(shapes):
        alive = jnp.arange(edges.shape[1], dtype=jnp.int32) < edge_count[n, 0]
        codes.append(jnp.where(alive, edges[1] * (3 * columns) + edges[0], -1))
    codes = jnp.concatenate(codes).reshape(-1, 128)
    gathered, main, halo, graph = gather_all(plan, pack, cells, codes)
    width = pack.shape[2]
    full = gathered.reshape(-1, width, width)
    mats = full[:-1]
    embed = full[-1, :, :lanes]
    head = full[-1, :, lanes:]
    gains = full[-1, :, lanes + variables : lanes + variables + 4].T.astype(jnp.float32)
    main = main.reshape(-1, 2 * lanes)
    inputs = main[:, :lanes]
    wanted = main[:, lanes:]
    weight = sum(
        main[:, lanes + variables + n : lanes + variables + n + 1].astype(jnp.float32) for n in range(3)
    )
    halo = halo.reshape(2, grid_rows, lanes)
    inputs_ext = jnp.concatenate([halo[0], inputs, halo[1]])
    graph = graph.reshape(2, -1)
    graphs = []
    start = 0
    for edges, columns, rows in shapes:
        found = []
        for b in range(2):
            code = graph[b, start : start + edges.shape[1]]
            found.append(adjacency(code % (3 * columns), code // (3 * columns), rows, 3 * columns))
        graphs.append(found)
        start += edges.shape[1]
    encoder, processor, decoder = graphs

    def extended(rows):
        size = rows.shape[0] // 2
        before = lax.ppermute(rows[size:], BOTH, plan.ring(1))
        after = lax.ppermute(rows[:size], BOTH, plan.ring(-1))
        return jnp.concatenate([before, rows, after])

    def collect(graph, ext):
        size = ext.shape[0] // 4
        return jnp.concatenate(
            [matmul(graph[b], ext[b * size : (b + 3) * size]) for b in range(2)]
        ).astype(jnp.bfloat16)

    def collect_back(graph, grad_agg):
        low = grad_agg.astype(jnp.bfloat16)
        size = low.shape[0] // 2
        pieces = [left_dot(graph[b], low[b * size : (b + 1) * size]) for b in range(2)]
        rows = pieces[0].shape[0] // 3
        before = pieces[0][:rows].astype(jnp.bfloat16)
        after = pieces[1][2 * rows :].astype(jnp.bfloat16)
        from_right = lax.ppermute(before, BOTH, plan.ring(-1)).astype(jnp.float32)
        from_left = lax.ppermute(after, BOTH, plan.ring(1)).astype(jnp.float32)
        first = from_left + pieces[0][rows : 2 * rows] + pieces[1][:rows]
        second = pieces[0][2 * rows :] + pieces[1][rows : 2 * rows] + from_right
        return jnp.concatenate([first, second]).astype(jnp.bfloat16).astype(jnp.float32)

    hidden_ext = right_dot(inputs_ext, embed)
    grid_hidden = hidden_ext[grid_rows : 3 * grid_rows]
    low_ext = hidden_ext.astype(jnp.bfloat16)
    grid_low = low_ext[grid_rows : 3 * grid_rows]
    aggs = [collect(encoder, low_ext)]
    nodes, kept_first = update_fwd(0, None, aggs[0], mats, gains)
    kept = [kept_first]
    lows = [None]
    for index in (1, 2):
        mesh_low = nodes.astype(jnp.bfloat16)
        lows.append(mesh_low)
        aggs.append(collect(processor, extended(mesh_low)))
        branch, kept_now = update_fwd(index, mesh_low, aggs[index], mats, gains)
        kept.append(kept_now)
        nodes = nodes + branch
    aggs.append(collect(decoder, extended(nodes.astype(jnp.bfloat16))))
    branch, kept_now = update_fwd(3, grid_low, aggs[3], mats, gains)
    kept.append(kept_now)
    out_low = (grid_hidden + branch).astype(jnp.bfloat16)
    error = matmul(out_low, head) - wanted.astype(jnp.float32)
    error = jnp.where(jnp.arange(lanes) < variables, error, 0.0)
    loss_local = jnp.sum(weight * error * error)
    weight_local = jnp.sum(weight)
    grad_pred = (2.0 * weight * error).astype(jnp.bfloat16)
    grad_head = left_dot(out_low, grad_pred)
    grad_grid = right_dot(grad_pred, head)
    pieces = [None] * 11
    gain_grads = [None] * 4
    grad_base, grad_agg, pieces[3], pieces[6], pieces[10], gain_grads[3] = update_bwd(
        3, grid_low, aggs[3], mats, gains, kept[3], grad_grid
    )
    grad_grid = grad_grid + grad_base
    grad_nodes = collect_back(decoder, grad_agg)
    for index in (2, 1):
        (
            grad_base,
            grad_agg,
            pieces[index],
            pieces[3 + index],
            pieces[7 + index],
            gain_grads[index],
        ) = update_bwd(index, lows[index], aggs[index], mats, gains, kept[index], grad_nodes)
        grad_nodes = grad_nodes + grad_base + collect_back(processor, grad_agg)
    _, grad_agg, pieces[0], _, pieces[7], gain_grads[0] = update_bwd(
        0, None, aggs[0], mats, gains, kept[0], grad_nodes
    )
    grad_grid = grad_grid + collect_back(encoder, grad_agg)
    grad_embed = left_dot(grad_grid.astype(jnp.bfloat16), inputs)
    gain_part = jnp.pad(jnp.stack(gain_grads).T, ((0, 0), (variables, lanes - variables - 4)))
    pieces.append(jnp.concatenate([grad_embed, grad_head + gain_part], axis=1))
    grads = jnp.stack(pieces).reshape(gathered.shape)
    row = jnp.arange(8)[:, None]
    stats = jnp.where(row == 1, loss_local, jnp.where(row == 2, weight_local, 0.0))
    stats = jnp.where(jnp.arange(128)[None, :] == 0, stats, 0.0)
    share, total = reduce_all(plan, grads, grads.astype(jnp.bfloat16), stats)
    square_sum, loss_sum, weight_sum = (jnp.sum(total[n]) for n in range(3))
    shares = (
        share[-1, :, :variables].T,
        share[:-1],
        share[-1, :, lanes : lanes + variables],
        share[-1, :, lanes + variables : lanes + variables + 4].T,
    )
    grad_norm = jnp.sqrt(square_sum)
    scale = jnp.minimum(1.0, CLIP / (grad_norm + 1e-06))
    return (
        loss_sum,
        weight_sum,
        grad_norm,
        *adamw(embed_weight, embed_first, embed_second, shares[0], scale, RATE),
        *adamw(node_mats, mats_first, mats_second, shares[1], scale, RATE),
        *adamw(head_weight, head_first, head_second, shares[2], scale, RATE),
        *adamw(norm_gains, gains_first, gains_second, shares[3], scale, GAIN_RATE),
    )


def solution(mesh):
    plan = Plan(mesh.shape["nodes"])
    cells = P(None, BOTH, None)
    columns = P(None, BOTH)
    rows = P(BOTH, None)
    blocks = P(None, "nodes")
    return jax.shard_map(
        lambda *args: on_device(plan, *args),
        mesh=mesh,
        in_specs=(
            (cells, cells, columns, blocks, blocks, blocks, blocks, blocks)
            + (columns,) * 3
            + (cells,) * 3
            + (rows,) * 3
            + (columns,) * 3
        ),
        out_specs=(P(), P(), P()) + (columns,) * 4 + (cells,) * 4 + (rows,) * 4 + (columns,) * 4,
        check_vma=False,
    )
```

```python
import functools
import math

import jax
import jax.numpy as jnp
from jax import lax
from jax.experimental import pallas as pl
from jax.experimental.pallas import tpu as pltpu
from jax.sharding import PartitionSpec as P

M_DEV = 640
STEP = 5
MICRO = 4


EPS_NORM = 1e-05
CLIP = 0.5
RATE = 0.04
GAIN_RATE = 0.4
BETA_ONE = 0.5
BETA_TWO = 0.6
EPS_ADAM = 1e-08
DECAY = 0.1

BOTH = ("nodes", "feat")


def matmul(a, b):
    return jnp.dot(a, b, preferred_element_type=jnp.float32)


def left_dot(a, b):
    return lax.dot_general(a, b, (((0,), (0,)), ((), ())), preferred_element_type=jnp.float32)


def right_dot(a, b):
    return lax.dot_general(a, b, (((1,), (1,)), ((), ())), preferred_element_type=jnp.float32)


class Plan:
    def __init__(self, nodes):
        self.nodes = nodes
        self.chips = nodes // MICRO
        self.bits = self.chips.bit_length() - 1
        width = math.isqrt(self.chips)
        self.width = width if width * width == self.chips else 0

    def device(self, m, j, c):
        return (m * self.chips + walk(j % self.chips, self.width)) * 2 + c

    def ring(self, step):
        pairs = []
        length = 2 * self.chips
        for m in range(MICRO):
            for q in range(length):
                to = (q + step) % length
                pairs.append((self.device(m, q // 2, q % 2), self.device(m, to // 2, to % 2)))
        return pairs


MESH = pl.DeviceIdType.MESH
CODE_BITS = 12


def walk(value, width):
    if width == 0:
        return value
    row, col = value // width, value % width
    return row * width + col + (row % 2) * (width - 1 - 2 * col)


class Spot:
    def __init__(self, plan):
        me = lax.axis_index("nodes")
        self.plan = plan
        self.core = lax.axis_index("feat")
        self.z = me // plan.chips
        self.p = me % plan.chips

    def bit(self, b):
        return (self.p // (1 << b)) % 2

    def peer_z(self, d):
        return {"nodes": ((self.z + d) % MICRO) * self.plan.chips + self.p, "feat": self.core}

    def peer_bit(self, b):
        other = self.p + (1 - 2 * self.bit(b)) * (1 << b)
        return {"nodes": self.z * self.plan.chips + other, "feat": self.core}

    def in_plane(self, p, core):
        return {"nodes": self.z * self.plan.chips + p, "feat": core}

    def sibling(self):
        return self.in_plane(self.p, 1 - self.core)

    def partners(self):
        chips = self.plan.chips
        found = [self.peer_z(d) for d in range(1, MICRO)]
        for turn in range(chips):
            p = (self.p + turn) % chips
            if turn:
                found.append(self.in_plane(p, self.core))
            found.append(self.in_plane(p, 1 - self.core))
        return found

    def meet(self):
        barrier = pltpu.get_barrier_semaphore()
        found = self.partners()
        for other in found:
            pl.semaphore_signal(barrier, inc=1, device_id=other, device_id_type=MESH)
        pl.semaphore_wait(barrier, len(found))

    def held(self, done):
        bits = range(self.plan.bits - 1, -1, -1)
        return tuple(slice(None) if b in done else self.bit(b) for b in bits)


def remote(src, dst, send, recv, to):
    return pltpu.make_async_remote_copy(
        src_ref=src, dst_ref=dst, send_sem=send, recv_sem=recv, device_id=to, device_id_type=MESH
    )


def gather_kernel(
    plan,
    shapes,
    pack_ref,
    cells_ref,
    codes_ref,
    all_ref,
    main_ref,
    halo_ref,
    enc_ref,
    proc_ref,
    dec_ref,
    graph_ref,
    total,
    whole,
    cell_hop,
    code_hop,
    own_sem,
    out_sem,
    hop_send,
    hop_recv,
    plane_send,
    plane_recv,
    twin_send,
    twin_recv,
    move_send,
    move_recv,
):
    spot = Spot(plan)
    z, p, core = spot.z, spot.p, spot.core
    chips, bits = plan.chips, plan.bits
    groups = bits
    mats = pack_ref.shape[0] // groups
    code_rows = codes_ref.shape[0] // 2
    lanes = halo_ref.shape[-1]
    own = pltpu.make_async_copy(pack_ref, all_ref.at[(slice(None), z) + spot.held(()) + (core,)], own_sem)
    own.start()
    spot.meet()
    my_codes = codes_ref.at[pl.ds(pl.multiple_of(core * code_rows, 8), code_rows)]
    hops = []
    for d in range(1, MICRO):
        to = spot.peer_z(d)
        m = (z + d) % MICRO
        for n, (src, dst) in enumerate(
            (
                (my_codes, code_hop.at[d - 1]),
                (cells_ref.at[m], cell_hop.at[d - 1]),
                (pack_ref, all_ref.at[(slice(None), z) + spot.held(()) + (core,)]),
            )
        ):
            copy = remote(src, dst, hop_send.at[d - 1, n], hop_recv.at[d - 1, n], to)
            copy.start()
            hops.append(copy)
    quarter = p % 4
    bb, to_core = quarter % 2, quarter // 2
    slot = bb * 2 + core
    half_slot = (1 - bb) * 2 + core
    moves = []

    def move(d, n, src, dst, sem, chip, to_core):
        here = jnp.logical_and(chip == p, to_core == core)
        copy = remote(src, dst, move_send.at[d, n], sem, spot.in_plane(chip, to_core))

        @pl.when(here)
        def _():
            pltpu.make_async_copy(src, dst, sem).start()

        @pl.when(jnp.logical_not(here))
        def _():
            copy.start()

        moves.append((here, copy))

    def spread_codes(d):
        block = ((z - d) % MICRO) * chips + p
        codes = my_codes if d == 0 else code_hop.at[d - 1]
        rows = pl.ds(pl.multiple_of(core * code_rows, 8), code_rows)
        dst = graph_ref.at[bb, rows]
        move(d, 0, codes, dst, move_recv.at[0, slot], walk(block // 4, plan.width), to_core)

    def spread(d):
        block = ((z - d) % MICRO) * chips + p
        j = block // 4
        chip = walk(j, plan.width)
        q = (2 * j + to_core + 2 * bb - 1) % (2 * chips)
        near = walk(q // 2, plan.width)
        cells = cells_ref.at[z] if d == 0 else cell_hop.at[d - 1]
        move(
            d,
            1,
            cells.at[:, pl.ds(0, lanes)],
            halo_ref.at[1 - bb, core],
            move_recv.at[1, half_slot],
            near,
            q % 2,
        )
        move(d, 2, cells, main_ref.at[bb, core], move_recv.at[2, slot], chip, to_core)

    def region(d, done):
        return ((z - d) % MICRO,) + spot.held(done) + (core,)

    planes = {}

    def step(d, g, t):
        done = tuple((g + s) % bits for s in range(t))
        where = (pl.ds(g * mats, mats),) + region(d, done)
        copy = remote(
            all_ref.at[where],
            all_ref.at[where],
            plane_send.at[d, g, t],
            plane_recv.at[d, g, t],
            spot.peer_bit((g + t) % bits),
        )
        copy.start()
        planes[d, g, t] = copy

    for d in range(MICRO):
        if d:
            hops[3 * (d - 1)].wait_recv()
        spread_codes(d)
    outs = []

    def build(n, side_block):
        first, edges, rows, columns = shapes[n]
        chunk = math.gcd(edges, 1024) // 128
        area = (pl.ds(0, rows), pl.ds(0, columns))

        def ones(row, count):
            place = lax.broadcasted_iota(jnp.int32, (count, 128), 0).astype(jnp.int16)
            hit = place == row.astype(jnp.int16)
            return jnp.where(hit, jnp.bfloat16(1), jnp.bfloat16(0)).astype(jnp.float8_e4m3fn)

        def body(k, _):
            into, out = [], []
            for i in range(chunk):
                code = graph_ref[side_block, pl.ds(first + k * chunk + i, 1), :]
                into.append(ones(code >> CODE_BITS, rows))
                out.append(ones(code & ((1 << CODE_BITS) - 1), columns))
            total[area] += right_dot(jnp.concatenate(into, axis=1), jnp.concatenate(out, axis=1))
            return 0

        total[area] = jnp.zeros((rows, columns), jnp.float32)
        lax.fori_loop(0, edges // (128 * chunk), body, 0)
        if len(outs) >= 2:
            outs[-2].wait()
        side = len(outs) % 2
        whole[(side,) + area] = total[area].astype(jnp.bfloat16)
        ref = (enc_ref, proc_ref, dec_ref)[n]
        copy = pltpu.make_async_copy(whole.at[(side,) + area], ref.at[side_block], out_sem.at[side])
        copy.start()
        outs.append(copy)

    work = [[], [(0, 0), (0, 1)], [(1, 0)], [(1, 1)], [(2, 0)], [(2, 1)]]
    twins = []
    for tick in range(MICRO + bits):
        for t in range(bits + 1):
            d = tick - t
            if d < 0 or d >= MICRO:
                continue
            if t == 0:
                if d == 0:
                    own.wait()
                else:
                    hops[3 * (d - 1) + 1].wait_recv()
                    hops[3 * (d - 1) + 2].wait_recv()
                spread(d)
            else:
                for g in range(groups):
                    planes[d, g, t - 1].wait_recv()
            if t < bits:
                for g in range(groups):
                    step(d, g, t)
            else:
                where = (slice(None),) + region(d, tuple(range(bits)))
                copy = remote(
                    all_ref.at[where], all_ref.at[where], twin_send.at[d], twin_recv.at[d], spot.sibling()
                )
                copy.start()
                twins.append(copy)
        if tick == 1:
            for n in range(4):
                dst = graph_ref.at[n // 2, pl.ds((n % 2) * code_rows, code_rows)]
                pltpu.make_async_copy(dst, dst, move_recv.at[0, n]).wait()
        for kind, block in work[tick] if tick < len(work) else []:
            build(kind, block)
    for copy in outs[-2:]:
        copy.wait()
    for copy in hops + list(planes.values()):
        copy.wait_send()
    for copy in twins:
        copy.wait()
    for here, copy in moves:

        @pl.when(jnp.logical_not(here))
        def _():
            copy.wait_send()

    for n in range(4):
        half, side = n % 2, n // 2
        for kind, dst in ((1, halo_ref.at[side, half]), (2, main_ref.at[side, half])):
            pltpu.make_async_copy(dst, dst, move_recv.at[kind, n]).wait()


def gather_all(plan, shapes, pack, cells, codes):
    mats, rows, width = pack.shape
    micro, half, lanes = cells.shape
    bits = plan.bits
    most_rows = max(shape[2] for shape in shapes)
    most_columns = max(shape[3] for shape in shapes)
    any_space = pl.BlockSpec(memory_space=pl.ANY)
    dma = pltpu.SemaphoreType.DMA
    return pl.pallas_call(
        functools.partial(gather_kernel, plan, shapes),
        out_shape=(
            jax.ShapeDtypeStruct((mats, MICRO) + (2,) * bits + (2, rows, width), pack.dtype),
            jax.ShapeDtypeStruct((2, 2, half, lanes), cells.dtype),
            jax.ShapeDtypeStruct((2, 2, half, lanes // 2), cells.dtype),
            *(jax.ShapeDtypeStruct((2,) + shape[2:], jnp.bfloat16) for shape in shapes),
        ),
        in_specs=[any_space] * 3,
        out_specs=(any_space,) * 6,
        scratch_shapes=[
            pltpu.VMEM((2,) + codes.shape, codes.dtype),
            pltpu.VMEM((most_rows, most_columns), jnp.float32),
            pltpu.VMEM((2, most_rows, most_columns), jnp.bfloat16),
            pltpu.VMEM((MICRO - 1, half, lanes), cells.dtype),
            pltpu.VMEM((MICRO - 1, codes.shape[0] // 2, codes.shape[1]), codes.dtype),
            dma,
            dma((2,)),
            dma((MICRO - 1, 3)),
            dma((MICRO - 1, 3)),
            dma((MICRO, bits, bits)),
            dma((MICRO, bits, bits)),
            dma((MICRO,)),
            dma((MICRO,)),
            dma((MICRO, 3)),
            dma((3, 4)),
        ],
        compiler_params=pltpu.CompilerParams(
            collective_id=0, has_side_effects=True, vmem_limit_bytes=48 << 20
        ),
        name="gather_all",
    )(pack, cells, codes)


def reduce_kernel(
    plan,
    grads_ref,
    low_ref,
    stats_ref,
    share_ref,
    total_ref,
    acc,
    twin_in,
    plane_out,
    plane_in,
    hop_out,
    hop_in,
    z_stats,
    plane_stats,
    twin_stats,
    own_sem,
    twin_send,
    twin_recv,
    plane_send,
    plane_recv,
    hop_send,
    hop_recv,
    stat_send,
    stat_recv,
):
    spot = Spot(plan)
    z, p, core = spot.z, spot.p, spot.core
    chips, bits = plan.chips, plan.bits
    groups = bits
    mats = grads_ref.shape[0]
    part = mats // groups
    every = (slice(None),) * bits
    order = [1, 2, 3, 0]
    owns = {}
    for d in order:
        item = (z + d) % MICRO
        owns[d] = pltpu.make_async_copy(
            grads_ref.at[(slice(None), item) + every + (core,)], acc.at[d], own_sem.at[d]
        )
        owns[d].start()
    spot.meet()
    twins = {}
    for d in order:
        item = (z + d) % MICRO
        twins[d] = remote(
            low_ref.at[(slice(None), item) + every + (1 - core,)],
            twin_in.at[d],
            twin_send.at[d],
            twin_recv.at[d],
            spot.sibling(),
        )
        twins[d].start()

    def starts(t):
        return sum(1 << (bits - 1 - s) for s in range(t))

    planes, hops = {}, []

    def send_step(d, g, t):
        done = tuple((g + s) % bits for s in range(t))
        b = (g + t) % bits
        count = 1 << (bits - 1 - t)
        at = starts(t)
        theirs = tuple(
            spot.bit(n) if n in done else (1 - spot.bit(n) if n == b else slice(None))
            for n in range(bits - 1, -1, -1)
        )

        def body(n, _):
            mat = g * part + n
            value = acc[(d, mat) + theirs]
            plane_out[d, mat, at : at + count] = value.reshape((count,) + value.shape[-2:]).astype(
                plane_out.dtype
            )
            return 0

        lax.fori_loop(0, part, body, 0)
        where = (d, pl.ds(g * part, part), pl.ds(at, count))
        planes[d, g, t] = remote(
            plane_out.at[where],
            plane_in.at[where],
            plane_send.at[d, g, t],
            plane_recv.at[d, g, t],
            spot.peer_bit(b),
        )
        planes[d, g, t].start()

    def add_step(d, g, t):
        planes[d, g, t].wait_recv()
        done = tuple((g + s) % bits for s in range(t + 1))
        count = 1 << (bits - 1 - t)
        at = starts(t)
        mine = tuple(spot.bit(n) if n in done else slice(None) for n in range(bits - 1, -1, -1))

        def body(n, _):
            mat = g * part + n
            where = (d, mat) + mine
            value = acc[where]
            came = plane_in[d, mat, at : at + count].astype(jnp.float32)
            acc[where] = value + came.reshape(value.shape)
            return 0

        lax.fori_loop(0, part, body, 0)

    for tick in range(MICRO + bits):
        for t in range(bits + 1):
            n = tick - t
            if n < 0 or n >= MICRO:
                continue
            d = order[n]
            if t == 0:
                owns[d].wait()
                twins[d].wait_recv()

                def body(mat, _):
                    acc[d, mat] = acc[d, mat] + twin_in[d, mat].astype(jnp.float32)
                    return 0

                lax.fori_loop(0, mats, body, 0)
            else:
                for g in range(groups):
                    add_step(d, g, t - 1)
            if t < bits:
                for g in range(groups):
                    send_step(d, g, t)
            elif d:

                def body(mat, _):
                    hop_out[d - 1, mat] = acc[(d, mat) + spot.held(())].astype(hop_out.dtype)
                    return 0

                lax.fori_loop(0, mats, body, 0)
                copy = remote(
                    hop_out.at[d - 1], hop_in.at[d - 1], hop_send.at[d - 1], hop_recv.at[d - 1], spot.peer_z(d)
                )
                copy.start()
                hops.append(copy)
    for copy in hops:
        copy.wait_recv()

    def body(mat, square):
        value = acc[(0, mat) + spot.held(())]
        for d in range(MICRO - 1):
            value = value + hop_in[d, mat].astype(jnp.float32)
        share_ref[mat] = value
        return square + value * value

    square = lax.fori_loop(0, mats, body, jnp.zeros(share_ref.shape[1:], jnp.float32))
    square = jnp.sum(square, axis=0, keepdims=True)
    lanes = total_ref.shape[1]
    square = sum(square[:, n : n + lanes] for n in range(0, square.shape[1], lanes))
    row = lax.broadcasted_iota(jnp.int32, total_ref.shape, 0)
    tile = jnp.where(row == 0, square, stats_ref[...])
    sends = []

    def exchange(buffer, index, targets, at):
        buffer[index] = tile
        copies = []
        for n, to in enumerate(targets):
            copy = remote(
                buffer.at[index], buffer.at[index], stat_send.at[at + n], stat_recv.at[at + n], to
            )
            copy.start()
            copies.append(copy)
        for copy in copies:
            copy.wait()
        total = buffer[0]
        for n in range(1, buffer.shape[0]):
            total = total + buffer[n]
        return total

    tile = exchange(z_stats, z, [spot.peer_z(d) for d in range(1, MICRO)], 0)
    tile = exchange(
        plane_stats, p, [spot.in_plane((p + d) % chips, core) for d in range(1, chips)], MICRO - 1
    )
    tile = exchange(twin_stats, core, [spot.sibling()], MICRO + chips - 2)
    total_ref[...] = tile
    for copy in list(twins.values()) + list(planes.values()) + hops:
        copy.wait_send()


def reduce_all(plan, grads, low, stats):
    mats, rows, width = grads.shape[0], grads.shape[-2], grads.shape[-1]
    bits, chips = plan.bits, plan.chips
    shards = (2,) * bits
    steps = chips - 1
    any_space = pl.BlockSpec(memory_space=pl.ANY)
    vmem = pl.BlockSpec(memory_space=pltpu.VMEM)
    dma = pltpu.SemaphoreType.DMA
    return pl.pallas_call(
        functools.partial(reduce_kernel, plan),
        out_shape=(
            jax.ShapeDtypeStruct((mats, rows, width), jnp.float32),
            jax.ShapeDtypeStruct(stats.shape, jnp.float32),
        ),
        in_specs=[any_space, any_space, vmem],
        out_specs=(vmem, vmem),
        scratch_shapes=[
            pltpu.VMEM((MICRO, mats) + shards + (rows, width), jnp.float32),
            pltpu.VMEM((MICRO, mats) + shards + (rows, width), low.dtype),
            pltpu.VMEM((MICRO, mats, steps, rows, width), jnp.bfloat16),
            pltpu.VMEM((MICRO, mats, steps, rows, width), jnp.bfloat16),
            pltpu.VMEM((MICRO - 1, mats, rows, width), jnp.bfloat16),
            pltpu.VMEM((MICRO - 1, mats, rows, width), jnp.bfloat16),
            pltpu.VMEM((MICRO,) + stats.shape, jnp.float32),
            pltpu.VMEM((chips,) + stats.shape, jnp.float32),
            pltpu.VMEM((2,) + stats.shape, jnp.float32),
            dma((MICRO,)),
            dma((MICRO,)),
            dma((MICRO,)),
            dma((MICRO, bits, bits)),
            dma((MICRO, bits, bits)),
            dma((MICRO - 1,)),
            dma((MICRO - 1,)),
            dma((MICRO + chips - 1,)),
            dma((MICRO + chips - 1,)),
        ],
        compiler_params=pltpu.CompilerParams(
            collective_id=1, has_side_effects=True, vmem_limit_bytes=56 << 20
        ),
        name="reduce_all",
    )(grads, low, stats)


def norm_rows(z, gain):
    mean = jnp.mean(z, axis=-1, keepdims=True)
    centred = z - mean
    spread = jnp.mean(centred * centred, axis=-1, keepdims=True)
    return centred * lax.rsqrt(spread + EPS_NORM) * gain


def update_fwd(index, base, agg, mats, gains):
    pre = matmul(agg, mats[index])
    if base is not None:
        pre = pre + matmul(base, mats[3 + index])
    active = jax.nn.silu(pre).astype(jnp.bfloat16)
    inner = matmul(active, mats[7 + index])
    return (norm_rows(inner, gains[index]), (pre, active, inner))


def update_bwd(index, base, agg, mats, gains, kept, grad_out):
    pre, active, inner = kept
    _, pull = jax.vjp(norm_rows, inner, gains[index])
    grad_inner, grad_gain = pull(grad_out)
    inner_low = grad_inner.astype(jnp.bfloat16)
    grad_second = left_dot(active, inner_low)
    grad_active = right_dot(inner_low, mats[7 + index])
    sigma = jax.nn.sigmoid(pre)
    pre_low = (grad_active * sigma * (1.0 + pre * (1.0 - sigma))).astype(jnp.bfloat16)
    grad_first = left_dot(agg, pre_low)
    grad_agg = right_dot(pre_low, mats[index])
    grad_self = None
    grad_base = None
    if base is not None:
        grad_self = left_dot(base, pre_low)
        grad_base = right_dot(pre_low, mats[3 + index])
    return (grad_base, grad_agg, grad_first, grad_self, grad_second, grad_gain)


def adamw(param, first, second, grad, scale, rate):
    clipped = grad * scale
    moment = BETA_ONE * first + (1.0 - BETA_ONE) * clipped
    square = BETA_TWO * second + (1.0 - BETA_TWO) * clipped * clipped
    fixed_one = moment / (1.0 - BETA_ONE**STEP)
    fixed_two = square / (1.0 - BETA_TWO**STEP)
    fresh = param - rate * (fixed_one / (jnp.sqrt(fixed_two) + EPS_ADAM) + DECAY * param)
    return (fresh, moment, square, fresh.astype(jnp.bfloat16))


def on_device(
    plan,
    grid_in,
    targets,
    area_weight,
    grid_count,
    g2m_edges,
    mesh_edges,
    m2g_edges,
    edge_count,
    embed_weight,
    embed_first,
    embed_second,
    node_mats,
    mats_first,
    mats_second,
    head_weight,
    head_first,
    head_second,
    norm_gains,
    gains_first,
    gains_second,
):
    half, variables = grid_in.shape[1:]
    grid_rows = 2 * half
    mesh_rows = M_DEV
    lanes = -(-variables // 128) * 128
    core = lax.axis_index("feat")

    position = core * half + jnp.arange(half, dtype=jnp.int32)
    weights = jnp.where(position[None, :] < grid_count, area_weight, 0.0)
    pieces = []
    rest = weights
    for _ in range(3):
        piece = lax.reduce_precision(rest, 8, 7)
        pieces.append(piece.astype(jnp.bfloat16))
        rest = rest - piece
    cells = jnp.concatenate(
        [
            jnp.pad(grid_in, ((0, 0), (0, 0), (0, lanes - variables))),
            targets,
            jnp.pad(jnp.stack(pieces, axis=-1), ((0, 0), (0, 0), (0, lanes - variables - 3))),
        ],
        axis=-1,
    )
    last = jnp.concatenate(
        [
            jnp.pad(embed_weight.T, ((0, 0), (0, lanes - variables))),
            head_weight,
            jnp.pad(norm_gains.T, ((0, 0), (0, lanes - variables - 4))),
        ],
        axis=-1,
    )
    pack = jnp.concatenate([node_mats, last[None]]).astype(jnp.bfloat16)
    graphs = ((g2m_edges, grid_rows, mesh_rows), (mesh_edges, mesh_rows, mesh_rows), (m2g_edges, mesh_rows, grid_rows))
    codes, shapes = [], []
    first = 0
    for n, (edges, columns, rows) in enumerate(graphs):
        per = edges.shape[1]
        alive = jnp.arange(per, dtype=jnp.int32) < edge_count[n, 0]
        codes.append(jnp.where(alive, edges[1] * (1 << CODE_BITS) + edges[0], -1))
        shapes.append((first // 128, per, rows, 3 * columns))
        first += per
    codes = jnp.concatenate(codes).reshape(-1, 128)
    gathered, main, halo, encoder, processor, decoder = gather_all(plan, shapes, pack, cells, codes)
    width = pack.shape[2]
    full = gathered.reshape(-1, width, width)
    mats = full[:-1]
    embed = full[-1, :, :lanes]
    head = full[-1, :, lanes:]
    gains = full[-1, :, lanes + variables : lanes + variables + 4].T.astype(jnp.float32)
    main = main.reshape(-1, 2 * lanes)
    inputs = main[:, :lanes]
    wanted = main[:, lanes:]
    weight = sum(
        main[:, lanes + variables + n : lanes + variables + n + 1].astype(jnp.float32) for n in range(3)
    )
    halo = halo.reshape(2, grid_rows, lanes)
    inputs_ext = jnp.concatenate([halo[0], inputs, halo[1]])
    def extended(rows):
        size = rows.shape[0] // 2
        before = lax.ppermute(rows[size:], BOTH, plan.ring(1))
        after = lax.ppermute(rows[:size], BOTH, plan.ring(-1))
        return jnp.concatenate([before, rows, after])

    def collect(graph, ext):
        size = ext.shape[0] // 4
        return jnp.concatenate(
            [matmul(graph[b], ext[b * size : (b + 3) * size]) for b in range(2)]
        ).astype(jnp.bfloat16)

    def collect_back(graph, grad_agg):
        low = grad_agg.astype(jnp.bfloat16)
        size = low.shape[0] // 2
        pieces = [left_dot(graph[b], low[b * size : (b + 1) * size]) for b in range(2)]
        rows = pieces[0].shape[0] // 3
        before = pieces[0][:rows].astype(jnp.bfloat16)
        after = pieces[1][2 * rows :].astype(jnp.bfloat16)
        from_right = lax.ppermute(before, BOTH, plan.ring(-1)).astype(jnp.float32)
        from_left = lax.ppermute(after, BOTH, plan.ring(1)).astype(jnp.float32)
        first = from_left + pieces[0][rows : 2 * rows] + pieces[1][:rows]
        second = pieces[0][2 * rows :] + pieces[1][rows : 2 * rows] + from_right
        return jnp.concatenate([first, second]).astype(jnp.bfloat16).astype(jnp.float32)

    hidden_ext = right_dot(inputs_ext, embed)
    grid_hidden = hidden_ext[grid_rows : 3 * grid_rows]
    low_ext = hidden_ext.astype(jnp.bfloat16)
    grid_low = low_ext[grid_rows : 3 * grid_rows]
    aggs = [collect(encoder, low_ext)]
    nodes, kept_first = update_fwd(0, None, aggs[0], mats, gains)
    kept = [kept_first]
    lows = [None]
    for index in (1, 2):
        mesh_low = nodes.astype(jnp.bfloat16)
        lows.append(mesh_low)
        aggs.append(collect(processor, extended(mesh_low)))
        branch, kept_now = update_fwd(index, mesh_low, aggs[index], mats, gains)
        kept.append(kept_now)
        nodes = nodes + branch
    aggs.append(collect(decoder, extended(nodes.astype(jnp.bfloat16))))
    branch, kept_now = update_fwd(3, grid_low, aggs[3], mats, gains)
    kept.append(kept_now)
    out_low = (grid_hidden + branch).astype(jnp.bfloat16)
    error = matmul(out_low, head) - wanted.astype(jnp.float32)
    error = jnp.where(jnp.arange(lanes) < variables, error, 0.0)
    loss_local = jnp.sum(weight * error * error)
    weight_local = jnp.sum(weight)
    grad_pred = (2.0 * weight * error).astype(jnp.bfloat16)
    grad_head = left_dot(out_low, grad_pred)
    grad_grid = right_dot(grad_pred, head)
    pieces = [None] * 11
    gain_grads = [None] * 4
    grad_base, grad_agg, pieces[3], pieces[6], pieces[10], gain_grads[3] = update_bwd(
        3, grid_low, aggs[3], mats, gains, kept[3], grad_grid
    )
    grad_grid = grad_grid + grad_base
    grad_nodes = collect_back(decoder, grad_agg)
    for index in (2, 1):
        (
            grad_base,
            grad_agg,
            pieces[index],
            pieces[3 + index],
            pieces[7 + index],
            gain_grads[index],
        ) = update_bwd(index, lows[index], aggs[index], mats, gains, kept[index], grad_nodes)
        grad_nodes = grad_nodes + grad_base + collect_back(processor, grad_agg)
    _, grad_agg, pieces[0], _, pieces[7], gain_grads[0] = update_bwd(
        0, None, aggs[0], mats, gains, kept[0], grad_nodes
    )
    grad_grid = grad_grid + collect_back(encoder, grad_agg)
    grad_embed = left_dot(grad_grid.astype(jnp.bfloat16), inputs)
    gain_part = jnp.pad(jnp.stack(gain_grads).T, ((0, 0), (variables, lanes - variables - 4)))
    pieces.append(jnp.concatenate([grad_embed, grad_head + gain_part], axis=1))
    grads = jnp.stack(pieces).reshape(gathered.shape)
    row = jnp.arange(8)[:, None]
    stats = jnp.where(row == 1, loss_local, jnp.where(row == 2, weight_local, 0.0))
    stats = jnp.where(jnp.arange(128)[None, :] == 0, stats, 0.0)
    share, total = reduce_all(plan, grads, grads.astype(jnp.bfloat16), stats)
    square_sum, loss_sum, weight_sum = (jnp.sum(total[n]) for n in range(3))
    shares = (
        share[-1, :, :variables].T,
        share[:-1],
        share[-1, :, lanes : lanes + variables],
        share[-1, :, lanes + variables : lanes + variables + 4].T,
    )
    grad_norm = jnp.sqrt(square_sum)
    scale = jnp.minimum(1.0, CLIP / (grad_norm + 1e-06))
    return (
        loss_sum,
        weight_sum,
        grad_norm,
        *adamw(embed_weight, embed_first, embed_second, shares[0], scale, RATE),
        *adamw(node_mats, mats_first, mats_second, shares[1], scale, RATE),
        *adamw(head_weight, head_first, head_second, shares[2], scale, RATE),
        *adamw(norm_gains, gains_first, gains_second, shares[3], scale, GAIN_RATE),
    )


def solution(mesh):
    plan = Plan(mesh.shape["nodes"])
    cells = P(None, BOTH, None)
    columns = P(None, BOTH)
    rows = P(BOTH, None)
    blocks = P(None, "nodes")
    return jax.shard_map(
        lambda *args: on_device(plan, *args),
        mesh=mesh,
        in_specs=(
            (cells, cells, columns, blocks, blocks, blocks, blocks, blocks)
            + (columns,) * 3
            + (cells,) * 3
            + (rows,) * 3
            + (columns,) * 3
        ),
        out_specs=(P(), P(), P()) + (columns,) * 4 + (cells,) * 4 + (rows,) * 4 + (columns,) * 4,
        check_vma=False,
    )
```

```python
import functools
import math

import jax
import jax.numpy as jnp
from jax import lax
from jax.experimental import pallas as pl
from jax.experimental.pallas import tpu as pltpu
from jax.sharding import PartitionSpec as P

M_DEV = 640
STEP = 5
MICRO = 4


EPS_NORM = 1e-05
CLIP = 0.5
RATE = 0.04
GAIN_RATE = 0.4
BETA_ONE = 0.5
BETA_TWO = 0.6
EPS_ADAM = 1e-08
DECAY = 0.1

BOTH = ("nodes", "feat")


def matmul(a, b):
    return jnp.dot(a, b, preferred_element_type=jnp.float32)


def left_dot(a, b):
    return lax.dot_general(a, b, (((0,), (0,)), ((), ())), preferred_element_type=jnp.float32)


def right_dot(a, b):
    return lax.dot_general(a, b, (((1,), (1,)), ((), ())), preferred_element_type=jnp.float32)


class Plan:
    def __init__(self, nodes):
        self.nodes = nodes
        self.chips = nodes // MICRO
        self.bits = self.chips.bit_length() - 1
        width = math.isqrt(self.chips)
        self.width = width if width * width == self.chips else 0


MESH = pl.DeviceIdType.MESH
CODE_BITS = 12


def walk(value, width):
    if width == 0:
        return value
    row, col = value // width, value % width
    return row * width + col + (row % 2) * (width - 1 - 2 * col)


class Spot:
    def __init__(self, plan):
        me = lax.axis_index("nodes")
        self.plan = plan
        self.core = lax.axis_index("feat")
        self.z = me // plan.chips
        self.p = me % plan.chips

    def bit(self, b):
        return (self.p // (1 << b)) % 2

    def peer_z(self, d):
        return {"nodes": ((self.z + d) % MICRO) * self.plan.chips + self.p, "feat": self.core}

    def peer_bit(self, b):
        other = self.p + (1 - 2 * self.bit(b)) * (1 << b)
        return {"nodes": self.z * self.plan.chips + other, "feat": self.core}

    def in_plane(self, p, core):
        return {"nodes": self.z * self.plan.chips + p, "feat": core}

    def sibling(self):
        return self.in_plane(self.p, 1 - self.core)

    def partners(self):
        chips = self.plan.chips
        found = [self.peer_z(d) for d in range(1, MICRO)]
        for turn in range(chips):
            p = (self.p + turn) % chips
            if turn:
                found.append(self.in_plane(p, self.core))
            found.append(self.in_plane(p, 1 - self.core))
        return found

    def meet(self):
        barrier = pltpu.get_barrier_semaphore()
        found = self.partners()
        for other in found:
            pl.semaphore_signal(barrier, inc=1, device_id=other, device_id_type=MESH)
        pl.semaphore_wait(barrier, len(found))

    def held(self, done):
        bits = range(self.plan.bits - 1, -1, -1)
        return tuple(slice(None) if b in done else self.bit(b) for b in bits)


def remote(src, dst, send, recv, to):
    return pltpu.make_async_remote_copy(
        src_ref=src, dst_ref=dst, send_sem=send, recv_sem=recv, device_id=to, device_id_type=MESH
    )


def gather_kernel(
    plan,
    shapes,
    pack_ref,
    cells_ref,
    codes_ref,
    all_ref,
    main_ref,
    halo_ref,
    enc_ref,
    proc_ref,
    dec_ref,
    graph_ref,
    total,
    whole,
    cell_hop,
    code_hop,
    own_sem,
    out_sem,
    hop_send,
    hop_recv,
    plane_send,
    plane_recv,
    twin_send,
    twin_recv,
    move_send,
    move_recv,
):
    spot = Spot(plan)
    z, p, core = spot.z, spot.p, spot.core
    chips, bits = plan.chips, plan.bits
    groups = bits
    mats = pack_ref.shape[0] // groups
    code_rows = codes_ref.shape[0] // 2
    lanes = halo_ref.shape[-1]
    own = pltpu.make_async_copy(pack_ref, all_ref.at[(slice(None), z) + spot.held(()) + (core,)], own_sem)
    own.start()
    spot.meet()
    my_codes = codes_ref.at[pl.ds(pl.multiple_of(core * code_rows, 8), code_rows)]
    hops = []
    for d in range(1, MICRO):
        to = spot.peer_z(d)
        m = (z + d) % MICRO
        for n, (src, dst) in enumerate(
            (
                (my_codes, code_hop.at[d - 1]),
                (cells_ref.at[m], cell_hop.at[d - 1]),
                (pack_ref, all_ref.at[(slice(None), z) + spot.held(()) + (core,)]),
            )
        ):
            copy = remote(src, dst, hop_send.at[d - 1, n], hop_recv.at[d - 1, n], to)
            copy.start()
            hops.append(copy)
    quarter = p % 4
    bb, to_core = quarter % 2, quarter // 2
    slot = bb * 2 + core
    half_slot = (1 - bb) * 2 + core
    moves = []

    def move(d, n, src, dst, sem, chip, to_core):
        here = jnp.logical_and(chip == p, to_core == core)
        copy = remote(src, dst, move_send.at[d, n], sem, spot.in_plane(chip, to_core))

        @pl.when(here)
        def _():
            pltpu.make_async_copy(src, dst, sem).start()

        @pl.when(jnp.logical_not(here))
        def _():
            copy.start()

        moves.append((here, copy))

    def spread_codes(d):
        block = ((z - d) % MICRO) * chips + p
        codes = my_codes if d == 0 else code_hop.at[d - 1]
        rows = pl.ds(pl.multiple_of(core * code_rows, 8), code_rows)
        dst = graph_ref.at[bb, rows]
        move(d, 0, codes, dst, move_recv.at[0, slot], walk(block // 4, plan.width), to_core)

    def spread(d):
        block = ((z - d) % MICRO) * chips + p
        j = block // 4
        chip = walk(j, plan.width)
        q = (2 * j + to_core + 2 * bb - 1) % (2 * chips)
        near = walk(q // 2, plan.width)
        cells = cells_ref.at[z] if d == 0 else cell_hop.at[d - 1]
        move(
            d,
            1,
            cells.at[:, pl.ds(0, lanes)],
            halo_ref.at[1 - bb, core],
            move_recv.at[1, half_slot],
            near,
            q % 2,
        )
        move(d, 2, cells, main_ref.at[bb, core], move_recv.at[2, slot], chip, to_core)

    def region(d, done):
        return ((z - d) % MICRO,) + spot.held(done) + (core,)

    planes = {}

    def step(d, g, t):
        done = tuple((g + s) % bits for s in range(t))
        where = (pl.ds(g * mats, mats),) + region(d, done)
        copy = remote(
            all_ref.at[where],
            all_ref.at[where],
            plane_send.at[d, g, t],
            plane_recv.at[d, g, t],
            spot.peer_bit((g + t) % bits),
        )
        copy.start()
        planes[d, g, t] = copy

    for d in range(MICRO):
        if d:
            hops[3 * (d - 1)].wait_recv()
        spread_codes(d)
    outs = []

    def build(n, side_block):
        first, edges, rows, columns = shapes[n]
        chunk = math.gcd(edges, 1024) // 128
        area = (pl.ds(0, rows), pl.ds(0, columns))

        def ones(row, count):
            place = lax.broadcasted_iota(jnp.int32, (count, 128), 0).astype(jnp.int16)
            hit = place == row.astype(jnp.int16)
            return jnp.where(hit, jnp.bfloat16(1), jnp.bfloat16(0)).astype(jnp.float8_e4m3fn)

        def body(k, _):
            into, out = [], []
            for i in range(chunk):
                code = graph_ref[side_block, pl.ds(first + k * chunk + i, 1), :]
                into.append(ones(code >> CODE_BITS, rows))
                out.append(ones(code & ((1 << CODE_BITS) - 1), columns))
            total[area] += right_dot(jnp.concatenate(into, axis=1), jnp.concatenate(out, axis=1))
            return 0

        total[area] = jnp.zeros((rows, columns), jnp.float32)
        lax.fori_loop(0, edges // (128 * chunk), body, 0)
        if len(outs) >= 2:
            outs[-2].wait()
        side = len(outs) % 2
        whole[(side,) + area] = total[area].astype(jnp.bfloat16)
        ref = (enc_ref, proc_ref, dec_ref)[n]
        copy = pltpu.make_async_copy(whole.at[(side,) + area], ref.at[side_block], out_sem.at[side])
        copy.start()
        outs.append(copy)

    work = [[], [(0, 0), (0, 1)], [(1, 0)], [(1, 1)], [(2, 0)], [(2, 1)]]
    twins = []
    for tick in range(MICRO + bits):
        for t in range(bits + 1):
            d = tick - t
            if d < 0 or d >= MICRO:
                continue
            if t == 0:
                if d == 0:
                    own.wait()
                else:
                    hops[3 * (d - 1) + 1].wait_recv()
                    hops[3 * (d - 1) + 2].wait_recv()
                spread(d)
            else:
                for g in range(groups):
                    planes[d, g, t - 1].wait_recv()
            if t < bits:
                for g in range(groups):
                    step(d, g, t)
            else:
                where = (slice(None),) + region(d, tuple(range(bits)))
                copy = remote(
                    all_ref.at[where], all_ref.at[where], twin_send.at[d], twin_recv.at[d], spot.sibling()
                )
                copy.start()
                twins.append(copy)
        if tick == 1:
            for n in range(4):
                dst = graph_ref.at[n // 2, pl.ds((n % 2) * code_rows, code_rows)]
                pltpu.make_async_copy(dst, dst, move_recv.at[0, n]).wait()
        for kind, block in work[tick] if tick < len(work) else []:
            build(kind, block)
    for copy in outs[-2:]:
        copy.wait()
    for copy in hops + list(planes.values()):
        copy.wait_send()
    for copy in twins:
        copy.wait()
    for here, copy in moves:

        @pl.when(jnp.logical_not(here))
        def _():
            copy.wait_send()

    for n in range(4):
        half, side = n % 2, n // 2
        for kind, dst in ((1, halo_ref.at[side, half]), (2, main_ref.at[side, half])):
            pltpu.make_async_copy(dst, dst, move_recv.at[kind, n]).wait()


def gather_all(plan, shapes, pack, cells, codes):
    mats, rows, width = pack.shape
    micro, half, lanes = cells.shape
    bits = plan.bits
    most_rows = max(shape[2] for shape in shapes)
    most_columns = max(shape[3] for shape in shapes)
    any_space = pl.BlockSpec(memory_space=pl.ANY)
    dma = pltpu.SemaphoreType.DMA
    return pl.pallas_call(
        functools.partial(gather_kernel, plan, shapes),
        out_shape=(
            jax.ShapeDtypeStruct((mats, MICRO) + (2,) * bits + (2, rows, width), pack.dtype),
            jax.ShapeDtypeStruct((2, 2, half, lanes), cells.dtype),
            jax.ShapeDtypeStruct((2, 2, half, lanes // 2), cells.dtype),
            *(jax.ShapeDtypeStruct((2,) + shape[2:], jnp.bfloat16) for shape in shapes),
        ),
        in_specs=[any_space] * 3,
        out_specs=(any_space,) * 6,
        scratch_shapes=[
            pltpu.VMEM((2,) + codes.shape, codes.dtype),
            pltpu.VMEM((most_rows, most_columns), jnp.float32),
            pltpu.VMEM((2, most_rows, most_columns), jnp.bfloat16),
            pltpu.VMEM((MICRO - 1, half, lanes), cells.dtype),
            pltpu.VMEM((MICRO - 1, codes.shape[0] // 2, codes.shape[1]), codes.dtype),
            dma,
            dma((2,)),
            dma((MICRO - 1, 3)),
            dma((MICRO - 1, 3)),
            dma((MICRO, bits, bits)),
            dma((MICRO, bits, bits)),
            dma((MICRO,)),
            dma((MICRO,)),
            dma((MICRO, 3)),
            dma((3, 4)),
        ],
        compiler_params=pltpu.CompilerParams(
            collective_id=0, has_side_effects=True, vmem_limit_bytes=48 << 20
        ),
        name="gather_all",
    )(pack, cells, codes)


def reduce_kernel(
    plan,
    grads_ref,
    low_ref,
    stats_ref,
    share_ref,
    total_ref,
    acc,
    twin_in,
    plane_out,
    plane_in,
    hop_out,
    hop_in,
    z_stats,
    plane_stats,
    twin_stats,
    own_sem,
    twin_send,
    twin_recv,
    plane_send,
    plane_recv,
    hop_send,
    hop_recv,
    stat_send,
    stat_recv,
):
    spot = Spot(plan)
    z, p, core = spot.z, spot.p, spot.core
    chips, bits = plan.chips, plan.bits
    groups = bits
    mats = grads_ref.shape[0]
    part = mats // groups
    every = (slice(None),) * bits
    order = [1, 2, 3, 0]
    owns = {}
    for d in order:
        item = (z + d) % MICRO
        owns[d] = pltpu.make_async_copy(
            grads_ref.at[(slice(None), item) + every + (core,)], acc.at[d], own_sem.at[d]
        )
        owns[d].start()
    spot.meet()
    twins = {}
    for d in order:
        item = (z + d) % MICRO
        twins[d] = remote(
            low_ref.at[(slice(None), item) + every + (1 - core,)],
            twin_in.at[d],
            twin_send.at[d],
            twin_recv.at[d],
            spot.sibling(),
        )
        twins[d].start()

    def starts(t):
        return sum(1 << (bits - 1 - s) for s in range(t))

    planes, hops = {}, []

    def send_step(d, g, t):
        done = tuple((g + s) % bits for s in range(t))
        b = (g + t) % bits
        count = 1 << (bits - 1 - t)
        at = starts(t)
        theirs = tuple(
            spot.bit(n) if n in done else (1 - spot.bit(n) if n == b else slice(None))
            for n in range(bits - 1, -1, -1)
        )

        def body(n, _):
            mat = g * part + n
            value = acc[(d, mat) + theirs]
            plane_out[d, mat, at : at + count] = value.reshape((count,) + value.shape[-2:]).astype(
                plane_out.dtype
            )
            return 0

        lax.fori_loop(0, part, body, 0)
        where = (d, pl.ds(g * part, part), pl.ds(at, count))
        planes[d, g, t] = remote(
            plane_out.at[where],
            plane_in.at[where],
            plane_send.at[d, g, t],
            plane_recv.at[d, g, t],
            spot.peer_bit(b),
        )
        planes[d, g, t].start()

    def add_step(d, g, t):
        planes[d, g, t].wait_recv()
        done = tuple((g + s) % bits for s in range(t + 1))
        count = 1 << (bits - 1 - t)
        at = starts(t)
        mine = tuple(spot.bit(n) if n in done else slice(None) for n in range(bits - 1, -1, -1))

        def body(n, _):
            mat = g * part + n
            where = (d, mat) + mine
            value = acc[where]
            came = plane_in[d, mat, at : at + count].astype(jnp.float32)
            acc[where] = value + came.reshape(value.shape)
            return 0

        lax.fori_loop(0, part, body, 0)

    for tick in range(MICRO + bits):
        for t in range(bits + 1):
            n = tick - t
            if n < 0 or n >= MICRO:
                continue
            d = order[n]
            if t == 0:
                owns[d].wait()
                twins[d].wait_recv()

                def body(mat, _):
                    acc[d, mat] = acc[d, mat] + twin_in[d, mat].astype(jnp.float32)
                    return 0

                lax.fori_loop(0, mats, body, 0)
            else:
                for g in range(groups):
                    add_step(d, g, t - 1)
            if t < bits:
                for g in range(groups):
                    send_step(d, g, t)
            elif d:

                def body(mat, _):
                    hop_out[d - 1, mat] = acc[(d, mat) + spot.held(())].astype(hop_out.dtype)
                    return 0

                lax.fori_loop(0, mats, body, 0)
                copy = remote(
                    hop_out.at[d - 1], hop_in.at[d - 1], hop_send.at[d - 1], hop_recv.at[d - 1], spot.peer_z(d)
                )
                copy.start()
                hops.append(copy)
    for copy in hops:
        copy.wait_recv()

    def body(mat, square):
        value = acc[(0, mat) + spot.held(())]
        for d in range(MICRO - 1):
            value = value + hop_in[d, mat].astype(jnp.float32)
        share_ref[mat] = value
        return square + value * value

    square = lax.fori_loop(0, mats, body, jnp.zeros(share_ref.shape[1:], jnp.float32))
    square = jnp.sum(square, axis=0, keepdims=True)
    lanes = total_ref.shape[1]
    square = sum(square[:, n : n + lanes] for n in range(0, square.shape[1], lanes))
    row = lax.broadcasted_iota(jnp.int32, total_ref.shape, 0)
    tile = jnp.where(row == 0, square, stats_ref[...])
    sends = []

    def exchange(buffer, index, targets, at):
        buffer[index] = tile
        copies = []
        for n, to in enumerate(targets):
            copy = remote(
                buffer.at[index], buffer.at[index], stat_send.at[at + n], stat_recv.at[at + n], to
            )
            copy.start()
            copies.append(copy)
        for copy in copies:
            copy.wait()
        total = buffer[0]
        for n in range(1, buffer.shape[0]):
            total = total + buffer[n]
        return total

    tile = exchange(z_stats, z, [spot.peer_z(d) for d in range(1, MICRO)], 0)
    tile = exchange(
        plane_stats, p, [spot.in_plane((p + d) % chips, core) for d in range(1, chips)], MICRO - 1
    )
    tile = exchange(twin_stats, core, [spot.sibling()], MICRO + chips - 2)
    total_ref[...] = tile
    for copy in list(twins.values()) + list(planes.values()) + hops:
        copy.wait_send()


def reduce_all(plan, grads, low, stats):
    mats, rows, width = grads.shape[0], grads.shape[-2], grads.shape[-1]
    bits, chips = plan.bits, plan.chips
    shards = (2,) * bits
    steps = chips - 1
    any_space = pl.BlockSpec(memory_space=pl.ANY)
    vmem = pl.BlockSpec(memory_space=pltpu.VMEM)
    dma = pltpu.SemaphoreType.DMA
    return pl.pallas_call(
        functools.partial(reduce_kernel, plan),
        out_shape=(
            jax.ShapeDtypeStruct((mats, rows, width), jnp.float32),
            jax.ShapeDtypeStruct(stats.shape, jnp.float32),
        ),
        in_specs=[any_space, any_space, vmem],
        out_specs=(vmem, vmem),
        scratch_shapes=[
            pltpu.VMEM((MICRO, mats) + shards + (rows, width), jnp.float32),
            pltpu.VMEM((MICRO, mats) + shards + (rows, width), low.dtype),
            pltpu.VMEM((MICRO, mats, steps, rows, width), jnp.bfloat16),
            pltpu.VMEM((MICRO, mats, steps, rows, width), jnp.bfloat16),
            pltpu.VMEM((MICRO - 1, mats, rows, width), jnp.bfloat16),
            pltpu.VMEM((MICRO - 1, mats, rows, width), jnp.bfloat16),
            pltpu.VMEM((MICRO,) + stats.shape, jnp.float32),
            pltpu.VMEM((chips,) + stats.shape, jnp.float32),
            pltpu.VMEM((2,) + stats.shape, jnp.float32),
            dma((MICRO,)),
            dma((MICRO,)),
            dma((MICRO,)),
            dma((MICRO, bits, bits)),
            dma((MICRO, bits, bits)),
            dma((MICRO - 1,)),
            dma((MICRO - 1,)),
            dma((MICRO + chips - 1,)),
            dma((MICRO + chips - 1,)),
        ],
        compiler_params=pltpu.CompilerParams(
            collective_id=1, has_side_effects=True, vmem_limit_bytes=56 << 20
        ),
        name="reduce_all",
    )(grads, low, stats)


def sigmoid(value):
    return 1.0 / (1.0 + jnp.exp(-value))


def centred(z):
    mean = jnp.mean(z, axis=-1, keepdims=True)
    away = z - mean
    spread = jnp.mean(away * away, axis=-1, keepdims=True)
    scale = lax.rsqrt(spread + EPS_NORM)
    return away * scale, scale


def train_kernel(
    plan,
    variables,
    pack_ref,
    cells_ref,
    halo_ref,
    enc_ref,
    proc_ref,
    dec_ref,
    grads_ref,
    low_ref,
    stats_ref,
    wts,
    cells,
    halo,
    enc,
    proc,
    dec,
    grid_low,
    grid_hid,
    ext,
    hid,
    pre,
    aggs,
    grid_agg,
    out_low,
    grid_pred,
    act,
    d_inner,
    d_pre,
    d_agg,
    parcel,
    gains,
    gain_grads,
    stage,
    stage_low,
    load_sem,
    stage_sem,
    ex_send,
    ex_recv,
):
    spot = Spot(plan)
    core = spot.core
    outer, inner = core, 1 - core
    lanes = halo.shape[-1]
    last = wts.shape[0] - 1
    mesh_rows, width = hid.shape[1:]
    grid_rows = grid_hid.shape[1]
    ring = 2 * walk(spot.p, plan.width) + core

    loads = {}

    def load(name, src, dst):
        loads[name] = pltpu.make_async_copy(src, dst, load_sem.at[len(loads)])
        loads[name].start()

    load("last", pack_ref.at[last], wts.at[last])
    load("halo", halo_ref, halo)
    load("cells", cells_ref, cells)
    load("enc", enc_ref, enc)
    for n in (0, 7):
        load(n, pack_ref.at[n], wts.at[n])
    load("proc", proc_ref, proc)
    for n in (1, 4, 8, 2, 5, 9):
        load(n, pack_ref.at[n], wts.at[n])
    load("dec", dec_ref, dec)
    for n in (3, 6, 10):
        load(n, pack_ref.at[n], wts.at[n])

    def near(blk):
        q = (ring + 2 * blk - 1 + 2 * plan.chips) % (2 * plan.chips)
        return spot.in_plane(walk(q // 2, plan.width), q % 2)

    barrier = pltpu.get_barrier_semaphore()
    for side in range(2):
        pl.semaphore_signal(barrier, inc=1, device_id=near(side), device_id_type=MESH)
    pl.semaphore_wait(barrier, 2)

    def exchange(turn, blk, src):
        dst = ext.at[turn % 3, 3 * (1 - blk)]
        return remote(src, dst, ex_send.at[turn, blk], ex_recv.at[turn, blk], near(blk))

    def arrived(turn, blk):
        dst = ext.at[turn % 3, 3 * blk]
        pltpu.make_async_copy(dst, dst, ex_recv.at[turn, 1 - blk]).wait()

    def sent(turn, blk, src):
        pltpu.make_async_copy(src, src, ex_send.at[turn, blk]).wait()

    def tiles(rows, body):
        size = rows // 4

        def one(n, _):
            body(pl.ds(pl.multiple_of(n * size, 16), size))
            return 0

        lax.fori_loop(0, rows // size, one, 0)

    for name in ("last", "halo", "cells"):
        loads[name].wait()
    group = (lanes + variables) // 128 * 128
    first_gain = lanes + variables - group
    gains[...] = wts[last, :, group : group + 128].astype(jnp.float32).T

    def gain(k):
        return gains[first_gain + k : first_gain + k + 1, :]

    gain_grads[...] = jnp.zeros_like(gain_grads)
    stats_ref[...] = jnp.zeros_like(stats_ref)

    for b in range(4):
        if b in (0, 3):
            rows = halo[b // 3]
        else:
            rows = cells[(b - 1) * grid_rows : b * grid_rows, :lanes]
        hidden = right_dot(rows, wts[last, :, :lanes])
        if b in (1, 2):
            grid_hid[b - 1] = hidden
        grid_low[b] = hidden.astype(jnp.bfloat16)

    def forward(k, low_agg, base):
        value = matmul(low_agg, wts[k])
        if base is not None:
            value = value + matmul(base, wts[3 + k])
        active = (value * sigmoid(value)).astype(jnp.bfloat16)
        return value, active, matmul(active, wts[7 + k])

    def mesh_forward(k, blk):
        def body(rows):
            base = None if k == 0 else ext[k - 1, 1 + blk, rows]
            value, _, inside = forward(k, aggs[k, blk, rows], base)
            pre[k, blk, rows] = value
            result = centred(inside)[0] * gain(k)
            if k:
                result = hid[blk, rows] + result
            hid[blk, rows] = result
            ext[k, 1 + blk, rows] = result.astype(jnp.bfloat16)

        tiles(mesh_rows, body)
        exchange(k, blk, ext.at[k, 1 + blk]).start()

    def collect(graph, blk, turn):
        size = mesh_rows
        own = pl.ds(pl.multiple_of(size * (1 - blk), 128), 2 * size)
        rest = pl.ds(pl.multiple_of(2 * size * blk, 128), size)
        total = matmul(graph[blk, :, own], ext[turn, 1:3].reshape(2 * size, width))
        arrived(turn, blk)
        total = total + matmul(graph[blk, :, rest], ext[turn, 3 * blk])
        return total.astype(jnp.bfloat16)

    loads["enc"].wait()
    for blk in (outer, inner):
        senders = grid_low[pl.ds(blk, 3)].reshape(3 * grid_rows, width)
        aggs[0, blk] = matmul(enc[blk], senders).astype(jnp.bfloat16)
        if blk is outer:
            for n in (0, 7):
                loads[n].wait()
        mesh_forward(0, blk)
    loads["proc"].wait()
    for k in (1, 2):
        for n in (k, 3 + k, 7 + k):
            loads[n].wait()
        for blk in (outer, inner):
            aggs[k, blk] = collect(proc, blk, k - 1)
            mesh_forward(k, blk)

    def backward(k, value, active, inside, grad):
        along, scale = centred(inside)
        gain_grads[k : k + 1, :] += jnp.sum(along * grad, axis=0, keepdims=True)
        grad = grad * gain(k)
        grad = grad - jnp.mean(grad, axis=-1, keepdims=True)
        grad = scale * (grad - along * jnp.mean(grad * along, axis=-1, keepdims=True))
        low = grad.astype(jnp.bfloat16)
        back = right_dot(low, wts[7 + k])
        sig = sigmoid(value)
        pre_low = (back * sig * (1.0 + value * (1.0 - sig))).astype(jnp.bfloat16)
        from_agg = right_dot(pre_low, wts[k]).astype(jnp.bfloat16)
        return low, pre_low, from_agg

    def send_back(graph, blk, turn, rows):
        cols = pl.ds(pl.multiple_of(2 * mesh_rows * blk, 128), mesh_rows)
        if turn > 3:
            sent(turn - 1, blk, parcel.at[blk])
        parcel[blk] = left_dot(graph[blk, :, cols], d_agg[blk, pl.ds(0, rows)]).astype(jnp.bfloat16)
        exchange(turn, blk, parcel.at[blk]).start()

    def own_back(graph, b, rows):
        total = None
        for blk in range(2):
            region = b - blk + 1
            cols = pl.ds(pl.multiple_of(region * mesh_rows, 128), mesh_rows)
            part = left_dot(graph[blk, :, cols], d_agg[blk, pl.ds(0, rows)])
            total = part if total is None else total + part
        return total

    stages = []

    def put(mat, value):
        side = len(stages) % 2
        if len(stages) >= 2:
            for copy in stages[-2]:
                copy.wait()
        stage[side] = value
        stage_low[side] = value.astype(jnp.bfloat16)
        copies = (
            pltpu.make_async_copy(stage.at[side], grads_ref.at[mat], stage_sem.at[side, 0]),
            pltpu.make_async_copy(stage_low.at[side], low_ref.at[mat], stage_sem.at[side, 1]),
        )
        for copy in copies:
            copy.start()
        stages.append(copies)

    def flat(value):
        return value.reshape(value.shape[0] * value.shape[1], value.shape[2])

    loads["dec"].wait()
    for n in (3, 6, 10):
        loads[n].wait()
    for blk in (outer, inner):
        grid_agg[blk] = collect(dec, blk, 2)

        def body(rows):
            base = grid_low[1 + blk, rows]
            value, active, inside = forward(3, grid_agg[blk, rows], base)
            out = grid_hid[blk, rows] + centred(inside)[0] * gain(3)
            low = out.astype(jnp.bfloat16)
            out_low[blk, rows] = low
            size = low.shape[0]
            cell = pl.ds(pl.multiple_of(blk * grid_rows + rows.start, 16), size)
            lane = lax.broadcasted_iota(jnp.int32, (size, 128), 1)
            tail = cells[cell, group : group + 128].astype(jnp.float32)
            piece = (lane >= first_gain) & (lane < first_gain + 3)
            weight = jnp.sum(jnp.where(piece, tail, 0.0), axis=1, keepdims=True)
            error = matmul(low, wts[last, :, lanes : 2 * lanes])
            error = error - cells[cell, lanes : 2 * lanes].astype(jnp.float32)
            place = lax.broadcasted_iota(jnp.int32, error.shape, 1)
            error = jnp.where(place < variables, error, 0.0)
            weighted = weight * error
            loss = jnp.sum(weighted * error, axis=0, keepdims=True)
            stats_ref[1:2, :] += sum(loss[:, n : n + 128] for n in range(0, lanes, 128))
            stats_ref[2:3, :] += jnp.sum(jnp.where(lane == 0, weight, 0.0), axis=0, keepdims=True)
            pred_low = (2.0 * weighted).astype(jnp.bfloat16)
            grid_pred[blk, rows] = pred_low
            grad = right_dot(pred_low, wts[last, :, lanes : 2 * lanes])
            inner_low, pre_low, from_agg = backward(3, value, active, inside, grad)
            act[blk, rows] = active
            d_inner[blk, rows] = inner_low
            d_pre[blk, rows] = pre_low
            d_agg[blk, rows] = from_agg
            grid_hid[blk, rows] = grad + right_dot(pre_low, wts[6])

        tiles(grid_rows, body)
        send_back(dec, blk, 3, grid_rows)
    used = pl.ds(0, grid_rows)
    for b in range(2):
        hid[b] = own_back(dec, b, grid_rows)
    put(10, left_dot(flat(act[:, used]), flat(d_inner[:, used])))
    put(3, left_dot(flat(grid_agg[...]), flat(d_pre[:, used])))
    put(6, left_dot(flat(grid_low[1:3]), flat(d_pre[:, used])))
    head_grad = left_dot(flat(out_low[...]), flat(grid_pred[...]))

    def finish(turn, blk, total_ref, add):
        arrived(turn, blk)

        def body(rows):
            total = total_ref[blk, rows] + ext[turn % 3, 3 * blk, rows].astype(jnp.float32)
            total = total.astype(jnp.bfloat16).astype(jnp.float32)
            hid[blk, rows] = hid[blk, rows] + total if add else total

        tiles(mesh_rows, body)

    def mesh_backward(k, blk):
        def body(rows):
            value = pre[k, blk, rows]
            active = (value * sigmoid(value)).astype(jnp.bfloat16)
            grad = hid[blk, rows]
            inner_low, pre_low, from_agg = backward(k, value, active, matmul(active, wts[7 + k]), grad)
            act[blk, rows] = active
            d_inner[blk, rows] = inner_low
            d_pre[blk, rows] = pre_low
            d_agg[blk, rows] = from_agg
            if k:
                hid[blk, rows] = grad + right_dot(pre_low, wts[3 + k])

        tiles(mesh_rows, body)

    turn = 3
    for k in (2, 1):
        for blk in (outer, inner):
            finish(turn, blk, hid if k == 2 else pre.at[2], k < 2)
            mesh_backward(k, blk)
            send_back(proc, blk, turn + 1, mesh_rows)
        turn += 1
        for b in range(2):
            pre[k, b] = own_back(proc, b, mesh_rows)
        put(7 + k, left_dot(flat(act[...]), flat(d_inner[...])))
        put(k, left_dot(flat(aggs[k]), flat(d_pre[...])))
        put(3 + k, left_dot(flat(ext[k - 1, 1:3]), flat(d_pre[...])))
    for blk in (outer, inner):
        finish(turn, blk, pre.at[1], True)
        mesh_backward(0, blk)
    put(7, left_dot(flat(act[...]), flat(d_inner[...])))
    put(0, left_dot(flat(aggs[0]), flat(d_pre[...])))
    embed_grad = None
    for b in range(4):
        total = None
        for blk in range(2):
            region = b - blk
            if 0 <= region < 3:
                cols = slice(region * grid_rows, (region + 1) * grid_rows)
                part = left_dot(enc[blk, :, cols], d_agg[blk])
                total = part if total is None else total + part
        low = total.astype(jnp.bfloat16)
        if b in (1, 2):
            low = (grid_hid[b - 1] + low.astype(jnp.float32)).astype(jnp.bfloat16)
            rows = cells[(b - 1) * grid_rows : b * grid_rows, :lanes]
        else:
            rows = halo[b // 3]
        part = left_dot(low, rows)
        embed_grad = part if embed_grad is None else embed_grad + part
    gains[...] = jnp.zeros_like(gains)
    gains[first_gain : first_gain + 4, :] = gain_grads[0:4, :]
    across = gains[...].T
    split = group - lanes
    put(
        last,
        jnp.concatenate([embed_grad, head_grad[:, :split], head_grad[:, split:] + across], axis=1),
    )
    for copies in stages[-2:]:
        for copy in copies:
            copy.wait()
    for blk in range(2):
        for n in range(3):
            sent(n, blk, ext.at[n, 1 + blk])
        sent(5, blk, parcel.at[blk])


def train(plan, variables, pack, cells, halo, encoder, processor, decoder):
    mats, width = pack.shape[0], pack.shape[2]
    lanes = halo.shape[-1]
    mesh_rows, grid_rows = encoder.shape[1], decoder.shape[1]
    any_space = pl.BlockSpec(memory_space=pl.ANY)
    dma = pltpu.SemaphoreType.DMA
    low, full = jnp.bfloat16, jnp.float32
    mesh_pair, grid_pair = (2, mesh_rows, width), (2, grid_rows, width)
    return pl.pallas_call(
        functools.partial(train_kernel, plan, variables),
        out_shape=(
            jax.ShapeDtypeStruct(pack.shape, full),
            jax.ShapeDtypeStruct(pack.shape, low),
            jax.ShapeDtypeStruct((8, 128), full),
        ),
        in_specs=[any_space] * 6,
        out_specs=(any_space, any_space, pl.BlockSpec(memory_space=pltpu.VMEM)),
        scratch_shapes=[
            pltpu.VMEM(pack.shape, low),
            pltpu.VMEM(cells.shape, low),
            pltpu.VMEM(halo.shape, low),
            pltpu.VMEM(encoder.shape, low),
            pltpu.VMEM(processor.shape, low),
            pltpu.VMEM(decoder.shape, low),
            pltpu.VMEM((4,) + grid_pair[1:], low),
            pltpu.VMEM(grid_pair, full),
            pltpu.VMEM((3, 4) + mesh_pair[1:], low),
            pltpu.VMEM(mesh_pair, full),
            pltpu.VMEM((3,) + mesh_pair, full),
            pltpu.VMEM((3,) + mesh_pair, low),
            pltpu.VMEM(grid_pair, low),
            pltpu.VMEM(grid_pair, low),
            pltpu.VMEM((2, grid_rows, lanes), low),
            pltpu.VMEM(mesh_pair, low),
            pltpu.VMEM(mesh_pair, low),
            pltpu.VMEM(mesh_pair, low),
            pltpu.VMEM(mesh_pair, low),
            pltpu.VMEM(mesh_pair, low),
            pltpu.VMEM((128, width), full),
            pltpu.VMEM((8, width), full),
            pltpu.VMEM((2, width, width), full),
            pltpu.VMEM((2, width, width), low),
            dma((mats + 5,)),
            dma((2, 2)),
            dma((6, 2)),
            dma((6, 2)),
        ],
        compiler_params=pltpu.CompilerParams(
            collective_id=2, has_side_effects=True, vmem_limit_bytes=63 << 20
        ),
        name="train",
    )(pack, cells, halo, encoder, processor, decoder)


def adamw(param, first, second, grad, scale, rate):
    clipped = grad * scale
    moment = BETA_ONE * first + (1.0 - BETA_ONE) * clipped
    square = BETA_TWO * second + (1.0 - BETA_TWO) * clipped * clipped
    fixed_one = moment / (1.0 - BETA_ONE**STEP)
    fixed_two = square / (1.0 - BETA_TWO**STEP)
    fresh = param - rate * (fixed_one / (jnp.sqrt(fixed_two) + EPS_ADAM) + DECAY * param)
    return (fresh, moment, square, fresh.astype(jnp.bfloat16))


def on_device(
    plan,
    grid_in,
    targets,
    area_weight,
    grid_count,
    g2m_edges,
    mesh_edges,
    m2g_edges,
    edge_count,
    embed_weight,
    embed_first,
    embed_second,
    node_mats,
    mats_first,
    mats_second,
    head_weight,
    head_first,
    head_second,
    norm_gains,
    gains_first,
    gains_second,
):
    half, variables = grid_in.shape[1:]
    grid_rows = 2 * half
    mesh_rows = M_DEV
    lanes = -(-variables // 128) * 128
    core = lax.axis_index("feat")

    position = core * half + jnp.arange(half, dtype=jnp.int32)
    weights = jnp.where(position[None, :] < grid_count, area_weight, 0.0)
    pieces = []
    rest = weights
    for _ in range(3):
        piece = lax.reduce_precision(rest, 8, 7)
        pieces.append(piece.astype(jnp.bfloat16))
        rest = rest - piece
    cells = jnp.concatenate(
        [
            jnp.pad(grid_in, ((0, 0), (0, 0), (0, lanes - variables))),
            targets,
            jnp.pad(jnp.stack(pieces, axis=-1), ((0, 0), (0, 0), (0, lanes - variables - 3))),
        ],
        axis=-1,
    )
    last = jnp.concatenate(
        [
            jnp.pad(embed_weight.T, ((0, 0), (0, lanes - variables))),
            head_weight,
            jnp.pad(norm_gains.T, ((0, 0), (0, lanes - variables - 4))),
        ],
        axis=-1,
    )
    pack = jnp.concatenate([node_mats, last[None]]).astype(jnp.bfloat16)
    graphs = ((g2m_edges, grid_rows, mesh_rows), (mesh_edges, mesh_rows, mesh_rows), (m2g_edges, mesh_rows, grid_rows))
    codes, shapes = [], []
    first = 0
    for n, (edges, columns, rows) in enumerate(graphs):
        per = edges.shape[1]
        alive = jnp.arange(per, dtype=jnp.int32) < edge_count[n, 0]
        codes.append(jnp.where(alive, edges[1] * (1 << CODE_BITS) + edges[0], -1))
        shapes.append((first // 128, per, rows, 3 * columns))
        first += per
    codes = jnp.concatenate(codes).reshape(-1, 128)
    gathered, main, halo, encoder, processor, decoder = gather_all(plan, shapes, pack, cells, codes)
    width = pack.shape[2]
    full = gathered.reshape(-1, width, width)
    main = main.reshape(-1, 2 * lanes)
    halo = halo.reshape(2, grid_rows, lanes)
    grads, low, stats = train(plan, variables, full, main, halo, encoder, processor, decoder)
    grads, low = (value.reshape(gathered.shape) for value in (grads, low))
    share, total = reduce_all(plan, grads, low, stats)
    square_sum, loss_sum, weight_sum = (jnp.sum(total[n]) for n in range(3))
    shares = (
        share[-1, :, :variables].T,
        share[:-1],
        share[-1, :, lanes : lanes + variables],
        share[-1, :, lanes + variables : lanes + variables + 4].T,
    )
    grad_norm = jnp.sqrt(square_sum)
    scale = jnp.minimum(1.0, CLIP / (grad_norm + 1e-06))
    return (
        loss_sum,
        weight_sum,
        grad_norm,
        *adamw(embed_weight, embed_first, embed_second, shares[0], scale, RATE),
        *adamw(node_mats, mats_first, mats_second, shares[1], scale, RATE),
        *adamw(head_weight, head_first, head_second, shares[2], scale, RATE),
        *adamw(norm_gains, gains_first, gains_second, shares[3], scale, GAIN_RATE),
    )


def solution(mesh):
    plan = Plan(mesh.shape["nodes"])
    cells = P(None, BOTH, None)
    columns = P(None, BOTH)
    rows = P(BOTH, None)
    blocks = P(None, "nodes")
    return jax.shard_map(
        lambda *args: on_device(plan, *args),
        mesh=mesh,
        in_specs=(
            (cells, cells, columns, blocks, blocks, blocks, blocks, blocks)
            + (columns,) * 3
            + (cells,) * 3
            + (rows,) * 3
            + (columns,) * 3
        ),
        out_specs=(P(), P(), P()) + (columns,) * 4 + (cells,) * 4 + (rows,) * 4 + (columns,) * 4,
        check_vma=False,
    )
```

```python
import functools
import math

import jax
import jax.numpy as jnp
from jax import lax
from jax.experimental import pallas as pl
from jax.experimental.pallas import tpu as pltpu
from jax.sharding import PartitionSpec as P

M_DEV = 640
STEP = 5
MICRO = 4


EPS_NORM = 1e-05
CLIP = 0.5
RATE = 0.04
GAIN_RATE = 0.4
BETA_ONE = 0.5
BETA_TWO = 0.6
EPS_ADAM = 1e-08
DECAY = 0.1

BOTH = ("nodes", "feat")


def matmul(a, b):
    return jnp.dot(a, b, preferred_element_type=jnp.float32)


def left_dot(a, b):
    return lax.dot_general(a, b, (((0,), (0,)), ((), ())), preferred_element_type=jnp.float32)


def right_dot(a, b):
    return lax.dot_general(a, b, (((1,), (1,)), ((), ())), preferred_element_type=jnp.float32)


class Plan:
    def __init__(self, nodes):
        self.nodes = nodes
        self.chips = nodes // MICRO
        self.bits = self.chips.bit_length() - 1
        width = math.isqrt(self.chips)
        self.width = width if width * width == self.chips else 0


MESH = pl.DeviceIdType.MESH
CODE_BITS = 12


def walk(value, width):
    if width == 0:
        return value
    row, col = value // width, value % width
    return row * width + col + (row % 2) * (width - 1 - 2 * col)


class Spot:
    def __init__(self, plan):
        me = lax.axis_index("nodes")
        self.plan = plan
        self.core = lax.axis_index("feat")
        self.z = me // plan.chips
        self.p = me % plan.chips

    def bit(self, b):
        return (self.p // (1 << b)) % 2

    def peer_z(self, d):
        return {"nodes": ((self.z + d) % MICRO) * self.plan.chips + self.p, "feat": self.core}

    def peer_bit(self, b):
        other = self.p + (1 - 2 * self.bit(b)) * (1 << b)
        return {"nodes": self.z * self.plan.chips + other, "feat": self.core}

    def in_plane(self, p, core):
        return {"nodes": self.z * self.plan.chips + p, "feat": core}

    def sibling(self):
        return self.in_plane(self.p, 1 - self.core)

    def partners(self):
        chips = self.plan.chips
        found = [self.peer_z(d) for d in range(1, MICRO)]
        for turn in range(chips):
            p = (self.p + turn) % chips
            if turn:
                found.append(self.in_plane(p, self.core))
            found.append(self.in_plane(p, 1 - self.core))
        return found

    def meet(self):
        barrier = pltpu.get_barrier_semaphore()
        found = self.partners()
        for other in found:
            pl.semaphore_signal(barrier, inc=1, device_id=other, device_id_type=MESH)
        pl.semaphore_wait(barrier, len(found))

    def held(self, done):
        bits = range(self.plan.bits - 1, -1, -1)
        return tuple(slice(None) if b in done else self.bit(b) for b in bits)


def remote(src, dst, send, recv, to):
    return pltpu.make_async_remote_copy(
        src_ref=src, dst_ref=dst, send_sem=send, recv_sem=recv, device_id=to, device_id_type=MESH
    )


def gather_kernel(
    plan,
    shapes,
    pack_ref,
    cells_ref,
    codes_ref,
    all_ref,
    main_ref,
    halo_ref,
    enc_ref,
    proc_ref,
    dec_ref,
    graph_ref,
    total,
    whole,
    cell_hop,
    code_hop,
    own_sem,
    out_sem,
    hop_send,
    hop_recv,
    plane_send,
    plane_recv,
    twin_send,
    twin_recv,
    move_send,
    move_recv,
):
    spot = Spot(plan)
    z, p, core = spot.z, spot.p, spot.core
    chips, bits = plan.chips, plan.bits
    groups = bits
    mats = pack_ref.shape[0] // groups
    code_rows = codes_ref.shape[0] // 2
    lanes = halo_ref.shape[-1]
    own = pltpu.make_async_copy(pack_ref, all_ref.at[(slice(None), z) + spot.held(()) + (core,)], own_sem)
    own.start()
    spot.meet()
    my_codes = codes_ref.at[pl.ds(pl.multiple_of(core * code_rows, 8), code_rows)]
    hops = []
    for d in range(1, MICRO):
        to = spot.peer_z(d)
        m = (z + d) % MICRO
        for n, (src, dst) in enumerate(
            (
                (my_codes, code_hop.at[d - 1]),
                (cells_ref.at[m], cell_hop.at[d - 1]),
                (pack_ref, all_ref.at[(slice(None), z) + spot.held(()) + (core,)]),
            )
        ):
            copy = remote(src, dst, hop_send.at[d - 1, n], hop_recv.at[d - 1, n], to)
            copy.start()
            hops.append(copy)
    quarter = p % 4
    bb, to_core = quarter % 2, quarter // 2
    slot = bb * 2 + core
    half_slot = (1 - bb) * 2 + core
    moves = []

    def move(d, n, src, dst, sem, chip, to_core):
        here = jnp.logical_and(chip == p, to_core == core)
        copy = remote(src, dst, move_send.at[d, n], sem, spot.in_plane(chip, to_core))

        @pl.when(here)
        def _():
            pltpu.make_async_copy(src, dst, sem).start()

        @pl.when(jnp.logical_not(here))
        def _():
            copy.start()

        moves.append((here, copy))

    def spread_codes(d):
        block = ((z - d) % MICRO) * chips + p
        codes = my_codes if d == 0 else code_hop.at[d - 1]
        rows = pl.ds(pl.multiple_of(core * code_rows, 8), code_rows)
        dst = graph_ref.at[bb, rows]
        move(d, 0, codes, dst, move_recv.at[0, slot], walk(block // 4, plan.width), to_core)

    def spread(d):
        block = ((z - d) % MICRO) * chips + p
        j = block // 4
        chip = walk(j, plan.width)
        q = (2 * j + to_core + 2 * bb - 1) % (2 * chips)
        near = walk(q // 2, plan.width)
        cells = cells_ref.at[z] if d == 0 else cell_hop.at[d - 1]
        move(
            d,
            1,
            cells.at[:, pl.ds(0, lanes)],
            halo_ref.at[1 - bb, core],
            move_recv.at[1, half_slot],
            near,
            q % 2,
        )
        move(d, 2, cells, main_ref.at[bb, core], move_recv.at[2, slot], chip, to_core)

    def region(d, done):
        return ((z - d) % MICRO,) + spot.held(done) + (core,)

    planes = {}

    def step(d, g, t):
        done = tuple((g + s) % bits for s in range(t))
        where = (pl.ds(g * mats, mats),) + region(d, done)
        copy = remote(
            all_ref.at[where],
            all_ref.at[where],
            plane_send.at[d, g, t],
            plane_recv.at[d, g, t],
            spot.peer_bit((g + t) % bits),
        )
        copy.start()
        planes[d, g, t] = copy

    for d in range(MICRO):
        if d:
            hops[3 * (d - 1)].wait_recv()
        spread_codes(d)
    outs = []

    def build(n, side_block):
        first, edges, rows, columns = shapes[n]
        chunk = math.gcd(edges, 1024) // 128
        area = (pl.ds(0, rows), pl.ds(0, columns))

        def ones(row, count):
            place = lax.broadcasted_iota(jnp.int32, (count, 128), 0).astype(jnp.int16)
            hit = place == row.astype(jnp.int16)
            return jnp.where(hit, jnp.bfloat16(1), jnp.bfloat16(0)).astype(jnp.float8_e4m3fn)

        def body(k, _):
            into, out = [], []
            for i in range(chunk):
                code = graph_ref[side_block, pl.ds(first + k * chunk + i, 1), :]
                into.append(ones(code >> CODE_BITS, rows))
                out.append(ones(code & ((1 << CODE_BITS) - 1), columns))
            total[area] += right_dot(jnp.concatenate(into, axis=1), jnp.concatenate(out, axis=1))
            return 0

        total[area] = jnp.zeros((rows, columns), jnp.float32)
        lax.fori_loop(0, edges // (128 * chunk), body, 0)
        if len(outs) >= 2:
            outs[-2].wait()
        side = len(outs) % 2
        whole[(side,) + area] = total[area].astype(jnp.bfloat16)
        ref = (enc_ref, proc_ref, dec_ref)[n]
        copy = pltpu.make_async_copy(whole.at[(side,) + area], ref.at[side_block], out_sem.at[side])
        copy.start()
        outs.append(copy)

    work = [[], [(0, 0), (0, 1)], [(1, 0)], [(1, 1)], [(2, 0)], [(2, 1)]]
    twins = []
    for tick in range(MICRO + bits):
        for t in range(bits + 1):
            d = tick - t
            if d < 0 or d >= MICRO:
                continue
            if t == 0:
                if d == 0:
                    own.wait()
                else:
                    hops[3 * (d - 1) + 1].wait_recv()
                    hops[3 * (d - 1) + 2].wait_recv()
                spread(d)
            else:
                for g in range(groups):
                    planes[d, g, t - 1].wait_recv()
            if t < bits:
                for g in range(groups):
                    step(d, g, t)
            else:
                where = (slice(None),) + region(d, tuple(range(bits)))
                copy = remote(
                    all_ref.at[where], all_ref.at[where], twin_send.at[d], twin_recv.at[d], spot.sibling()
                )
                copy.start()
                twins.append(copy)
        if tick == 1:
            for n in range(4):
                dst = graph_ref.at[n // 2, pl.ds((n % 2) * code_rows, code_rows)]
                pltpu.make_async_copy(dst, dst, move_recv.at[0, n]).wait()
        for kind, block in work[tick] if tick < len(work) else []:
            build(kind, block)
    for copy in outs[-2:]:
        copy.wait()
    for copy in hops + list(planes.values()):
        copy.wait_send()
    for copy in twins:
        copy.wait()
    for here, copy in moves:

        @pl.when(jnp.logical_not(here))
        def _():
            copy.wait_send()

    for n in range(4):
        half, side = n % 2, n // 2
        for kind, dst in ((1, halo_ref.at[side, half]), (2, main_ref.at[side, half])):
            pltpu.make_async_copy(dst, dst, move_recv.at[kind, n]).wait()


def gather_all(plan, shapes, pack, cells, codes):
    mats, rows, width = pack.shape
    micro, half, lanes = cells.shape
    bits = plan.bits
    most_rows = max(shape[2] for shape in shapes)
    most_columns = max(shape[3] for shape in shapes)
    any_space = pl.BlockSpec(memory_space=pl.ANY)
    dma = pltpu.SemaphoreType.DMA
    return pl.pallas_call(
        functools.partial(gather_kernel, plan, shapes),
        out_shape=(
            jax.ShapeDtypeStruct((mats, MICRO) + (2,) * bits + (2, rows, width), pack.dtype),
            jax.ShapeDtypeStruct((2, 2, half, lanes), cells.dtype),
            jax.ShapeDtypeStruct((2, 2, half, lanes // 2), cells.dtype),
            *(jax.ShapeDtypeStruct((2,) + shape[2:], jnp.bfloat16) for shape in shapes),
        ),
        in_specs=[any_space] * 3,
        out_specs=(any_space,) * 6,
        scratch_shapes=[
            pltpu.VMEM((2,) + codes.shape, codes.dtype),
            pltpu.VMEM((most_rows, most_columns), jnp.float32),
            pltpu.VMEM((2, most_rows, most_columns), jnp.bfloat16),
            pltpu.VMEM((MICRO - 1, half, lanes), cells.dtype),
            pltpu.VMEM((MICRO - 1, codes.shape[0] // 2, codes.shape[1]), codes.dtype),
            dma,
            dma((2,)),
            dma((MICRO - 1, 3)),
            dma((MICRO - 1, 3)),
            dma((MICRO, bits, bits)),
            dma((MICRO, bits, bits)),
            dma((MICRO,)),
            dma((MICRO,)),
            dma((MICRO, 3)),
            dma((3, 4)),
        ],
        compiler_params=pltpu.CompilerParams(
            collective_id=0, has_side_effects=True, vmem_limit_bytes=48 << 20
        ),
        name="gather_all",
    )(pack, cells, codes)


def reduce_kernel(
    plan,
    grads_ref,
    low_ref,
    stats_ref,
    share_ref,
    total_ref,
    acc,
    twin_in,
    plane_out,
    plane_in,
    hop_out,
    hop_in,
    z_stats,
    plane_stats,
    twin_stats,
    own_sem,
    twin_send,
    twin_recv,
    plane_send,
    plane_recv,
    hop_send,
    hop_recv,
    stat_send,
    stat_recv,
):
    spot = Spot(plan)
    z, p, core = spot.z, spot.p, spot.core
    chips, bits = plan.chips, plan.bits
    groups = bits
    mats = grads_ref.shape[0]
    part = mats // groups
    every = (slice(None),) * bits
    order = [1, 2, 3, 0]
    owns = {}
    for d in order:
        item = (z + d) % MICRO
        owns[d] = pltpu.make_async_copy(
            grads_ref.at[(slice(None), item) + every + (core,)], acc.at[d], own_sem.at[d]
        )
        owns[d].start()
    spot.meet()
    twins = {}
    for d in order:
        item = (z + d) % MICRO
        twins[d] = remote(
            low_ref.at[(slice(None), item) + every + (1 - core,)],
            twin_in.at[d],
            twin_send.at[d],
            twin_recv.at[d],
            spot.sibling(),
        )
        twins[d].start()

    def starts(t):
        return sum(1 << (bits - 1 - s) for s in range(t))

    planes, hops = {}, []

    def send_step(d, g, t):
        done = tuple((g + s) % bits for s in range(t))
        b = (g + t) % bits
        count = 1 << (bits - 1 - t)
        at = starts(t)
        theirs = tuple(
            spot.bit(n) if n in done else (1 - spot.bit(n) if n == b else slice(None))
            for n in range(bits - 1, -1, -1)
        )

        def body(n, _):
            mat = g * part + n
            value = acc[(d, mat) + theirs]
            plane_out[d, mat, at : at + count] = value.reshape((count,) + value.shape[-2:]).astype(
                plane_out.dtype
            )
            return 0

        lax.fori_loop(0, part, body, 0)
        where = (d, pl.ds(g * part, part), pl.ds(at, count))
        planes[d, g, t] = remote(
            plane_out.at[where],
            plane_in.at[where],
            plane_send.at[d, g, t],
            plane_recv.at[d, g, t],
            spot.peer_bit(b),
        )
        planes[d, g, t].start()

    def add_step(d, g, t):
        planes[d, g, t].wait_recv()
        done = tuple((g + s) % bits for s in range(t + 1))
        count = 1 << (bits - 1 - t)
        at = starts(t)
        mine = tuple(spot.bit(n) if n in done else slice(None) for n in range(bits - 1, -1, -1))

        def body(n, _):
            mat = g * part + n
            where = (d, mat) + mine
            value = acc[where]
            came = plane_in[d, mat, at : at + count].astype(jnp.float32)
            acc[where] = value + came.reshape(value.shape)
            return 0

        lax.fori_loop(0, part, body, 0)

    for tick in range(MICRO + bits):
        for t in range(bits + 1):
            n = tick - t
            if n < 0 or n >= MICRO:
                continue
            d = order[n]
            if t == 0:
                owns[d].wait()
                twins[d].wait_recv()

                def body(mat, _):
                    acc[d, mat] = acc[d, mat] + twin_in[d, mat].astype(jnp.float32)
                    return 0

                lax.fori_loop(0, mats, body, 0)
            else:
                for g in range(groups):
                    add_step(d, g, t - 1)
            if t < bits:
                for g in range(groups):
                    send_step(d, g, t)
            elif d:

                def body(mat, _):
                    hop_out[d - 1, mat] = acc[(d, mat) + spot.held(())].astype(hop_out.dtype)
                    return 0

                lax.fori_loop(0, mats, body, 0)
                copy = remote(
                    hop_out.at[d - 1], hop_in.at[d - 1], hop_send.at[d - 1], hop_recv.at[d - 1], spot.peer_z(d)
                )
                copy.start()
                hops.append(copy)
    for copy in hops:
        copy.wait_recv()

    def body(mat, square):
        value = acc[(0, mat) + spot.held(())]
        for d in range(MICRO - 1):
            value = value + hop_in[d, mat].astype(jnp.float32)
        share_ref[mat] = value
        return square + value * value

    square = lax.fori_loop(0, mats, body, jnp.zeros(share_ref.shape[1:], jnp.float32))
    square = jnp.sum(square, axis=0, keepdims=True)
    lanes = total_ref.shape[1]
    square = sum(square[:, n : n + lanes] for n in range(0, square.shape[1], lanes))
    row = lax.broadcasted_iota(jnp.int32, total_ref.shape, 0)
    tile = jnp.where(row == 0, square, stats_ref[...])
    sends = []

    def exchange(buffer, index, targets, at):
        buffer[index] = tile
        copies = []
        for n, to in enumerate(targets):
            copy = remote(
                buffer.at[index], buffer.at[index], stat_send.at[at + n], stat_recv.at[at + n], to
            )
            copy.start()
            copies.append(copy)
        for copy in copies:
            copy.wait()
        total = buffer[0]
        for n in range(1, buffer.shape[0]):
            total = total + buffer[n]
        return total

    tile = exchange(z_stats, z, [spot.peer_z(d) for d in range(1, MICRO)], 0)
    tile = exchange(
        plane_stats, p, [spot.in_plane((p + d) % chips, core) for d in range(1, chips)], MICRO - 1
    )
    tile = exchange(twin_stats, core, [spot.sibling()], MICRO + chips - 2)
    total_ref[...] = tile
    for copy in list(twins.values()) + list(planes.values()) + hops:
        copy.wait_send()


def reduce_all(plan, grads, low, stats):
    mats, rows, width = grads.shape[0], grads.shape[-2], grads.shape[-1]
    bits, chips = plan.bits, plan.chips
    shards = (2,) * bits
    steps = chips - 1
    any_space = pl.BlockSpec(memory_space=pl.ANY)
    vmem = pl.BlockSpec(memory_space=pltpu.VMEM)
    dma = pltpu.SemaphoreType.DMA
    return pl.pallas_call(
        functools.partial(reduce_kernel, plan),
        out_shape=(
            jax.ShapeDtypeStruct((mats, rows, width), jnp.float32),
            jax.ShapeDtypeStruct(stats.shape, jnp.float32),
        ),
        in_specs=[any_space, any_space, vmem],
        out_specs=(vmem, vmem),
        scratch_shapes=[
            pltpu.VMEM((MICRO, mats) + shards + (rows, width), jnp.float32),
            pltpu.VMEM((MICRO, mats) + shards + (rows, width), low.dtype),
            pltpu.VMEM((MICRO, mats, steps, rows, width), jnp.bfloat16),
            pltpu.VMEM((MICRO, mats, steps, rows, width), jnp.bfloat16),
            pltpu.VMEM((MICRO - 1, mats, rows, width), jnp.bfloat16),
            pltpu.VMEM((MICRO - 1, mats, rows, width), jnp.bfloat16),
            pltpu.VMEM((MICRO,) + stats.shape, jnp.float32),
            pltpu.VMEM((chips,) + stats.shape, jnp.float32),
            pltpu.VMEM((2,) + stats.shape, jnp.float32),
            dma((MICRO,)),
            dma((MICRO,)),
            dma((MICRO,)),
            dma((MICRO, bits, bits)),
            dma((MICRO, bits, bits)),
            dma((MICRO - 1,)),
            dma((MICRO - 1,)),
            dma((MICRO + chips - 1,)),
            dma((MICRO + chips - 1,)),
        ],
        compiler_params=pltpu.CompilerParams(
            collective_id=1, has_side_effects=True, vmem_limit_bytes=56 << 20
        ),
        name="reduce_all",
    )(grads, low, stats)


def sigmoid(value):
    return 1.0 / (1.0 + jnp.exp(-value))


def centred(z):
    mean = jnp.mean(z, axis=-1, keepdims=True)
    away = z - mean
    spread = jnp.mean(away * away, axis=-1, keepdims=True)
    scale = lax.rsqrt(spread + EPS_NORM)
    return away * scale, scale


def network(
    plan,
    spot,
    variables,
    hooks,
    stats_ref,
    wts,
    cells,
    halo,
    enc,
    proc,
    dec,
    grid_low,
    grid_hid,
    ext,
    hid,
    pre,
    aggs,
    grid_agg,
    head_grad,
    act,
    d_inner,
    d_pre,
    d_agg,
    parcel,
    gains,
    gain_grads,
    ex_send,
    ex_recv,
):
    core = spot.core
    outer, inner = core, 1 - core
    lanes = halo.shape[-1]
    last = wts.shape[0] - 1
    mesh_rows, width = hid.shape[1:]
    grid_rows = grid_hid.shape[1]
    ring = 2 * walk(spot.p, plan.width) + core

    def near(blk):
        q = (ring + 2 * blk - 1 + 2 * plan.chips) % (2 * plan.chips)
        return spot.in_plane(walk(q // 2, plan.width), q % 2)

    def exchange(turn, blk, src):
        dst = ext.at[turn % 3, 3 * (1 - blk)]
        return remote(src, dst, ex_send.at[turn, blk], ex_recv.at[turn, blk], near(blk))

    def arrived(turn, blk):
        dst = ext.at[turn % 3, 3 * blk]
        pltpu.make_async_copy(dst, dst, ex_recv.at[turn, 1 - blk]).wait()

    def sent(turn, blk, src):
        pltpu.make_async_copy(src, src, ex_send.at[turn, blk]).wait()

    def tiles(rows, body):
        size = rows // 4

        def one(n, _):
            body(pl.ds(pl.multiple_of(n * size, 16), size))
            return 0

        lax.fori_loop(0, rows // size, one, 0)

    hooks.need("last", "halo", "cells")
    group = (lanes + variables) // 128 * 128
    first_gain = lanes + variables - group
    gains[...] = wts[last, :, group : group + 128].astype(jnp.float32).T

    def gain(k):
        return gains[first_gain + k : first_gain + k + 1, :]

    gain_grads[...] = jnp.zeros_like(gain_grads)
    head_grad[...] = jnp.zeros_like(head_grad)
    stats_ref[...] = jnp.zeros_like(stats_ref)

    for b in range(4):
        if b in (0, 3):
            rows = halo[b // 3]
        else:
            rows = cells[(b - 1) * grid_rows : b * grid_rows, :lanes]
        hidden = right_dot(rows, wts[last, :, :lanes])
        if b in (1, 2):
            grid_hid[b - 1] = hidden
        grid_low[b] = hidden.astype(jnp.bfloat16)

    def forward(k, low_agg, base):
        value = matmul(low_agg, wts[k])
        if base is not None:
            value = value + matmul(base, wts[3 + k])
        active = (value * sigmoid(value)).astype(jnp.bfloat16)
        return value, active, matmul(active, wts[7 + k])

    def mesh_forward(k, blk):
        def body(rows):
            base = None if k == 0 else ext[k - 1, 1 + blk, rows]
            value, _, inside = forward(k, aggs[k, blk, rows], base)
            if k:
                pre[k - 1, blk, rows] = value
            result = centred(inside)[0] * gain(k)
            if k:
                result = hid[blk, rows] + result
            hid[blk, rows] = result
            ext[k, 1 + blk, rows] = result.astype(jnp.bfloat16)

        tiles(mesh_rows, body)
        exchange(k, blk, ext.at[k, 1 + blk]).start()

    def collect(graph, blk, turn):
        size = mesh_rows
        own = pl.ds(pl.multiple_of(size * (1 - blk), 128), 2 * size)
        rest = pl.ds(pl.multiple_of(2 * size * blk, 128), size)
        total = matmul(graph[blk, :, own], ext[turn, 1:3].reshape(2 * size, width))
        arrived(turn, blk)
        total = total + matmul(graph[blk, :, rest], ext[turn, 3 * blk])
        return total.astype(jnp.bfloat16)

    hooks.need("enc")
    for blk in (outer, inner):
        senders = grid_low[pl.ds(blk, 3)].reshape(3 * grid_rows, width)
        aggs[0, blk] = matmul(enc[blk], senders).astype(jnp.bfloat16)
        if blk is outer:
            hooks.need(0, 7)
        mesh_forward(0, blk)
    hooks.need("proc")
    for k in (1, 2):
        hooks.need(k, 3 + k, 7 + k)
        for blk in (outer, inner):
            aggs[k, blk] = collect(proc, blk, k - 1)
            mesh_forward(k, blk)

    def backward(k, value, active, inside, grad):
        along, scale = centred(inside)
        gain_grads[k : k + 1, :] += jnp.sum(along * grad, axis=0, keepdims=True)
        grad = grad * gain(k)
        grad = grad - jnp.mean(grad, axis=-1, keepdims=True)
        grad = scale * (grad - along * jnp.mean(grad * along, axis=-1, keepdims=True))
        low = grad.astype(jnp.bfloat16)
        back = right_dot(low, wts[7 + k])
        sig = sigmoid(value)
        pre_low = (back * sig * (1.0 + value * (1.0 - sig))).astype(jnp.bfloat16)
        from_agg = right_dot(pre_low, wts[k]).astype(jnp.bfloat16)
        return low, pre_low, from_agg

    def send_back(graph, blk, turn, rows):
        cols = pl.ds(pl.multiple_of(2 * mesh_rows * blk, 128), mesh_rows)
        if turn > 3:
            sent(turn - 1, blk, parcel.at[blk])
        parcel[blk] = left_dot(graph[blk, :, cols], d_agg[blk, pl.ds(0, rows)]).astype(jnp.bfloat16)
        exchange(turn, blk, parcel.at[blk]).start()

    def own_back(graph, b, rows):
        total = None
        for blk in range(2):
            region = b - blk + 1
            cols = pl.ds(pl.multiple_of(region * mesh_rows, 128), mesh_rows)
            part = left_dot(graph[blk, :, cols], d_agg[blk, pl.ds(0, rows)])
            total = part if total is None else total + part
        return total

    def flat(value):
        return value.reshape(value.shape[0] * value.shape[1], value.shape[2])

    hooks.need("dec", 3, 6, 10)
    for blk in (outer, inner):
        grid_agg[blk] = collect(dec, blk, 2)

        def body(rows):
            base = grid_low[1 + blk, rows]
            value, active, inside = forward(3, grid_agg[blk, rows], base)
            out = grid_hid[blk, rows] + centred(inside)[0] * gain(3)
            low = out.astype(jnp.bfloat16)
            size = low.shape[0]
            cell = pl.ds(pl.multiple_of(blk * grid_rows + rows.start, 16), size)
            lane = lax.broadcasted_iota(jnp.int32, (size, 128), 1)
            tail = cells[cell, group : group + 128].astype(jnp.float32)
            piece = (lane >= first_gain) & (lane < first_gain + 3)
            weight = jnp.sum(jnp.where(piece, tail, 0.0), axis=1, keepdims=True)
            error = matmul(low, wts[last, :, lanes : 2 * lanes])
            error = error - cells[cell, lanes : 2 * lanes].astype(jnp.float32)
            place = lax.broadcasted_iota(jnp.int32, error.shape, 1)
            error = jnp.where(place < variables, error, 0.0)
            weighted = weight * error
            loss = jnp.sum(weighted * error, axis=0, keepdims=True)
            stats_ref[1:2, :] += sum(loss[:, n : n + 128] for n in range(0, lanes, 128))
            stats_ref[2:3, :] += jnp.sum(jnp.where(lane == 0, weight, 0.0), axis=0, keepdims=True)
            pred_low = (2.0 * weighted).astype(jnp.bfloat16)
            head_grad[...] += left_dot(low, pred_low)
            grad = right_dot(pred_low, wts[last, :, lanes : 2 * lanes])
            inner_low, pre_low, from_agg = backward(3, value, active, inside, grad)
            act[blk, rows] = active
            d_inner[blk, rows] = inner_low
            d_pre[blk, rows] = pre_low
            d_agg[blk, rows] = from_agg
            grid_hid[blk, rows] = grad + right_dot(pre_low, wts[6])

        tiles(grid_rows, body)
        send_back(dec, blk, 3, grid_rows)
    used = pl.ds(0, grid_rows)
    for b in range(2):
        hid[b] = own_back(dec, b, grid_rows)
    hooks.put(10, left_dot(flat(act[:, used]), flat(d_inner[:, used])))
    hooks.put(3, left_dot(flat(grid_agg[...]), flat(d_pre[:, used])))
    hooks.put(6, left_dot(flat(grid_low[1:3]), flat(d_pre[:, used])))

    def finish(turn, blk, total_ref, add):
        arrived(turn, blk)

        def body(rows):
            total = total_ref[blk, rows] + ext[turn % 3, 3 * blk, rows].astype(jnp.float32)
            total = total.astype(jnp.bfloat16).astype(jnp.float32)
            hid[blk, rows] = hid[blk, rows] + total if add else total

        tiles(mesh_rows, body)

    def mesh_backward(k, blk):
        def body(rows):
            value = pre[k - 1, blk, rows] if k else matmul(aggs[0, blk, rows], wts[0])
            active = (value * sigmoid(value)).astype(jnp.bfloat16)
            grad = hid[blk, rows]
            inner_low, pre_low, from_agg = backward(k, value, active, matmul(active, wts[7 + k]), grad)
            act[blk, rows] = active
            d_inner[blk, rows] = inner_low
            d_pre[blk, rows] = pre_low
            d_agg[blk, rows] = from_agg
            if k:
                hid[blk, rows] = grad + right_dot(pre_low, wts[3 + k])

        tiles(mesh_rows, body)

    turn = 3
    for k in (2, 1):
        for blk in (outer, inner):
            finish(turn, blk, hid if k == 2 else pre.at[1], k < 2)
            hooks.pause()
            mesh_backward(k, blk)
            send_back(proc, blk, turn + 1, mesh_rows)
        turn += 1
        for b in range(2):
            pre[k - 1, b] = own_back(proc, b, mesh_rows)
        hooks.pause()
        hooks.put(7 + k, left_dot(flat(act[...]), flat(d_inner[...])))
        hooks.put(k, left_dot(flat(aggs[k]), flat(d_pre[...])))
        hooks.put(3 + k, left_dot(flat(ext[k - 1, 1:3]), flat(d_pre[...])))
    for blk in (outer, inner):
        finish(turn, blk, pre.at[0], True)
        hooks.pause()
        mesh_backward(0, blk)
    hooks.pause()
    hooks.put(7, left_dot(flat(act[...]), flat(d_inner[...])))
    hooks.put(0, left_dot(flat(aggs[0]), flat(d_pre[...])))
    embed_grad = None
    for b in range(4):
        total = None
        for blk in range(2):
            region = b - blk
            if 0 <= region < 3:
                cols = slice(region * grid_rows, (region + 1) * grid_rows)
                part = left_dot(enc[blk, :, cols], d_agg[blk])
                total = part if total is None else total + part
        low = total.astype(jnp.bfloat16)
        if b in (1, 2):
            low = (grid_hid[b - 1] + low.astype(jnp.float32)).astype(jnp.bfloat16)
            rows = cells[(b - 1) * grid_rows : b * grid_rows, :lanes]
        else:
            rows = halo[b // 3]
        part = left_dot(low, rows)
        embed_grad = part if embed_grad is None else embed_grad + part
    gains[...] = jnp.zeros_like(gains)
    gains[first_gain : first_gain + 4, :] = gain_grads[0:4, :]
    across = gains[...].T
    split = group - lanes
    hooks.put(
        last,
        jnp.concatenate([embed_grad, head_grad[:, :split], head_grad[:, split:] + across], axis=1),
    )
    for blk in range(2):
        for n in range(3):
            sent(n, blk, ext.at[n, 1 + blk])
        sent(5, blk, parcel.at[blk])


class Loads:
    def __init__(self, sem, pairs):
        self.copies = {}
        for n, (name, (src, dst)) in enumerate(pairs.items()):
            self.copies[name] = pltpu.make_async_copy(src, dst, sem.at[n])
            self.copies[name].start()

    def need(self, *names):
        for name in names:
            self.copies[name].wait()


class Store:
    def __init__(self, grads_ref, low_ref, stage, stage_low, sem):
        self.refs = (grads_ref, low_ref)
        self.stages = (stage, stage_low)
        self.sem = sem
        self.copies = []

    def put(self, mat, value):
        side = len(self.copies) % 2
        if len(self.copies) >= 2:
            for copy in self.copies[-2]:
                copy.wait()
        copies = []
        for n, (ref, stage) in enumerate(zip(self.refs, self.stages)):
            stage[side] = value.astype(stage.dtype)
            copies.append(pltpu.make_async_copy(stage.at[side], ref.at[mat], self.sem.at[side, n]))
            copies[-1].start()
        self.copies.append(copies)

    def pause(self):
        pass

    def finish(self):
        for copies in self.copies[-2:]:
            for copy in copies:
                copy.wait()


class Reduce:
    def __init__(self, plan, spot, refs, sems):
        self.plan, self.spot = plan, spot
        self.acc, self.low, self.twin_in, self.plane_out, self.plane_in = refs[:5]
        self.hop_out, self.hop_in, self.own = refs[5:]
        self.twin_send, self.twin_recv, self.plane_send, self.plane_recv = sems[:4]
        self.hop_send, self.hop_recv = sems[4:]
        self.batch, self.phase = -1, 0
        self.batches = []
        self.twins, self.planes, self.hops = {}, {}, {}

    def need(self, *names):
        self.source.need(*names)

    def put(self, mat, value):
        size = self.acc.shape[0]
        if not self.batches or len(self.batches[-1]) == size:
            self.batches.append([])
            self.batch, self.phase = len(self.batches) - 1, 0
            if self.batch:
                for copy in self.twins[self.batch - 1]:
                    copy.wait_send()
            self.twins[self.batch] = []
        slot = len(self.batches[-1])
        self.batches[-1].append(mat)
        rows, width = self.acc.shape[-2:]
        halves = value.reshape(-1, 2, rows, width)
        first = self.spot.core == 0
        shape = self.acc.shape[1:]
        self.acc[slot] = jnp.where(first, halves[:, 0], halves[:, 1]).reshape(shape)
        theirs = jnp.where(first, halves[:, 1], halves[:, 0]).reshape(shape)
        self.low[slot] = theirs.astype(self.low.dtype)
        side = self.batch % 2
        copy = remote(
            self.low.at[slot],
            self.twin_in.at[side, slot],
            self.twin_send.at[slot],
            self.twin_recv.at[side, slot],
            self.spot.sibling(),
        )
        copy.start()
        self.twins[self.batch].append(copy)

    def pause(self):
        self.phase += 1
        self.advance(self.phase)

    def index(self, fixed):
        return tuple(fixed.get(b, slice(None)) for b in range(self.plan.bits - 1, -1, -1))

    def advance(self, phase):
        spot, bits = self.spot, self.plan.bits
        size = self.acc.shape[0]
        batch = self.batch
        rows, width = self.acc.shape[-2:]
        if phase == 1:
            for copy in self.twins[batch]:
                copy.wait_recv()
            side = batch % 2

            def body(n, _):
                slot, item = n // MICRO, n % MICRO
                self.acc[slot, item] += self.twin_in[side, slot, item].astype(jnp.float32)
                return 0

            lax.fori_loop(0, size * MICRO, body, 0)
        elif phase <= bits + 1:
            self.add(batch, phase - 2)
        if phase <= bits:
            self.send(batch, phase - 1)
        elif phase == bits + 1:
            if batch:
                for copy in self.hops[batch - 1]:
                    copy.wait_send()
            self.hops[batch] = []
            mine = self.index({b: spot.bit(b) for b in range(bits)})
            for slot in range(size):
                self.own[batch, slot] = self.acc[(slot, spot.z) + mine]
                for d in range(1, MICRO):
                    value = self.acc[(slot, (spot.z + d) % MICRO) + mine]
                    self.hop_out[d - 1, slot] = value.astype(self.hop_out.dtype)
            for d in range(1, MICRO):
                copy = remote(
                    self.hop_out.at[d - 1],
                    self.hop_in.at[batch, d - 1],
                    self.hop_send.at[d - 1],
                    self.hop_recv.at[batch, d - 1],
                    spot.peer_z(d),
                )
                copy.start()
                self.hops[batch].append(copy)

    def steps(self, t, d):
        bits = self.plan.bits
        count = 1 << (bits - 1 - t)
        at = sum(1 << (bits - 1 - s) for s in range(t))
        done = [(d + s) % bits for s in range(t)]
        return (d + t) % bits, done, at, count

    def send(self, batch, t):
        spot = self.spot
        size = self.acc.shape[0]
        rows, width = self.acc.shape[-2:]
        for d in range(MICRO):
            b, done, at, count = self.steps(t, d)
            if batch:
                self.planes[batch - 1, t, d].wait_send()
            item = (spot.z + d) % MICRO
            fixed = {n: spot.bit(n) for n in done}
            fixed[b] = 1 - spot.bit(b)
            theirs = self.index(fixed)

            def body(slot, _):
                value = self.acc[(slot, item) + theirs].reshape(count, rows, width)
                self.plane_out[d, slot, at : at + count] = value.astype(self.plane_out.dtype)
                return 0

            lax.fori_loop(0, size, body, 0)
            where = (d, slice(None), pl.ds(at, count))
            copy = remote(
                self.plane_out.at[where],
                self.plane_in.at[(batch,) + where],
                self.plane_send.at[t, d],
                self.plane_recv.at[batch, t, d],
                spot.peer_bit(b),
            )
            copy.start()
            self.planes[batch, t, d] = copy

    def add(self, batch, t):
        spot = self.spot
        size = self.acc.shape[0]
        for d in range(MICRO):
            b, done, at, count = self.steps(t, d)
            self.planes[batch, t, d].wait_recv()
            item = (spot.z + d) % MICRO
            mine = self.index({n: spot.bit(n) for n in done + [b]})

            def body(slot, _):
                where = (slot, item) + mine
                value = self.acc[where]
                came = self.plane_in[batch, d, slot, at : at + count].astype(jnp.float32)
                self.acc[where] = value + came.reshape(value.shape)
                return 0

            lax.fori_loop(0, size, body, 0)

    def finish(self, share_ref):
        for phase in range(self.phase + 1, self.plan.bits + 2):
            self.advance(phase)
        square = None
        for batch, mats in enumerate(self.batches):
            for copy in self.hops[batch]:
                copy.wait_recv()
            for slot, mat in enumerate(mats):
                value = self.own[batch, slot]
                for d in range(MICRO - 1):
                    value = value + self.hop_in[batch, d, slot].astype(jnp.float32)
                share_ref[mat] = value
                square = value * value if square is None else square + value * value
        last = len(self.batches) - 1
        for copy in self.twins[last] + self.hops[last]:
            copy.wait_send()
        for t in range(self.plan.bits):
            for d in range(MICRO):
                self.planes[last, t, d].wait_send()
        return square


def add_up(plan, spot, tile, refs, sems):
    send, recv = sems

    def exchange(tile, buffer, index, targets, at):
        buffer[index] = tile
        copies = []
        for n, to in enumerate(targets):
            copies.append(remote(buffer.at[index], buffer.at[index], send.at[at + n], recv.at[at + n], to))
            copies[-1].start()
        for copy in copies:
            copy.wait()
        total = buffer[0]
        for n in range(1, buffer.shape[0]):
            total = total + buffer[n]
        return total

    chips = plan.chips
    plane = [spot.in_plane((spot.p + d) % chips, spot.core) for d in range(1, chips)]
    plane += [spot.in_plane((spot.p + d) % chips, 1 - spot.core) for d in range(chips)]
    tile = exchange(tile, refs[0], 2 * spot.p + spot.core, plane, 0)
    return exchange(tile, refs[1], spot.z, [spot.peer_z(d) for d in range(1, MICRO)], 2 * chips - 1)


def fold_rows(square, lanes):
    square = jnp.sum(square, axis=0, keepdims=True)
    return sum(square[:, n : n + lanes] for n in range(0, square.shape[1], lanes))


def network_scratch(shapes):
    low, full = jnp.bfloat16, jnp.float32
    mesh_rows, grid_rows, width, lanes = shapes
    mesh_pair, grid_pair = (2, mesh_rows, width), (2, grid_rows, width)
    return [
        pltpu.VMEM((4,) + grid_pair[1:], low),
        pltpu.VMEM(grid_pair, full),
        pltpu.VMEM((3, 4) + mesh_pair[1:], low),
        pltpu.VMEM(mesh_pair, full),
        pltpu.VMEM((2,) + mesh_pair, full),
        pltpu.VMEM((3,) + mesh_pair, low),
        pltpu.VMEM(grid_pair, low),
        pltpu.VMEM((width, lanes), full),
        pltpu.VMEM(mesh_pair, low),
        pltpu.VMEM(mesh_pair, low),
        pltpu.VMEM(mesh_pair, low),
        pltpu.VMEM(mesh_pair, low),
        pltpu.VMEM(mesh_pair, low),
        pltpu.VMEM((128, width), full),
        pltpu.VMEM((8, width), full),
        pltpu.SemaphoreType.DMA((6, 2)),
        pltpu.SemaphoreType.DMA((6, 2)),
    ]


def reduce_scratch(plan, mats, rows, width):
    low, full = jnp.bfloat16, jnp.float32
    dma = pltpu.SemaphoreType.DMA
    batches, size = mats // 3, 3
    piece = (MICRO,) + (2,) * plan.bits + (rows, width)
    steps = (1 << plan.bits) - 1
    return [
        pltpu.VMEM((size,) + piece, full),
        pltpu.VMEM((size,) + piece, low),
        pltpu.VMEM((2, size) + piece, low),
        pltpu.VMEM((MICRO, size, steps, rows, width), low),
        pltpu.VMEM((batches, MICRO, size, steps, rows, width), low),
        pltpu.VMEM((MICRO - 1, size, rows, width), low),
        pltpu.VMEM((batches, MICRO - 1, size, rows, width), low),
        pltpu.VMEM((batches, size, rows, width), full),
    ], [
        dma((size,)),
        dma((2, size)),
        dma((plan.bits, MICRO)),
        dma((batches, plan.bits, MICRO)),
        dma((MICRO - 1,)),
        dma((batches, MICRO - 1)),
    ]


def load_pairs(ins, wts, cells, halo, graphs):
    pack_ref, cells_ref, halo_ref, *graph_refs = ins
    last = wts.shape[0] - 1
    pairs = {"last": (pack_ref.at[last], wts.at[last]), "halo": (halo_ref, halo), "cells": (cells_ref, cells)}

    def mats(*names):
        for n in names:
            pairs[n] = (pack_ref.at[n], wts.at[n])

    pairs["enc"] = (graph_refs[0], graphs[0])
    mats(0, 7)
    pairs["proc"] = (graph_refs[1], graphs[1])
    mats(1, 4, 8, 2, 5, 9)
    pairs["dec"] = (graph_refs[2], graphs[2])
    mats(3, 6, 10)
    return pairs


def train_kernel(plan, variables, summed, *refs):
    ins, refs = refs[:6], refs[6:]
    outs, refs = refs[:3], refs[3:]
    data, refs = refs[:6], refs[6:]
    work, refs = refs[:17], refs[17:]
    load_sem, refs = refs[0], refs[1:]
    wts, cells, halo, *graphs = data
    spot = Spot(plan)
    loads = Loads(load_sem, load_pairs(ins, wts, cells, halo, graphs))
    spot.meet()
    if not summed:
        stats_ref = outs[2]
        hooks = Store(outs[0], outs[1], *refs)
        hooks.need = loads.need
        network(plan, spot, variables, hooks, stats_ref, *data, *work)
        hooks.finish()
        return
    share_ref, total_ref, stats_ref = outs
    hooks = Reduce(plan, spot, refs[:8], refs[8:14])
    hooks.source = loads
    network(plan, spot, variables, hooks, stats_ref, *data, *work)
    square = fold_rows(hooks.finish(share_ref), stats_ref.shape[1])
    row = lax.broadcasted_iota(jnp.int32, stats_ref.shape, 0)
    tile = jnp.where(row == 0, square, stats_ref[...])
    total_ref[...] = add_up(plan, spot, tile, refs[14:16], refs[16:18])


def train(plan, variables, summed, rows, pack, cells, halo, encoder, processor, decoder):
    mats, width = pack.shape[0], pack.shape[2]
    lanes = halo.shape[-1]
    any_space = pl.BlockSpec(memory_space=pl.ANY)
    vmem = pl.BlockSpec(memory_space=pltpu.VMEM)
    dma = pltpu.SemaphoreType.DMA
    low, full = jnp.bfloat16, jnp.float32
    stats = jax.ShapeDtypeStruct((8, 128), full)
    chips = plan.chips
    if summed:
        out_shape = (jax.ShapeDtypeStruct((mats, rows, width), full), stats, stats)
        out_specs = (vmem, vmem, vmem)
        buffers, sems = reduce_scratch(plan, mats, rows, width)
        more = (
            buffers
            + sems
            + [pltpu.VMEM((n,) + stats.shape, full) for n in (2 * chips, MICRO)]
            + [dma((MICRO + 2 * chips - 2,))] * 2
        )
    else:
        out_shape = (jax.ShapeDtypeStruct(pack.shape, full), jax.ShapeDtypeStruct(pack.shape, low), stats)
        out_specs = (any_space, any_space, vmem)
        more = [pltpu.VMEM((2, width, width), full), pltpu.VMEM((2, width, width), low), dma((2, 2))]
    ins = (pack, cells, halo, encoder, processor, decoder)
    shapes = (encoder.shape[1], decoder.shape[1], width, lanes)
    return pl.pallas_call(
        functools.partial(train_kernel, plan, variables, summed),
        out_shape=out_shape,
        in_specs=[any_space] * 6,
        out_specs=out_specs,
        scratch_shapes=[pltpu.VMEM(value.shape, low) for value in ins]
        + network_scratch(shapes)
        + [dma((mats + 5,))]
        + more,
        compiler_params=pltpu.CompilerParams(
            collective_id=2, has_side_effects=True, vmem_limit_bytes=63 << 20
        ),
        name="train",
    )(*ins)


def adamw(param, first, second, grad, scale, rate):
    clipped = grad * scale
    moment = BETA_ONE * first + (1.0 - BETA_ONE) * clipped
    square = BETA_TWO * second + (1.0 - BETA_TWO) * clipped * clipped
    fixed_one = moment / (1.0 - BETA_ONE**STEP)
    fixed_two = square / (1.0 - BETA_TWO**STEP)
    fresh = param - rate * (fixed_one / (jnp.sqrt(fixed_two) + EPS_ADAM) + DECAY * param)
    return (fresh, moment, square, fresh.astype(jnp.bfloat16))


def on_device(
    plan,
    grid_in,
    targets,
    area_weight,
    grid_count,
    g2m_edges,
    mesh_edges,
    m2g_edges,
    edge_count,
    embed_weight,
    embed_first,
    embed_second,
    node_mats,
    mats_first,
    mats_second,
    head_weight,
    head_first,
    head_second,
    norm_gains,
    gains_first,
    gains_second,
):
    half, variables = grid_in.shape[1:]
    grid_rows = 2 * half
    mesh_rows = M_DEV
    lanes = -(-variables // 128) * 128
    core = lax.axis_index("feat")

    position = core * half + jnp.arange(half, dtype=jnp.int32)
    weights = jnp.where(position[None, :] < grid_count, area_weight, 0.0)
    pieces = []
    rest = weights
    for _ in range(3):
        piece = lax.reduce_precision(rest, 8, 7)
        pieces.append(piece.astype(jnp.bfloat16))
        rest = rest - piece
    cells = jnp.concatenate(
        [
            jnp.pad(grid_in, ((0, 0), (0, 0), (0, lanes - variables))),
            targets,
            jnp.pad(jnp.stack(pieces, axis=-1), ((0, 0), (0, 0), (0, lanes - variables - 3))),
        ],
        axis=-1,
    )
    last = jnp.concatenate(
        [
            jnp.pad(embed_weight.T, ((0, 0), (0, lanes - variables))),
            head_weight,
            jnp.pad(norm_gains.T, ((0, 0), (0, lanes - variables - 4))),
        ],
        axis=-1,
    )
    pack = jnp.concatenate([node_mats, last[None]]).astype(jnp.bfloat16)
    graphs = ((g2m_edges, grid_rows, mesh_rows), (mesh_edges, mesh_rows, mesh_rows), (m2g_edges, mesh_rows, grid_rows))
    codes, shapes = [], []
    first = 0
    for n, (edges, columns, rows) in enumerate(graphs):
        per = edges.shape[1]
        alive = jnp.arange(per, dtype=jnp.int32) < edge_count[n, 0]
        codes.append(jnp.where(alive, edges[1] * (1 << CODE_BITS) + edges[0], -1))
        shapes.append((first // 128, per, rows, 3 * columns))
        first += per
    codes = jnp.concatenate(codes).reshape(-1, 128)
    gathered, main, halo, encoder, processor, decoder = gather_all(plan, shapes, pack, cells, codes)
    width = pack.shape[2]
    full = gathered.reshape(-1, width, width)
    main = main.reshape(-1, 2 * lanes)
    halo = halo.reshape(2, grid_rows, lanes)
    rows = pack.shape[1]
    summed = rows % 16 == 0
    trained = train(plan, variables, summed, rows, full, main, halo, encoder, processor, decoder)
    if summed:
        share, total = trained[:2]
    else:
        grads, low, stats = trained
        share, total = reduce_all(plan, grads.reshape(gathered.shape), low.reshape(gathered.shape), stats)
    square_sum, loss_sum, weight_sum = (jnp.sum(total[n]) for n in range(3))
    shares = (
        share[-1, :, :variables].T,
        share[:-1],
        share[-1, :, lanes : lanes + variables],
        share[-1, :, lanes + variables : lanes + variables + 4].T,
    )
    grad_norm = jnp.sqrt(square_sum)
    scale = jnp.minimum(1.0, CLIP / (grad_norm + 1e-06))
    return (
        loss_sum,
        weight_sum,
        grad_norm,
        *adamw(embed_weight, embed_first, embed_second, shares[0], scale, RATE),
        *adamw(node_mats, mats_first, mats_second, shares[1], scale, RATE),
        *adamw(head_weight, head_first, head_second, shares[2], scale, RATE),
        *adamw(norm_gains, gains_first, gains_second, shares[3], scale, GAIN_RATE),
    )


def solution(mesh):
    plan = Plan(mesh.shape["nodes"])
    cells = P(None, BOTH, None)
    columns = P(None, BOTH)
    rows = P(BOTH, None)
    blocks = P(None, "nodes")
    return jax.shard_map(
        lambda *args: on_device(plan, *args),
        mesh=mesh,
        in_specs=(
            (cells, cells, columns, blocks, blocks, blocks, blocks, blocks)
            + (columns,) * 3
            + (cells,) * 3
            + (rows,) * 3
            + (columns,) * 3
        ),
        out_specs=(P(), P(), P()) + (columns,) * 4 + (cells,) * 4 + (rows,) * 4 + (columns,) * 4,
        check_vma=False,
    )
```

```python
import functools
import math

import jax
import jax.numpy as jnp
from jax import lax
from jax.experimental import pallas as pl
from jax.experimental.pallas import tpu as pltpu
from jax.sharding import PartitionSpec as P

M_DEV = 640
STEP = 5
MICRO = 4


EPS_NORM = 1e-05
CLIP = 0.5
RATE = 0.04
GAIN_RATE = 0.4
BETA_ONE = 0.5
BETA_TWO = 0.6
EPS_ADAM = 1e-08
DECAY = 0.1

BOTH = ("nodes", "feat")


def matmul(a, b):
    return jnp.dot(a, b, preferred_element_type=jnp.float32)


def left_dot(a, b):
    return lax.dot_general(a, b, (((0,), (0,)), ((), ())), preferred_element_type=jnp.float32)


def right_dot(a, b):
    return lax.dot_general(a, b, (((1,), (1,)), ((), ())), preferred_element_type=jnp.float32)


class Plan:
    def __init__(self, nodes):
        self.nodes = nodes
        self.chips = nodes // MICRO
        self.bits = self.chips.bit_length() - 1
        width = math.isqrt(self.chips)
        self.width = width if width * width == self.chips else 0


MESH = pl.DeviceIdType.MESH
CODE_BITS = 12
SLOTS = {mat: slot for slot, mat in enumerate((11, 0, 7, 1, 4, 8, 2, 5, 9, 3, 6, 10))}


def walk(value, width):
    if width == 0:
        return value
    row, col = value // width, value % width
    return row * width + col + (row % 2) * (width - 1 - 2 * col)


class Spot:
    def __init__(self, plan):
        me = lax.axis_index("nodes")
        self.plan = plan
        self.core = lax.axis_index("feat")
        self.z = me // plan.chips
        self.p = me % plan.chips

    def bit(self, b):
        return (self.p // (1 << b)) % 2

    def peer_z(self, d):
        return {"nodes": ((self.z + d) % MICRO) * self.plan.chips + self.p, "feat": self.core}

    def peer_bit(self, b):
        other = self.p + (1 - 2 * self.bit(b)) * (1 << b)
        return {"nodes": self.z * self.plan.chips + other, "feat": self.core}

    def in_plane(self, p, core):
        return {"nodes": self.z * self.plan.chips + p, "feat": core}

    def sibling(self):
        return self.in_plane(self.p, 1 - self.core)

    def partners(self):
        chips = self.plan.chips
        found = [self.peer_z(d) for d in range(1, MICRO)]
        for turn in range(chips):
            p = (self.p + turn) % chips
            if turn:
                found.append(self.in_plane(p, self.core))
            found.append(self.in_plane(p, 1 - self.core))
        return found

    def meet(self):
        barrier = pltpu.get_barrier_semaphore()
        found = self.partners()
        for other in found:
            pl.semaphore_signal(barrier, inc=1, device_id=other, device_id_type=MESH)
        pl.semaphore_wait(barrier, len(found))

    def held(self, done):
        bits = range(self.plan.bits - 1, -1, -1)
        return tuple(slice(None) if b in done else self.bit(b) for b in bits)


def remote(src, dst, send, recv, to):
    return pltpu.make_async_remote_copy(
        src_ref=src, dst_ref=dst, send_sem=send, recv_sem=recv, device_id=to, device_id_type=MESH
    )


def gather_kernel(
    plan,
    shapes,
    pack_ref,
    cells_ref,
    codes_ref,
    all_ref,
    main_ref,
    halo_ref,
    enc_ref,
    proc_ref,
    dec_ref,
    graph_ref,
    total,
    whole,
    cell_hop,
    code_hop,
    own_sem,
    out_sem,
    hop_send,
    hop_recv,
    plane_send,
    plane_recv,
    twin_send,
    twin_recv,
    move_send,
    move_recv,
):
    spot = Spot(plan)
    z, p, core = spot.z, spot.p, spot.core
    chips, bits = plan.chips, plan.bits
    groups = bits
    mats = pack_ref.shape[0] // groups
    code_rows = codes_ref.shape[0] // 2
    lanes = halo_ref.shape[-1]
    own = pltpu.make_async_copy(pack_ref, all_ref.at[(slice(None), z) + spot.held(()) + (core,)], own_sem)
    own.start()
    spot.meet()
    my_codes = codes_ref.at[pl.ds(pl.multiple_of(core * code_rows, 8), code_rows)]
    hops = []
    for d in range(1, MICRO):
        to = spot.peer_z(d)
        m = (z + d) % MICRO
        for n, (src, dst) in enumerate(
            (
                (my_codes, code_hop.at[d - 1]),
                (cells_ref.at[m], cell_hop.at[d - 1]),
                (pack_ref, all_ref.at[(slice(None), z) + spot.held(()) + (core,)]),
            )
        ):
            copy = remote(src, dst, hop_send.at[d - 1, n], hop_recv.at[d - 1, n], to)
            copy.start()
            hops.append(copy)
    quarter = p % 4
    bb, to_core = quarter % 2, quarter // 2
    slot = bb * 2 + core
    half_slot = (1 - bb) * 2 + core
    moves = []

    def move(d, n, src, dst, sem, chip, to_core):
        here = jnp.logical_and(chip == p, to_core == core)
        copy = remote(src, dst, move_send.at[d, n], sem, spot.in_plane(chip, to_core))

        @pl.when(here)
        def _():
            pltpu.make_async_copy(src, dst, sem).start()

        @pl.when(jnp.logical_not(here))
        def _():
            copy.start()

        moves.append((here, copy))

    def spread_codes(d):
        block = ((z - d) % MICRO) * chips + p
        codes = my_codes if d == 0 else code_hop.at[d - 1]
        rows = pl.ds(pl.multiple_of(core * code_rows, 8), code_rows)
        dst = graph_ref.at[bb, rows]
        move(d, 0, codes, dst, move_recv.at[0, slot], walk(block // 4, plan.width), to_core)

    def spread(d):
        block = ((z - d) % MICRO) * chips + p
        j = block // 4
        chip = walk(j, plan.width)
        q = (2 * j + to_core + 2 * bb - 1) % (2 * chips)
        near = walk(q // 2, plan.width)
        cells = cells_ref.at[z] if d == 0 else cell_hop.at[d - 1]
        move(
            d,
            1,
            cells.at[:, pl.ds(0, lanes)],
            halo_ref.at[1 - bb, core],
            move_recv.at[1, half_slot],
            near,
            q % 2,
        )
        move(d, 2, cells, main_ref.at[bb, core], move_recv.at[2, slot], chip, to_core)

    def region(d, done):
        return ((z - d) % MICRO,) + spot.held(done) + (core,)

    planes = {}

    def step(d, g, t):
        done = tuple((g + s) % bits for s in range(t))
        where = (pl.ds(g * mats, mats),) + region(d, done)
        copy = remote(
            all_ref.at[where],
            all_ref.at[where],
            plane_send.at[d, g, t],
            plane_recv.at[d, g, t],
            spot.peer_bit((g + t) % bits),
        )
        copy.start()
        planes[d, g, t] = copy

    for d in range(MICRO):
        if d:
            hops[3 * (d - 1)].wait_recv()
        spread_codes(d)
    outs = []

    def build(n, side_block):
        first, edges, rows, columns = shapes[n]
        chunk = math.gcd(edges, 1024) // 128
        area = (pl.ds(0, rows), pl.ds(0, columns))

        def ones(row, count):
            place = lax.broadcasted_iota(jnp.int32, (count, 128), 0).astype(jnp.int16)
            hit = place == row.astype(jnp.int16)
            return jnp.where(hit, jnp.bfloat16(1), jnp.bfloat16(0)).astype(jnp.float8_e4m3fn)

        def body(k, _):
            into, out = [], []
            for i in range(chunk):
                code = graph_ref[side_block, pl.ds(first + k * chunk + i, 1), :]
                into.append(ones(code >> CODE_BITS, rows))
                out.append(ones(code & ((1 << CODE_BITS) - 1), columns))
            total[area] += right_dot(jnp.concatenate(into, axis=1), jnp.concatenate(out, axis=1))
            return 0

        total[area] = jnp.zeros((rows, columns), jnp.float32)
        lax.fori_loop(0, edges // (128 * chunk), body, 0)
        if len(outs) >= 2:
            outs[-2].wait()
        side = len(outs) % 2
        whole[(side,) + area] = total[area].astype(jnp.bfloat16)
        ref = (enc_ref, proc_ref, dec_ref)[n]
        copy = pltpu.make_async_copy(whole.at[(side,) + area], ref.at[side_block], out_sem.at[side])
        copy.start()
        outs.append(copy)

    work = [[], [(0, 0), (0, 1)], [(1, 0)], [(1, 1)], [(2, 0)], [(2, 1)]]
    twins = []
    for tick in range(MICRO + bits):
        for t in range(bits + 1):
            d = tick - t
            if d < 0 or d >= MICRO:
                continue
            if t == 0:
                if d == 0:
                    own.wait()
                else:
                    hops[3 * (d - 1) + 1].wait_recv()
                    hops[3 * (d - 1) + 2].wait_recv()
                spread(d)
            else:
                for g in range(groups):
                    planes[d, g, t - 1].wait_recv()
            if t < bits:
                for g in range(groups):
                    step(d, g, t)
            else:
                where = (slice(None),) + region(d, tuple(range(bits)))
                copy = remote(
                    all_ref.at[where], all_ref.at[where], twin_send.at[d], twin_recv.at[d], spot.sibling()
                )
                copy.start()
                twins.append(copy)
        if tick == 1:
            for n in range(4):
                dst = graph_ref.at[n // 2, pl.ds((n % 2) * code_rows, code_rows)]
                pltpu.make_async_copy(dst, dst, move_recv.at[0, n]).wait()
        for kind, block in work[tick] if tick < len(work) else []:
            build(kind, block)
    for copy in outs[-2:]:
        copy.wait()
    for copy in hops + list(planes.values()):
        copy.wait_send()
    for copy in twins:
        copy.wait()
    for here, copy in moves:

        @pl.when(jnp.logical_not(here))
        def _():
            copy.wait_send()

    for n in range(4):
        half, side = n % 2, n // 2
        for kind, dst in ((1, halo_ref.at[side, half]), (2, main_ref.at[side, half])):
            pltpu.make_async_copy(dst, dst, move_recv.at[kind, n]).wait()


def gather_all(plan, shapes, pack, cells, codes):
    mats, rows, width = pack.shape
    micro, half, lanes = cells.shape
    bits = plan.bits
    most_rows = max(shape[2] for shape in shapes)
    most_columns = max(shape[3] for shape in shapes)
    any_space = pl.BlockSpec(memory_space=pl.ANY)
    dma = pltpu.SemaphoreType.DMA
    return pl.pallas_call(
        functools.partial(gather_kernel, plan, shapes),
        out_shape=(
            jax.ShapeDtypeStruct((mats, MICRO) + (2,) * bits + (2, rows, width), pack.dtype),
            jax.ShapeDtypeStruct((2, 2, half, lanes), cells.dtype),
            jax.ShapeDtypeStruct((2, 2, half, lanes // 2), cells.dtype),
            *(jax.ShapeDtypeStruct((2,) + shape[2:], jnp.bfloat16) for shape in shapes),
        ),
        in_specs=[any_space] * 3,
        out_specs=(any_space,) * 6,
        scratch_shapes=[
            pltpu.VMEM((2,) + codes.shape, codes.dtype),
            pltpu.VMEM((most_rows, most_columns), jnp.float32),
            pltpu.VMEM((2, most_rows, most_columns), jnp.bfloat16),
            pltpu.VMEM((MICRO - 1, half, lanes), cells.dtype),
            pltpu.VMEM((MICRO - 1, codes.shape[0] // 2, codes.shape[1]), codes.dtype),
            dma,
            dma((2,)),
            dma((MICRO - 1, 3)),
            dma((MICRO - 1, 3)),
            dma((MICRO, bits, bits)),
            dma((MICRO, bits, bits)),
            dma((MICRO,)),
            dma((MICRO,)),
            dma((MICRO, 3)),
            dma((3, 4)),
        ],
        compiler_params=pltpu.CompilerParams(
            collective_id=0, has_side_effects=True, vmem_limit_bytes=48 << 20
        ),
        name="gather_all",
    )(pack, cells, codes)


def reduce_kernel(
    plan,
    grads_ref,
    low_ref,
    stats_ref,
    share_ref,
    total_ref,
    acc,
    twin_in,
    plane_out,
    plane_in,
    hop_out,
    hop_in,
    z_stats,
    plane_stats,
    twin_stats,
    own_sem,
    twin_send,
    twin_recv,
    plane_send,
    plane_recv,
    hop_send,
    hop_recv,
    stat_send,
    stat_recv,
):
    spot = Spot(plan)
    z, p, core = spot.z, spot.p, spot.core
    chips, bits = plan.chips, plan.bits
    groups = bits
    mats = grads_ref.shape[0]
    part = mats // groups
    every = (slice(None),) * bits
    order = [1, 2, 3, 0]
    owns = {}
    for d in order:
        item = (z + d) % MICRO
        owns[d] = pltpu.make_async_copy(
            grads_ref.at[(slice(None), item) + every + (core,)], acc.at[d], own_sem.at[d]
        )
        owns[d].start()
    spot.meet()
    twins = {}
    for d in order:
        item = (z + d) % MICRO
        twins[d] = remote(
            low_ref.at[(slice(None), item) + every + (1 - core,)],
            twin_in.at[d],
            twin_send.at[d],
            twin_recv.at[d],
            spot.sibling(),
        )
        twins[d].start()

    def starts(t):
        return sum(1 << (bits - 1 - s) for s in range(t))

    planes, hops = {}, []

    def send_step(d, g, t):
        done = tuple((g + s) % bits for s in range(t))
        b = (g + t) % bits
        count = 1 << (bits - 1 - t)
        at = starts(t)
        theirs = tuple(
            spot.bit(n) if n in done else (1 - spot.bit(n) if n == b else slice(None))
            for n in range(bits - 1, -1, -1)
        )

        def body(n, _):
            mat = g * part + n
            value = acc[(d, mat) + theirs]
            plane_out[d, mat, at : at + count] = value.reshape((count,) + value.shape[-2:]).astype(
                plane_out.dtype
            )
            return 0

        lax.fori_loop(0, part, body, 0)
        where = (d, pl.ds(g * part, part), pl.ds(at, count))
        planes[d, g, t] = remote(
            plane_out.at[where],
            plane_in.at[where],
            plane_send.at[d, g, t],
            plane_recv.at[d, g, t],
            spot.peer_bit(b),
        )
        planes[d, g, t].start()

    def add_step(d, g, t):
        planes[d, g, t].wait_recv()
        done = tuple((g + s) % bits for s in range(t + 1))
        count = 1 << (bits - 1 - t)
        at = starts(t)
        mine = tuple(spot.bit(n) if n in done else slice(None) for n in range(bits - 1, -1, -1))

        def body(n, _):
            mat = g * part + n
            where = (d, mat) + mine
            value = acc[where]
            came = plane_in[d, mat, at : at + count].astype(jnp.float32)
            acc[where] = value + came.reshape(value.shape)
            return 0

        lax.fori_loop(0, part, body, 0)

    for tick in range(MICRO + bits):
        for t in range(bits + 1):
            n = tick - t
            if n < 0 or n >= MICRO:
                continue
            d = order[n]
            if t == 0:
                owns[d].wait()
                twins[d].wait_recv()

                def body(mat, _):
                    acc[d, mat] = acc[d, mat] + twin_in[d, mat].astype(jnp.float32)
                    return 0

                lax.fori_loop(0, mats, body, 0)
            else:
                for g in range(groups):
                    add_step(d, g, t - 1)
            if t < bits:
                for g in range(groups):
                    send_step(d, g, t)
            elif d:

                def body(mat, _):
                    hop_out[d - 1, mat] = acc[(d, mat) + spot.held(())].astype(hop_out.dtype)
                    return 0

                lax.fori_loop(0, mats, body, 0)
                copy = remote(
                    hop_out.at[d - 1], hop_in.at[d - 1], hop_send.at[d - 1], hop_recv.at[d - 1], spot.peer_z(d)
                )
                copy.start()
                hops.append(copy)
    for copy in hops:
        copy.wait_recv()

    def body(mat, square):
        value = acc[(0, mat) + spot.held(())]
        for d in range(MICRO - 1):
            value = value + hop_in[d, mat].astype(jnp.float32)
        share_ref[mat] = value
        return square + value * value

    square = lax.fori_loop(0, mats, body, jnp.zeros(share_ref.shape[1:], jnp.float32))
    square = jnp.sum(square, axis=0, keepdims=True)
    lanes = total_ref.shape[1]
    square = sum(square[:, n : n + lanes] for n in range(0, square.shape[1], lanes))
    row = lax.broadcasted_iota(jnp.int32, total_ref.shape, 0)
    tile = jnp.where(row == 0, square, stats_ref[...])
    sends = []

    def exchange(buffer, index, targets, at):
        buffer[index] = tile
        copies = []
        for n, to in enumerate(targets):
            copy = remote(
                buffer.at[index], buffer.at[index], stat_send.at[at + n], stat_recv.at[at + n], to
            )
            copy.start()
            copies.append(copy)
        for copy in copies:
            copy.wait()
        total = buffer[0]
        for n in range(1, buffer.shape[0]):
            total = total + buffer[n]
        return total

    tile = exchange(z_stats, z, [spot.peer_z(d) for d in range(1, MICRO)], 0)
    tile = exchange(
        plane_stats, p, [spot.in_plane((p + d) % chips, core) for d in range(1, chips)], MICRO - 1
    )
    tile = exchange(twin_stats, core, [spot.sibling()], MICRO + chips - 2)
    total_ref[...] = tile
    for copy in list(twins.values()) + list(planes.values()) + hops:
        copy.wait_send()


def reduce_all(plan, grads, low, stats):
    mats, rows, width = grads.shape[0], grads.shape[-2], grads.shape[-1]
    bits, chips = plan.bits, plan.chips
    shards = (2,) * bits
    steps = chips - 1
    any_space = pl.BlockSpec(memory_space=pl.ANY)
    vmem = pl.BlockSpec(memory_space=pltpu.VMEM)
    dma = pltpu.SemaphoreType.DMA
    return pl.pallas_call(
        functools.partial(reduce_kernel, plan),
        out_shape=(
            jax.ShapeDtypeStruct((mats, rows, width), jnp.float32),
            jax.ShapeDtypeStruct(stats.shape, jnp.float32),
        ),
        in_specs=[any_space, any_space, vmem],
        out_specs=(vmem, vmem),
        scratch_shapes=[
            pltpu.VMEM((MICRO, mats) + shards + (rows, width), jnp.float32),
            pltpu.VMEM((MICRO, mats) + shards + (rows, width), low.dtype),
            pltpu.VMEM((MICRO, mats, steps, rows, width), jnp.bfloat16),
            pltpu.VMEM((MICRO, mats, steps, rows, width), jnp.bfloat16),
            pltpu.VMEM((MICRO - 1, mats, rows, width), jnp.bfloat16),
            pltpu.VMEM((MICRO - 1, mats, rows, width), jnp.bfloat16),
            pltpu.VMEM((MICRO,) + stats.shape, jnp.float32),
            pltpu.VMEM((chips,) + stats.shape, jnp.float32),
            pltpu.VMEM((2,) + stats.shape, jnp.float32),
            dma((MICRO,)),
            dma((MICRO,)),
            dma((MICRO,)),
            dma((MICRO, bits, bits)),
            dma((MICRO, bits, bits)),
            dma((MICRO - 1,)),
            dma((MICRO - 1,)),
            dma((MICRO + chips - 1,)),
            dma((MICRO + chips - 1,)),
        ],
        compiler_params=pltpu.CompilerParams(
            collective_id=1, has_side_effects=True, vmem_limit_bytes=56 << 20
        ),
        name="reduce_all",
    )(grads, low, stats)


class Matrices:
    def __init__(self, ref):
        self.ref = ref
        self.width = ref.shape[-1]
        self.shape = (ref.shape[0], self.width, self.width)

    def __getitem__(self, index):
        index = index if isinstance(index, tuple) else (index,)
        where = (SLOTS[index[0]],) + (slice(None),) * (len(self.ref.shape) - 2) + index[2:3]
        value = self.ref[where]
        return value.reshape(self.width, value.shape[-1])


def sigmoid(value):
    return 1.0 / (1.0 + jnp.exp(-value))


def centred(z):
    mean = jnp.mean(z, axis=-1, keepdims=True)
    away = z - mean
    spread = jnp.mean(away * away, axis=-1, keepdims=True)
    scale = lax.rsqrt(spread + EPS_NORM)
    return away * scale, scale


def network(
    plan,
    spot,
    variables,
    hooks,
    stats_ref,
    wts,
    cells,
    halo,
    enc,
    proc,
    dec,
    grid_low,
    grid_hid,
    ext,
    hid,
    pre,
    aggs,
    grid_agg,
    head_grad,
    act,
    d_inner,
    d_pre,
    d_agg,
    parcel,
    gains,
    gain_grads,
    ex_send,
    ex_recv,
):
    core = spot.core
    outer, inner = core, 1 - core
    lanes = halo.shape[-1]
    last = wts.shape[0] - 1
    mesh_rows, width = hid.shape[1:]
    grid_rows = grid_hid.shape[1]
    ring = 2 * walk(spot.p, plan.width) + core

    def near(blk):
        q = (ring + 2 * blk - 1 + 2 * plan.chips) % (2 * plan.chips)
        return spot.in_plane(walk(q // 2, plan.width), q % 2)

    def exchange(turn, blk, src):
        dst = ext.at[turn % 3, 3 * (1 - blk)]
        return remote(src, dst, ex_send.at[turn, blk], ex_recv.at[turn, blk], near(blk))

    def arrived(turn, blk):
        dst = ext.at[turn % 3, 3 * blk]
        pltpu.make_async_copy(dst, dst, ex_recv.at[turn, 1 - blk]).wait()

    def sent(turn, blk, src):
        pltpu.make_async_copy(src, src, ex_send.at[turn, blk]).wait()

    def tiles(rows, body):
        size = rows // 4

        def one(n, _):
            body(pl.ds(pl.multiple_of(n * size, 16), size))
            return 0

        lax.fori_loop(0, rows // size, one, 0)

    hooks.need("last", "halo", "cells")
    group = (lanes + variables) // 128 * 128
    first_gain = lanes + variables - group
    gains[...] = wts[last, :, group : group + 128].astype(jnp.float32).T

    def gain(k):
        return gains[first_gain + k : first_gain + k + 1, :]

    gain_grads[...] = jnp.zeros_like(gain_grads)
    head_grad[...] = jnp.zeros_like(head_grad)
    stats_ref[...] = jnp.zeros_like(stats_ref)

    for b in range(4):
        if b in (0, 3):
            rows = halo[b // 3]
        else:
            rows = cells[(b - 1) * grid_rows : b * grid_rows, :lanes]
        hidden = right_dot(rows, wts[last, :, :lanes])
        if b in (1, 2):
            grid_hid[b - 1] = hidden
        grid_low[b] = hidden.astype(jnp.bfloat16)

    def forward(k, low_agg, base):
        value = matmul(low_agg, wts[k])
        if base is not None:
            value = value + matmul(base, wts[3 + k])
        active = (value * sigmoid(value)).astype(jnp.bfloat16)
        return value, active, matmul(active, wts[7 + k])

    def mesh_forward(k, blk):
        def body(rows):
            base = None if k == 0 else ext[k - 1, 1 + blk, rows]
            value, _, inside = forward(k, aggs[k, blk, rows], base)
            if k:
                pre[k - 1, blk, rows] = value
            result = centred(inside)[0] * gain(k)
            if k:
                result = hid[blk, rows] + result
            hid[blk, rows] = result
            ext[k, 1 + blk, rows] = result.astype(jnp.bfloat16)

        tiles(mesh_rows, body)
        exchange(k, blk, ext.at[k, 1 + blk]).start()
        hooks.pump(2)

    def collect(graph, blk, turn):
        size = mesh_rows
        own = pl.ds(pl.multiple_of(size * (1 - blk), 128), 2 * size)
        rest = pl.ds(pl.multiple_of(2 * size * blk, 128), size)
        total = matmul(graph[blk, :, own], ext[turn, 1:3].reshape(2 * size, width))
        arrived(turn, blk)
        total = total + matmul(graph[blk, :, rest], ext[turn, 3 * blk])
        return total.astype(jnp.bfloat16)

    hooks.need("enc")
    for blk in (outer, inner):
        senders = grid_low[pl.ds(blk, 3)].reshape(3 * grid_rows, width)
        aggs[0, blk] = matmul(enc[blk], senders).astype(jnp.bfloat16)
        if blk is outer:
            hooks.need(0, 7)
        mesh_forward(0, blk)
    hooks.need("proc")
    for k in (1, 2):
        hooks.between(k)
        hooks.need(k, 3 + k, 7 + k)
        for blk in (outer, inner):
            aggs[k, blk] = collect(proc, blk, k - 1)
            mesh_forward(k, blk)

    def backward(k, value, active, inside, grad):
        along, scale = centred(inside)
        gain_grads[k : k + 1, :] += jnp.sum(along * grad, axis=0, keepdims=True)
        grad = grad * gain(k)
        grad = grad - jnp.mean(grad, axis=-1, keepdims=True)
        grad = scale * (grad - along * jnp.mean(grad * along, axis=-1, keepdims=True))
        low = grad.astype(jnp.bfloat16)
        back = right_dot(low, wts[7 + k])
        sig = sigmoid(value)
        pre_low = (back * sig * (1.0 + value * (1.0 - sig))).astype(jnp.bfloat16)
        from_agg = right_dot(pre_low, wts[k]).astype(jnp.bfloat16)
        return low, pre_low, from_agg

    def send_back(graph, blk, turn, rows):
        cols = pl.ds(pl.multiple_of(2 * mesh_rows * blk, 128), mesh_rows)
        if turn > 3:
            sent(turn - 1, blk, parcel.at[blk])
        parcel[blk] = left_dot(graph[blk, :, cols], d_agg[blk, pl.ds(0, rows)]).astype(jnp.bfloat16)
        exchange(turn, blk, parcel.at[blk]).start()

    def own_back(graph, b, rows):
        total = None
        for blk in range(2):
            region = b - blk + 1
            cols = pl.ds(pl.multiple_of(region * mesh_rows, 128), mesh_rows)
            part = left_dot(graph[blk, :, cols], d_agg[blk, pl.ds(0, rows)])
            total = part if total is None else total + part
        return total

    def flat(value):
        return value.reshape(value.shape[0] * value.shape[1], value.shape[2])

    hooks.between(3)
    hooks.need("targets", "dec", 3, 6, 10)
    for blk in (outer, inner):
        grid_agg[blk] = collect(dec, blk, 2)

        def body(rows):
            base = grid_low[1 + blk, rows]
            value, active, inside = forward(3, grid_agg[blk, rows], base)
            out = grid_hid[blk, rows] + centred(inside)[0] * gain(3)
            low = out.astype(jnp.bfloat16)
            size = low.shape[0]
            cell = pl.ds(pl.multiple_of(blk * grid_rows + rows.start, 16), size)
            lane = lax.broadcasted_iota(jnp.int32, (size, 128), 1)
            tail = cells[cell, group : group + 128].astype(jnp.float32)
            piece = (lane >= first_gain) & (lane < first_gain + 3)
            weight = jnp.sum(jnp.where(piece, tail, 0.0), axis=1, keepdims=True)
            error = matmul(low, wts[last, :, lanes : 2 * lanes])
            error = error - cells[cell, lanes : 2 * lanes].astype(jnp.float32)
            place = lax.broadcasted_iota(jnp.int32, error.shape, 1)
            error = jnp.where(place < variables, error, 0.0)
            weighted = weight * error
            loss = jnp.sum(weighted * error, axis=0, keepdims=True)
            stats_ref[1:2, :] += sum(loss[:, n : n + 128] for n in range(0, lanes, 128))
            stats_ref[2:3, :] += jnp.sum(jnp.where(lane == 0, weight, 0.0), axis=0, keepdims=True)
            pred_low = (2.0 * weighted).astype(jnp.bfloat16)
            head_grad[...] += left_dot(low, pred_low)
            grad = right_dot(pred_low, wts[last, :, lanes : 2 * lanes])
            inner_low, pre_low, from_agg = backward(3, value, active, inside, grad)
            act[blk, rows] = active
            d_inner[blk, rows] = inner_low
            d_pre[blk, rows] = pre_low
            d_agg[blk, rows] = from_agg
            grid_hid[blk, rows] = grad + right_dot(pre_low, wts[6])

        tiles(grid_rows, body)
        send_back(dec, blk, 3, grid_rows)
    used = pl.ds(0, grid_rows)
    for b in range(2):
        hid[b] = own_back(dec, b, grid_rows)
    hooks.put(10, left_dot(flat(act[:, used]), flat(d_inner[:, used])))
    hooks.put(3, left_dot(flat(grid_agg[...]), flat(d_pre[:, used])))
    hooks.put(6, left_dot(flat(grid_low[1:3]), flat(d_pre[:, used])))

    def finish(turn, blk, total_ref, add):
        arrived(turn, blk)

        def body(rows):
            total = total_ref[blk, rows] + ext[turn % 3, 3 * blk, rows].astype(jnp.float32)
            total = total.astype(jnp.bfloat16).astype(jnp.float32)
            hid[blk, rows] = hid[blk, rows] + total if add else total

        tiles(mesh_rows, body)

    def mesh_backward(k, blk):
        def body(rows):
            value = pre[k - 1, blk, rows] if k else matmul(aggs[0, blk, rows], wts[0])
            active = (value * sigmoid(value)).astype(jnp.bfloat16)
            grad = hid[blk, rows]
            inner_low, pre_low, from_agg = backward(k, value, active, matmul(active, wts[7 + k]), grad)
            act[blk, rows] = active
            d_inner[blk, rows] = inner_low
            d_pre[blk, rows] = pre_low
            d_agg[blk, rows] = from_agg
            if k:
                hid[blk, rows] = grad + right_dot(pre_low, wts[3 + k])

        tiles(mesh_rows, body)

    turn = 3
    for k in (2, 1):
        for blk in (outer, inner):
            finish(turn, blk, hid if k == 2 else pre.at[1], k < 2)
            hooks.pause()
            mesh_backward(k, blk)
            send_back(proc, blk, turn + 1, mesh_rows)
        turn += 1
        for b in range(2):
            pre[k - 1, b] = own_back(proc, b, mesh_rows)
        hooks.pause()
        hooks.put(7 + k, left_dot(flat(act[...]), flat(d_inner[...])))
        hooks.put(k, left_dot(flat(aggs[k]), flat(d_pre[...])))
        hooks.put(3 + k, left_dot(flat(ext[k - 1, 1:3]), flat(d_pre[...])))
    for blk in (outer, inner):
        finish(turn, blk, pre.at[0], True)
        hooks.pause()
        mesh_backward(0, blk)
    hooks.pause()
    hooks.put(7, left_dot(flat(act[...]), flat(d_inner[...])))
    hooks.put(0, left_dot(flat(aggs[0]), flat(d_pre[...])))
    embed_grad = None
    for b in range(4):
        total = None
        for blk in range(2):
            region = b - blk
            if 0 <= region < 3:
                cols = slice(region * grid_rows, (region + 1) * grid_rows)
                part = left_dot(enc[blk, :, cols], d_agg[blk])
                total = part if total is None else total + part
        low = total.astype(jnp.bfloat16)
        if b in (1, 2):
            low = (grid_hid[b - 1] + low.astype(jnp.float32)).astype(jnp.bfloat16)
            rows = cells[(b - 1) * grid_rows : b * grid_rows, :lanes]
        else:
            rows = halo[b // 3]
        part = left_dot(low, rows)
        embed_grad = part if embed_grad is None else embed_grad + part
    gains[...] = jnp.zeros_like(gains)
    gains[first_gain : first_gain + 4, :] = gain_grads[0:4, :]
    across = gains[...].T
    split = group - lanes
    hooks.put(
        last,
        jnp.concatenate([embed_grad, head_grad[:, :split], head_grad[:, split:] + across], axis=1),
    )
    for blk in range(2):
        for n in range(3):
            sent(n, blk, ext.at[n, 1 + blk])
        sent(5, blk, parcel.at[blk])


class Loads:
    def __init__(self, sem, pairs):
        self.copies = {}
        for n, (name, (src, dst)) in enumerate(pairs.items()):
            self.copies[name] = pltpu.make_async_copy(src, dst, sem.at[n])
            self.copies[name].start()

    def need(self, *names):
        for name in names:
            if name != "targets":
                self.copies[name].wait()

    def pump(self, count):
        pass

    def between(self, k):
        pass


class Store:
    def __init__(self, grads_ref, low_ref, stage, stage_low, sem):
        self.refs = (grads_ref, low_ref)
        self.stages = (stage, stage_low)
        self.sem = sem
        self.copies = []

    def put(self, mat, value):
        side = len(self.copies) % 2
        if len(self.copies) >= 2:
            for copy in self.copies[-2]:
                copy.wait()
        copies = []
        for n, (ref, stage) in enumerate(zip(self.refs, self.stages)):
            stage[side] = value.astype(stage.dtype)
            copies.append(pltpu.make_async_copy(stage.at[side], ref.at[mat], self.sem.at[side, n]))
            copies[-1].start()
        self.copies.append(copies)

    def pause(self):
        pass

    def finish(self):
        for copies in self.copies[-2:]:
            for copy in copies:
                copy.wait()


class Reduce:
    def __init__(self, plan, spot, refs, sems):
        self.plan, self.spot = plan, spot
        self.acc, self.low, self.twin_in, self.plane_out, self.plane_in = refs[:5]
        self.hop_out, self.hop_in, self.own = refs[5:]
        self.twin_send, self.twin_recv, self.plane_send, self.plane_recv = sems[:4]
        self.hop_send, self.hop_recv = sems[4:]
        self.batch, self.phase = -1, 0
        self.batches = []
        self.twins, self.planes, self.hops = {}, {}, {}

    def follow(self, source):
        self.need, self.pump, self.between = source.need, source.pump, source.between

    def put(self, mat, value):
        size = self.acc.shape[0]
        if not self.batches or len(self.batches[-1]) == size:
            self.batches.append([])
            self.batch, self.phase = len(self.batches) - 1, 0
            if self.batch:
                for copy in self.twins[self.batch - 1]:
                    copy.wait_send()
            self.twins[self.batch] = []
        slot = len(self.batches[-1])
        self.batches[-1].append(mat)
        rows, width = self.acc.shape[-2:]
        halves = value.reshape(-1, 2, rows, width)
        first = self.spot.core == 0
        shape = self.acc.shape[1:]
        self.acc[slot] = jnp.where(first, halves[:, 0], halves[:, 1]).reshape(shape)
        theirs = jnp.where(first, halves[:, 1], halves[:, 0]).reshape(shape)
        self.low[slot] = theirs.astype(self.low.dtype)
        side = self.batch % 2
        copy = remote(
            self.low.at[slot],
            self.twin_in.at[side, slot],
            self.twin_send.at[slot],
            self.twin_recv.at[side, slot],
            self.spot.sibling(),
        )
        copy.start()
        self.twins[self.batch].append(copy)

    def pause(self):
        self.phase += 1
        self.advance(self.phase)

    def index(self, fixed):
        return tuple(fixed.get(b, slice(None)) for b in range(self.plan.bits - 1, -1, -1))

    def advance(self, phase):
        spot, bits = self.spot, self.plan.bits
        size = self.acc.shape[0]
        batch = self.batch
        rows, width = self.acc.shape[-2:]
        if phase == 1:
            for copy in self.twins[batch]:
                copy.wait_recv()
            side = batch % 2

            def body(n, _):
                slot, item = n // MICRO, n % MICRO
                self.acc[slot, item] += self.twin_in[side, slot, item].astype(jnp.float32)
                return 0

            lax.fori_loop(0, size * MICRO, body, 0)
        elif phase <= bits + 1:
            self.add(batch, phase - 2)
        if phase <= bits:
            self.send(batch, phase - 1)
        elif phase == bits + 1:
            if batch:
                for copy in self.hops[batch - 1]:
                    copy.wait_send()
            self.hops[batch] = []
            mine = self.index({b: spot.bit(b) for b in range(bits)})
            for slot in range(size):
                self.own[batch, slot] = self.acc[(slot, spot.z) + mine]
                for d in range(1, MICRO):
                    value = self.acc[(slot, (spot.z + d) % MICRO) + mine]
                    self.hop_out[d - 1, slot] = value.astype(self.hop_out.dtype)
            for d in range(1, MICRO):
                copy = remote(
                    self.hop_out.at[d - 1],
                    self.hop_in.at[batch, d - 1],
                    self.hop_send.at[d - 1],
                    self.hop_recv.at[batch, d - 1],
                    spot.peer_z(d),
                )
                copy.start()
                self.hops[batch].append(copy)

    def steps(self, t, d):
        bits = self.plan.bits
        count = 1 << (bits - 1 - t)
        at = sum(1 << (bits - 1 - s) for s in range(t))
        done = [(d + s) % bits for s in range(t)]
        return (d + t) % bits, done, at, count

    def send(self, batch, t):
        spot = self.spot
        size = self.acc.shape[0]
        rows, width = self.acc.shape[-2:]
        for d in range(MICRO):
            b, done, at, count = self.steps(t, d)
            if batch:
                self.planes[batch - 1, t, d].wait_send()
            item = (spot.z + d) % MICRO
            fixed = {n: spot.bit(n) for n in done}
            fixed[b] = 1 - spot.bit(b)
            theirs = self.index(fixed)

            def body(slot, _):
                value = self.acc[(slot, item) + theirs].reshape(count, rows, width)
                self.plane_out[d, slot, at : at + count] = value.astype(self.plane_out.dtype)
                return 0

            lax.fori_loop(0, size, body, 0)
            where = (d, slice(None), pl.ds(at, count))
            copy = remote(
                self.plane_out.at[where],
                self.plane_in.at[(batch,) + where],
                self.plane_send.at[t, d],
                self.plane_recv.at[batch, t, d],
                spot.peer_bit(b),
            )
            copy.start()
            self.planes[batch, t, d] = copy

    def add(self, batch, t):
        spot = self.spot
        size = self.acc.shape[0]
        for d in range(MICRO):
            b, done, at, count = self.steps(t, d)
            self.planes[batch, t, d].wait_recv()
            item = (spot.z + d) % MICRO
            mine = self.index({n: spot.bit(n) for n in done + [b]})

            def body(slot, _):
                where = (slot, item) + mine
                value = self.acc[where]
                came = self.plane_in[batch, d, slot, at : at + count].astype(jnp.float32)
                self.acc[where] = value + came.reshape(value.shape)
                return 0

            lax.fori_loop(0, size, body, 0)

    def finish(self, share_ref):
        for phase in range(self.phase + 1, self.plan.bits + 2):
            self.advance(phase)
        square = None
        for batch, mats in enumerate(self.batches):
            for copy in self.hops[batch]:
                copy.wait_recv()
            for slot, mat in enumerate(mats):
                value = self.own[batch, slot]
                for d in range(MICRO - 1):
                    value = value + self.hop_in[batch, d, slot].astype(jnp.float32)
                share_ref[mat] = value
                square = value * value if square is None else square + value * value
        last = len(self.batches) - 1
        for copy in self.twins[last] + self.hops[last]:
            copy.wait_send()
        for t in range(self.plan.bits):
            for d in range(MICRO):
                self.planes[last, t, d].wait_send()
        return square


def add_up(plan, spot, tile, refs, sems):
    send, recv = sems

    def exchange(tile, buffer, index, targets, at):
        buffer[index] = tile
        copies = []
        for n, to in enumerate(targets):
            copies.append(remote(buffer.at[index], buffer.at[index], send.at[at + n], recv.at[at + n], to))
            copies[-1].start()
        for copy in copies:
            copy.wait()
        total = buffer[0]
        for n in range(1, buffer.shape[0]):
            total = total + buffer[n]
        return total

    chips = plan.chips
    plane = [spot.in_plane((spot.p + d) % chips, spot.core) for d in range(1, chips)]
    plane += [spot.in_plane((spot.p + d) % chips, 1 - spot.core) for d in range(chips)]
    tile = exchange(tile, refs[0], 2 * spot.p + spot.core, plane, 0)
    return exchange(tile, refs[1], spot.z, [spot.peer_z(d) for d in range(1, MICRO)], 2 * chips - 1)


def fold_rows(square, lanes):
    square = jnp.sum(square, axis=0, keepdims=True)
    return sum(square[:, n : n + lanes] for n in range(0, square.shape[1], lanes))


def network_scratch(shapes):
    low, full = jnp.bfloat16, jnp.float32
    mesh_rows, grid_rows, width, lanes = shapes
    mesh_pair, grid_pair = (2, mesh_rows, width), (2, grid_rows, width)
    return [
        pltpu.VMEM((4,) + grid_pair[1:], low),
        pltpu.VMEM(grid_pair, full),
        pltpu.VMEM((3, 4) + mesh_pair[1:], low),
        pltpu.VMEM(mesh_pair, full),
        pltpu.VMEM((2,) + mesh_pair, full),
        pltpu.VMEM((3,) + mesh_pair, low),
        pltpu.VMEM(grid_pair, low),
        pltpu.VMEM((width, lanes), full),
        pltpu.VMEM(mesh_pair, low),
        pltpu.VMEM(mesh_pair, low),
        pltpu.VMEM(mesh_pair, low),
        pltpu.VMEM(mesh_pair, low),
        pltpu.VMEM(mesh_pair, low),
        pltpu.VMEM((128, width), full),
        pltpu.VMEM((8, width), full),
        pltpu.SemaphoreType.DMA((6, 2)),
        pltpu.SemaphoreType.DMA((6, 2)),
    ]


def reduce_scratch(plan, mats, rows, width):
    low, full = jnp.bfloat16, jnp.float32
    dma = pltpu.SemaphoreType.DMA
    batches, size = mats // 3, 3
    piece = (MICRO,) + (2,) * plan.bits + (rows, width)
    steps = (1 << plan.bits) - 1
    return [
        pltpu.VMEM((size,) + piece, full),
        pltpu.VMEM((size,) + piece, low),
        pltpu.VMEM((2, size) + piece, low),
        pltpu.VMEM((MICRO, size, steps, rows, width), low),
        pltpu.VMEM((batches, MICRO, size, steps, rows, width), low),
        pltpu.VMEM((MICRO - 1, size, rows, width), low),
        pltpu.VMEM((batches, MICRO - 1, size, rows, width), low),
        pltpu.VMEM((batches, size, rows, width), full),
    ], [
        dma((size,)),
        dma((2, size)),
        dma((plan.bits, MICRO)),
        dma((batches, plan.bits, MICRO)),
        dma((MICRO - 1,)),
        dma((batches, MICRO - 1)),
    ]


def load_pairs(ins, wts, cells, halo, graphs):
    pack_ref, cells_ref, halo_ref, *graph_refs = ins
    last = wts.shape[0] - 1
    pairs = {"last": (pack_ref.at[SLOTS[last]], wts.at[SLOTS[last]]), "halo": (halo_ref, halo), "cells": (cells_ref, cells)}

    def mats(*names):
        for n in names:
            pairs[n] = (pack_ref.at[SLOTS[n]], wts.at[SLOTS[n]])

    pairs["enc"] = (graph_refs[0], graphs[0])
    mats(0, 7)
    pairs["proc"] = (graph_refs[1], graphs[1])
    mats(1, 4, 8, 2, 5, 9)
    pairs["dec"] = (graph_refs[2], graphs[2])
    mats(3, 6, 10)
    return pairs


def train_kernel(plan, variables, *refs):
    ins, refs = refs[:6], refs[6:]
    outs, refs = refs[:3], refs[3:]
    data, refs = refs[:6], refs[6:]
    work, refs = refs[:17], refs[17:]
    load_sem, refs = refs[0], refs[1:]
    wts, cells, halo, *graphs = data
    spot = Spot(plan)
    loads = Loads(load_sem, load_pairs(ins, wts, cells, halo, graphs))
    spot.meet()
    hooks = Store(outs[0], outs[1], *refs)
    hooks.need, hooks.pump, hooks.between = loads.need, loads.pump, loads.between
    network(plan, spot, variables, hooks, outs[2], Matrices(wts), *data[1:], *work)
    hooks.finish()


def train(plan, variables, pack, cells, halo, encoder, processor, decoder):
    mats, width = pack.shape[0], pack.shape[2]
    lanes = halo.shape[-1]
    any_space = pl.BlockSpec(memory_space=pl.ANY)
    vmem = pl.BlockSpec(memory_space=pltpu.VMEM)
    dma = pltpu.SemaphoreType.DMA
    low, full = jnp.bfloat16, jnp.float32
    stats = jax.ShapeDtypeStruct((8, 128), full)
    out_shape = (jax.ShapeDtypeStruct(pack.shape, full), jax.ShapeDtypeStruct(pack.shape, low), stats)
    out_specs = (any_space, any_space, vmem)
    more = [pltpu.VMEM((2, width, width), full), pltpu.VMEM((2, width, width), low), dma((2, 2))]
    ins = (pack, cells, halo, encoder, processor, decoder)
    shapes = (encoder.shape[1], decoder.shape[1], width, lanes)
    return pl.pallas_call(
        functools.partial(train_kernel, plan, variables),
        out_shape=out_shape,
        in_specs=[any_space] * 6,
        out_specs=out_specs,
        scratch_shapes=[pltpu.VMEM(value.shape, low) for value in ins]
        + network_scratch(shapes)
        + [dma((mats + 5,))]
        + more,
        compiler_params=pltpu.CompilerParams(
            collective_id=2, has_side_effects=True, vmem_limit_bytes=63 << 20
        ),
        name="train",
    )(*ins)


LAG = 5
EARLY = 7
HOP_EVERY = 3


class Gather:
    def __init__(self, plan, spot, shapes, ins, data, bufs, sems):
        self.plan, self.spot, self.shapes = plan, spot, shapes
        self.pack, self.cells_in, self.codes_in = ins
        self.wts, self.cells, self.halo, *self.graphs = data
        self.codes, self.code_hop, self.cell_hop, self.sums = bufs
        self.own_sem, self.hop_send, self.hop_recv, self.plane_send, self.plane_recv = sems[:5]
        self.twin_send, self.twin_recv, self.move_send, self.move_recv = sems[5:]
        self.size = 3
        self.parts = self.wts.shape[0] // self.size
        self.half = self.cells_in.shape[1]
        self.lanes = self.halo.shape[-1]
        self.sent, self.hops, self.planes, self.twins, self.moves = [], {}, {}, {}, []
        self.todo, self.done = [], set()
        z, p, core = spot.z, spot.p, spot.core
        block = p % 4
        self.bb, self.to_core = block % 2, block // 2

    def mats(self, part):
        return pl.ds(part * self.size, self.size)

    def region(self, part, z, done):
        return (self.mats(part), z) + self.spot.held(done) + (self.spot.core,)

    def wide(self, n):
        return pl.ds(n * self.lanes, self.lanes)

    def hop_slot(self, d, n):
        ref, first = self.cell_hop[d - 1]
        return ref.at[pl.ds(first, self.half), self.wide(n)]

    def code_part(self):
        size = self.code_hop.shape[1]
        return pl.ds(pl.multiple_of(self.spot.core * size, 8), size)

    def start(self):
        spot = self.spot
        every = self.region(0, spot.z, ())[1:]
        self.own = pltpu.make_async_copy(self.pack, self.wts.at[(slice(None),) + every], self.own_sem)
        self.own.start()
        spot.meet()
        self.jobs = ["codes", "cells", 0, 1, 2, 3, "targets"]
        for job in self.jobs[:EARLY]:
            self.hop(job)
        for d in range(MICRO):
            if d:
                self.hops["codes", d].wait_recv()
                codes = self.code_hop.at[d - 1]
            else:
                codes = self.codes_in.at[self.code_part()]
            chip, _ = self.places(d)
            dst = self.codes.at[self.bb, self.code_part()]
            self.move(0, d, codes, dst, self.bb * 2 + spot.core, chip, self.to_core)
        self.own.wait()
        for d in range(MICRO):
            self.todo.append((("cells", d), functools.partial(self.move_cells, d)))
        units = [(part, 0) for part in range(self.parts)]
        units += [(part, d) for part in range(self.parts) for d in range(1, MICRO)]
        self.units = units
        bits = self.plan.bits
        for tick in range(len(units) + bits * LAG):
            if tick % HOP_EVERY == 0 and EARLY + tick // HOP_EVERY < len(self.jobs):
                job = self.jobs[EARLY + tick // HOP_EVERY]
                self.todo.append((("hop", job), functools.partial(self.hop, job)))
            self.todo.append((("tick", tick), functools.partial(self.tick, units, tick)))
        for d in range(MICRO):
            self.todo.append((("targets", d), functools.partial(self.move_targets, d)))

    def hop(self, job):
        spot = self.spot
        every = self.region(0, spot.z, ())[1:]
        n = self.jobs.index(job)
        for d in range(1, MICRO):
            m = (spot.z + d) % MICRO
            if job == "codes":
                pair = self.codes_in.at[self.code_part()], self.code_hop.at[d - 1]
            elif job == "cells":
                pair = self.cells_in.at[m, :, self.wide(0)], self.hop_slot(d, 0)
            elif job == "targets":
                pair = self.cells_in.at[m, :, self.wide(1)], self.hop_slot(d, 1)
            else:
                pair = self.pack.at[self.mats(job)], self.wts.at[(self.mats(job),) + every]
            copy = remote(*pair, self.hop_send.at[d - 1, n], self.hop_recv.at[d - 1, n], spot.peer_z(d))
            copy.start()
            self.hops[job, d] = copy
            self.sent.append(copy)

    def places(self, d):
        chips = self.plan.chips
        j = (((self.spot.z - d) % MICRO) * chips + self.spot.p) // 4
        q = (2 * j + self.to_core + 2 * self.bb - 1) % (2 * chips)
        return walk(j, self.plan.width), (walk(q // 2, self.plan.width), q % 2)

    def move(self, kind, d, src, dst, slot, chip, to_core):
        spot = self.spot
        here = jnp.logical_and(chip == spot.p, to_core == spot.core)
        sem = self.move_recv.at[kind, slot]
        copy = remote(src, dst, self.move_send.at[kind, d], sem, spot.in_plane(chip, to_core))

        @pl.when(here)
        def _():
            pltpu.make_async_copy(src, dst, sem).start()

        @pl.when(jnp.logical_not(here))
        def _():
            copy.start()

        self.moves.append((here, copy))

    def rows(self, bb, core):
        return pl.ds(pl.multiple_of((bb * 2 + core) * self.half, 16), self.half)

    def move_cells(self, d):
        if d:
            self.hops["cells", d].wait_recv()
            src = self.hop_slot(d, 0)
        else:
            src = self.cells_in.at[self.spot.z, :, self.wide(0)]
        core = self.spot.core
        chip, near = self.places(d)
        side = 1 - self.bb
        dst = self.halo.at[side, pl.ds(pl.multiple_of(core * self.half, 16), self.half)]
        self.move(1, d, src, dst, side * 2 + core, *near)
        dst = self.cells.at[self.rows(self.bb, core), self.wide(0)]
        self.move(2, d, src, dst, self.bb * 2 + core, chip, self.to_core)

    def move_targets(self, d):
        if d:
            self.hops["targets", d].wait_recv()
            src = self.hop_slot(d, 1)
        else:
            src = self.cells_in.at[self.spot.z, :, self.wide(1)]
        core = self.spot.core
        chip, _ = self.places(d)
        dst = self.cells.at[self.rows(self.bb, core), self.wide(1)]
        self.move(3, d, src, dst, self.bb * 2 + core, chip, self.to_core)

    def moved(self, kind):
        for n in range(4):
            side, core = n // 2, n % 2
            if kind == 0:
                size = self.code_hop.shape[1]
                dst = self.codes.at[side, pl.ds(core * size, size)]
            elif kind == 1:
                dst = self.halo.at[side, pl.ds(core * self.half, self.half)]
            else:
                dst = self.cells.at[pl.ds(n * self.half, self.half), self.wide(kind - 2)]
            pltpu.make_async_copy(dst, dst, self.move_recv.at[kind, n]).wait()

    def tick(self, units, tick):
        bits, spot = self.plan.bits, self.spot
        for t in range(bits, -1, -1):
            u = tick - t * LAG
            if u < 0 or u >= len(units):
                continue
            part, d = units[u]
            if t:
                self.planes[u, t - 1].wait_recv()
            elif d:
                self.hops[part, d].wait_recv()
            order = [(part + s) % bits for s in range(bits)]
            where = self.wts.at[self.region(part, (spot.z - d) % MICRO, order[:t])]
            if t < bits:
                to = spot.peer_bit(order[t])
                copy = remote(where, where, self.plane_send.at[u, t], self.plane_recv.at[u, t], to)
                self.planes[u, t] = copy
            else:
                copy = remote(where, where, self.twin_send.at[u], self.twin_recv.at[u], spot.sibling())
                self.twins[u] = copy
            copy.start()
            self.sent.append(copy)

    def pump(self, count):
        for _ in range(count):
            if self.todo:
                name, action = self.todo.pop(0)
                action()
                self.done.add(name)

    def until(self, name):
        while name not in self.done:
            self.pump(1)

    def once(self, name, action):
        if name not in self.done:
            action()
            self.done.add(name)

    def need(self, *names):
        for name in names:
            if name in ("enc", "proc", "dec"):
                continue
            if name == "cells":
                self.until(("cells", MICRO - 1))
                self.moved(2)
            elif name == "halo":
                self.until(("cells", MICRO - 1))
                self.moved(1)
            elif name == "targets":
                pass
            else:
                mat = self.wts.shape[0] - 1 if name == "last" else name
                part = SLOTS[mat] // self.size
                if ("part", part) in self.done:
                    continue
                mine = [u for u, unit in enumerate(self.units) if unit[0] == part]
                self.until(("tick", max(mine) + self.plan.bits * LAG))
                for u in mine:
                    self.twins[u].wait_recv()
                self.done.add(("part", part))

    def build(self, n, block, tiles, sums):
        first, edges, rows, columns = self.shapes[n]
        chunk = math.gcd(edges, 1024) // 128
        width = self.sums.shape[-1]
        spans = [(tile * width, min(width, columns - tile * width)) for tile in tiles]

        def ones(row, count):
            place = lax.broadcasted_iota(jnp.int32, (count, 128), 0).astype(jnp.int16)
            hit = place == row.astype(jnp.int16)
            return jnp.where(hit, jnp.bfloat16(1), jnp.bfloat16(0)).astype(jnp.float8_e4m3fn)

        def area(at, size):
            return at + (pl.ds(0, rows), pl.ds(0, size))

        for at, (_, size) in zip(sums, spans):
            self.sums[area(at, size)] = jnp.zeros((rows, size), jnp.float32)

        def body(k, _):
            codes = [self.codes[block, pl.ds(first + k * chunk + i, 1), :] for i in range(chunk)]
            into = jnp.concatenate([ones(code >> CODE_BITS, rows) for code in codes], axis=1)
            for at, (start, size) in zip(sums, spans):
                out = [ones((code & ((1 << CODE_BITS) - 1)) - start, size) for code in codes]
                self.sums[area(at, size)] += right_dot(into, jnp.concatenate(out, axis=1))
            return 0

        lax.fori_loop(0, edges // (128 * chunk), body, 0)
        for at, (start, size) in zip(sums, spans):
            self.graphs[n][block, :, start : start + size] = self.sums[area(at, size)].astype(jnp.bfloat16)

    def prepare(self):
        self.moved(0)
        width = self.sums.shape[-1]
        every = [(0, 0), (0, 1), (1, 0), (1, 1)]
        for n, block, count in ((0, 0, 2), (0, 1, 4), (1, 0, 6), (1, 1, 4)):
            tiles = list(range(-(-self.shapes[n][3] // width)))
            self.build(n, block, tiles, every[: len(tiles)])
            self.pump(count)

    def between(self, k):
        if k == 2:
            self.until(("targets", MICRO - 1))
            for here, copy in self.moves:

                @pl.when(jnp.logical_not(here))
                def _():
                    copy.wait_send()

            self.moves = []
            self.moved(3)
        if k in (1, 2):
            width = self.sums.shape[-1]
            tiles = list(range(-(-self.shapes[2][3] // width)))
            for n in range(0, len(tiles), 2):
                self.build(2, k - 1, tiles[n : n + 2], [(1, 0), (1, 1)])
                self.pump(2)

    def finish(self):
        for copy in self.sent:
            copy.wait_send()


def step_kernel(plan, variables, shapes, *refs):
    ins, refs = refs[:3], refs[3:]
    share_ref, total_ref, refs = refs[0], refs[1], refs[2:]
    data, refs = refs[:6], refs[6:]
    work, refs = refs[:17], refs[17:]
    reduce_refs, reduce_sems, refs = refs[:8], refs[8:14], refs[14:]
    tiles, tile_sems, refs = refs[:2], refs[2:4], refs[4:]
    codes, code_hop, stats, *sems = refs
    wts, cells, halo, *graphs = data
    ext, pre = work[2], work[4]
    half = ins[1].shape[1]
    cell_hop = [(ext.at[2, 1], 0), (ext.at[2, 1], half), (ext.at[2, 2], 0)]
    spot = Spot(plan)
    gather = Gather(plan, spot, shapes, ins, data, (codes, code_hop, cell_hop, pre), sems)
    gather.start()
    gather.prepare()
    hooks = Reduce(plan, spot, reduce_refs, reduce_sems)
    hooks.follow(gather)
    network(plan, spot, variables, hooks, stats, Matrices(wts), *data[1:], *work)
    square = fold_rows(hooks.finish(share_ref), stats.shape[1])
    row = lax.broadcasted_iota(jnp.int32, stats.shape, 0)
    tile = jnp.where(row == 0, square, stats[...])
    total_ref[...] = add_up(plan, spot, tile, tiles, tile_sems)
    gather.finish()


def step(plan, variables, shapes, pack, cells, codes):
    mats, rows, width = pack.shape
    _, half, lanes = cells.shape
    lanes //= 2
    chips, bits = plan.chips, plan.bits
    low, full = jnp.bfloat16, jnp.float32
    any_space = pl.BlockSpec(memory_space=pl.ANY)
    vmem = pl.BlockSpec(memory_space=pltpu.VMEM)
    dma = pltpu.SemaphoreType.DMA
    stats = jax.ShapeDtypeStruct((8, 128), full)
    buffers, sems = reduce_scratch(plan, mats, rows, width)
    mesh_rows, grid_rows = shapes[0][2], shapes[2][2]
    units = mats // 3 * MICRO
    return pl.pallas_call(
        functools.partial(step_kernel, plan, variables, shapes),
        out_shape=(jax.ShapeDtypeStruct((mats, rows, width), full), stats),
        in_specs=[any_space] * 3,
        out_specs=(vmem, vmem),
        scratch_shapes=[
            pltpu.VMEM((mats, MICRO) + (2,) * bits + (2, rows, width), low),
            pltpu.VMEM((4 * half, 2 * lanes), low),
            pltpu.VMEM((2, 2 * half, lanes), low),
        ]
        + [pltpu.VMEM((2,) + shape[2:], low) for shape in shapes]
        + network_scratch((mesh_rows, grid_rows, width, lanes))
        + buffers
        + sems
        + [pltpu.VMEM((n,) + stats.shape, full) for n in (2 * chips, MICRO)]
        + [dma((MICRO + 2 * chips - 2,))] * 2
        + [
            pltpu.VMEM((2,) + codes.shape, codes.dtype),
            pltpu.VMEM((MICRO - 1, codes.shape[0] // 2, codes.shape[1]), codes.dtype),
            pltpu.VMEM(stats.shape, full),
            dma,
            dma((MICRO - 1, 7)),
            dma((MICRO - 1, 7)),
            dma((units, bits)),
            dma((units, bits)),
            dma((units,)),
            dma((units,)),
            dma((4, MICRO)),
            dma((4, 4)),
        ],
        compiler_params=pltpu.CompilerParams(
            collective_id=3, has_side_effects=True, vmem_limit_bytes=63 << 20
        ),
        name="step",
    )(pack, cells, codes)


def adamw(param, first, second, grad, scale, rate):
    clipped = grad * scale
    moment = BETA_ONE * first + (1.0 - BETA_ONE) * clipped
    square = BETA_TWO * second + (1.0 - BETA_TWO) * clipped * clipped
    fixed_one = moment / (1.0 - BETA_ONE**STEP)
    fixed_two = square / (1.0 - BETA_TWO**STEP)
    fresh = param - rate * (fixed_one / (jnp.sqrt(fixed_two) + EPS_ADAM) + DECAY * param)
    return (fresh, moment, square, fresh.astype(jnp.bfloat16))


def on_device(
    plan,
    grid_in,
    targets,
    area_weight,
    grid_count,
    g2m_edges,
    mesh_edges,
    m2g_edges,
    edge_count,
    embed_weight,
    embed_first,
    embed_second,
    node_mats,
    mats_first,
    mats_second,
    head_weight,
    head_first,
    head_second,
    norm_gains,
    gains_first,
    gains_second,
):
    half, variables = grid_in.shape[1:]
    grid_rows = 2 * half
    mesh_rows = M_DEV
    lanes = -(-variables // 128) * 128
    core = lax.axis_index("feat")

    position = core * half + jnp.arange(half, dtype=jnp.int32)
    weights = jnp.where(position[None, :] < grid_count, area_weight, 0.0)
    pieces = []
    rest = weights
    for _ in range(3):
        piece = lax.reduce_precision(rest, 8, 7)
        pieces.append(piece.astype(jnp.bfloat16))
        rest = rest - piece
    cells = jnp.concatenate(
        [
            jnp.pad(grid_in, ((0, 0), (0, 0), (0, lanes - variables))),
            targets,
            jnp.pad(jnp.stack(pieces, axis=-1), ((0, 0), (0, 0), (0, lanes - variables - 3))),
        ],
        axis=-1,
    )
    last = jnp.concatenate(
        [
            jnp.pad(embed_weight.T, ((0, 0), (0, lanes - variables))),
            head_weight,
            jnp.pad(norm_gains.T, ((0, 0), (0, lanes - variables - 4))),
        ],
        axis=-1,
    )
    order = sorted(SLOTS, key=SLOTS.get)
    mats = [last if n == len(order) - 1 else node_mats[n] for n in order]
    pack = jnp.stack(mats).astype(jnp.bfloat16)
    graphs = ((g2m_edges, grid_rows, mesh_rows), (mesh_edges, mesh_rows, mesh_rows), (m2g_edges, mesh_rows, grid_rows))
    codes, shapes = [], []
    first = 0
    for n, (edges, columns, rows) in enumerate(graphs):
        per = edges.shape[1]
        alive = jnp.arange(per, dtype=jnp.int32) < edge_count[n, 0]
        codes.append(jnp.where(alive, edges[1] * (1 << CODE_BITS) + edges[0], -1))
        shapes.append((first // 128, per, rows, 3 * columns))
        first += per
    codes = jnp.concatenate(codes).reshape(-1, 128)
    rows, width = pack.shape[1:]
    if rows % 16 == 0:
        share, total = step(plan, variables, shapes, pack, cells, codes)
    else:
        gathered, main, halo, *counts = gather_all(plan, shapes, pack, cells, codes)
        full = gathered.reshape(-1, width, width)
        main = main.reshape(-1, 2 * lanes)
        halo = halo.reshape(2, grid_rows, lanes)
        grads, low, stats = train(plan, variables, full, main, halo, *counts)
        share, total = reduce_all(plan, grads.reshape(gathered.shape), low.reshape(gathered.shape), stats)
    square_sum, loss_sum, weight_sum = (jnp.sum(total[n]) for n in range(3))
    shares = (
        share[-1, :, :variables].T,
        share[:-1],
        share[-1, :, lanes : lanes + variables],
        share[-1, :, lanes + variables : lanes + variables + 4].T,
    )
    grad_norm = jnp.sqrt(square_sum)
    scale = jnp.minimum(1.0, CLIP / (grad_norm + 1e-06))
    return (
        loss_sum,
        weight_sum,
        grad_norm,
        *adamw(embed_weight, embed_first, embed_second, shares[0], scale, RATE),
        *adamw(node_mats, mats_first, mats_second, shares[1], scale, RATE),
        *adamw(head_weight, head_first, head_second, shares[2], scale, RATE),
        *adamw(norm_gains, gains_first, gains_second, shares[3], scale, GAIN_RATE),
    )


def solution(mesh):
    plan = Plan(mesh.shape["nodes"])
    cells = P(None, BOTH, None)
    columns = P(None, BOTH)
    rows = P(BOTH, None)
    blocks = P(None, "nodes")
    return jax.shard_map(
        lambda *args: on_device(plan, *args),
        mesh=mesh,
        in_specs=(
            (cells, cells, columns, blocks, blocks, blocks, blocks, blocks)
            + (columns,) * 3
            + (cells,) * 3
            + (rows,) * 3
            + (columns,) * 3
        ),
        out_specs=(P(), P(), P()) + (columns,) * 4 + (cells,) * 4 + (rows,) * 4 + (columns,) * 4,
        check_vma=False,
    )
```

```python
import functools
import math

import jax
import jax.numpy as jnp
from jax import lax
from jax.experimental import pallas as pl
from jax.experimental.pallas import tpu as pltpu
from jax.sharding import PartitionSpec as P

M_DEV = 640
STEP = 5
MICRO = 4


EPS_NORM = 1e-05
CLIP = 0.5
RATE = 0.04
GAIN_RATE = 0.4
BETA_ONE = 0.5
BETA_TWO = 0.6
EPS_ADAM = 1e-08
DECAY = 0.1

BOTH = ("nodes", "feat")


def matmul(a, b):
    return jnp.dot(a, b, preferred_element_type=jnp.float32)


def left_dot(a, b):
    return lax.dot_general(a, b, (((0,), (0,)), ((), ())), preferred_element_type=jnp.float32)


def right_dot(a, b):
    return lax.dot_general(a, b, (((1,), (1,)), ((), ())), preferred_element_type=jnp.float32)


class Plan:
    def __init__(self, nodes):
        self.nodes = nodes
        self.chips = nodes // MICRO
        self.bits = self.chips.bit_length() - 1
        width = math.isqrt(self.chips)
        self.width = width if width * width == self.chips else 0


MESH = pl.DeviceIdType.MESH
CODE_BITS = 12
SLOTS = {mat: slot for slot, mat in enumerate((11, 0, 7, 1, 4, 8, 2, 5, 9, 3, 6, 10))}


def walk(value, width):
    if width == 0:
        return value
    row, col = value // width, value % width
    return row * width + col + (row % 2) * (width - 1 - 2 * col)


class Spot:
    def __init__(self, plan):
        me = lax.axis_index("nodes")
        self.plan = plan
        self.core = lax.axis_index("feat")
        self.z = me // plan.chips
        self.p = me % plan.chips

    def bit(self, b):
        return (self.p // (1 << b)) % 2

    def peer_z(self, d):
        return {"nodes": ((self.z + d) % MICRO) * self.plan.chips + self.p, "feat": self.core}

    def peer_bit(self, b):
        other = self.p + (1 - 2 * self.bit(b)) * (1 << b)
        return {"nodes": self.z * self.plan.chips + other, "feat": self.core}

    def in_plane(self, p, core):
        return {"nodes": self.z * self.plan.chips + p, "feat": core}

    def sibling(self):
        return self.in_plane(self.p, 1 - self.core)

    def partners(self):
        chips = self.plan.chips
        found = [self.peer_z(d) for d in range(1, MICRO)]
        for turn in range(chips):
            p = (self.p + turn) % chips
            if turn:
                found.append(self.in_plane(p, self.core))
            found.append(self.in_plane(p, 1 - self.core))
        return found

    def meet(self):
        barrier = pltpu.get_barrier_semaphore()
        found = self.partners()
        for other in found:
            pl.semaphore_signal(barrier, inc=1, device_id=other, device_id_type=MESH)
        pl.semaphore_wait(barrier, len(found))

    def held(self, done):
        bits = range(self.plan.bits - 1, -1, -1)
        return tuple(slice(None) if b in done else self.bit(b) for b in bits)


def remote(src, dst, send, recv, to):
    return pltpu.make_async_remote_copy(
        src_ref=src, dst_ref=dst, send_sem=send, recv_sem=recv, device_id=to, device_id_type=MESH
    )


def gather_kernel(
    plan,
    shapes,
    pack_ref,
    cells_ref,
    codes_ref,
    all_ref,
    main_ref,
    halo_ref,
    enc_ref,
    proc_ref,
    dec_ref,
    graph_ref,
    total,
    whole,
    cell_hop,
    code_hop,
    own_sem,
    out_sem,
    hop_send,
    hop_recv,
    plane_send,
    plane_recv,
    twin_send,
    twin_recv,
    move_send,
    move_recv,
):
    spot = Spot(plan)
    z, p, core = spot.z, spot.p, spot.core
    chips, bits = plan.chips, plan.bits
    groups = bits
    mats = pack_ref.shape[0] // groups
    code_rows = codes_ref.shape[0] // 2
    lanes = halo_ref.shape[-1]
    own = pltpu.make_async_copy(pack_ref, all_ref.at[(slice(None), z) + spot.held(()) + (core,)], own_sem)
    own.start()
    spot.meet()
    my_codes = codes_ref.at[pl.ds(pl.multiple_of(core * code_rows, 8), code_rows)]
    hops = []
    for d in range(1, MICRO):
        to = spot.peer_z(d)
        m = (z + d) % MICRO
        for n, (src, dst) in enumerate(
            (
                (my_codes, code_hop.at[d - 1]),
                (cells_ref.at[m], cell_hop.at[d - 1]),
                (pack_ref, all_ref.at[(slice(None), z) + spot.held(()) + (core,)]),
            )
        ):
            copy = remote(src, dst, hop_send.at[d - 1, n], hop_recv.at[d - 1, n], to)
            copy.start()
            hops.append(copy)
    quarter = p % 4
    bb, to_core = quarter % 2, quarter // 2
    slot = bb * 2 + core
    half_slot = (1 - bb) * 2 + core
    moves = []

    def move(d, n, src, dst, sem, chip, to_core):
        here = jnp.logical_and(chip == p, to_core == core)
        copy = remote(src, dst, move_send.at[d, n], sem, spot.in_plane(chip, to_core))

        @pl.when(here)
        def _():
            pltpu.make_async_copy(src, dst, sem).start()

        @pl.when(jnp.logical_not(here))
        def _():
            copy.start()

        moves.append((here, copy))

    def spread_codes(d):
        block = ((z - d) % MICRO) * chips + p
        codes = my_codes if d == 0 else code_hop.at[d - 1]
        rows = pl.ds(pl.multiple_of(core * code_rows, 8), code_rows)
        dst = graph_ref.at[bb, rows]
        move(d, 0, codes, dst, move_recv.at[0, slot], walk(block // 4, plan.width), to_core)

    def spread(d):
        block = ((z - d) % MICRO) * chips + p
        j = block // 4
        chip = walk(j, plan.width)
        q = (2 * j + to_core + 2 * bb - 1) % (2 * chips)
        near = walk(q // 2, plan.width)
        cells = cells_ref.at[z] if d == 0 else cell_hop.at[d - 1]
        move(
            d,
            1,
            cells.at[:, pl.ds(0, lanes)],
            halo_ref.at[1 - bb, core],
            move_recv.at[1, half_slot],
            near,
            q % 2,
        )
        move(d, 2, cells, main_ref.at[bb, core], move_recv.at[2, slot], chip, to_core)

    def region(d, done):
        return ((z - d) % MICRO,) + spot.held(done) + (core,)

    planes = {}

    def step(d, g, t):
        done = tuple((g + s) % bits for s in range(t))
        where = (pl.ds(g * mats, mats),) + region(d, done)
        copy = remote(
            all_ref.at[where],
            all_ref.at[where],
            plane_send.at[d, g, t],
            plane_recv.at[d, g, t],
            spot.peer_bit((g + t) % bits),
        )
        copy.start()
        planes[d, g, t] = copy

    for d in range(MICRO):
        if d:
            hops[3 * (d - 1)].wait_recv()
        spread_codes(d)
    outs = []

    def build(n, side_block):
        first, edges, rows, columns = shapes[n]
        chunk = math.gcd(edges, 1024) // 128
        area = (pl.ds(0, rows), pl.ds(0, columns))

        def ones(row, count):
            place = lax.broadcasted_iota(jnp.int32, (count, 128), 0).astype(jnp.int16)
            hit = place == row.astype(jnp.int16)
            return jnp.where(hit, jnp.bfloat16(1), jnp.bfloat16(0)).astype(jnp.float8_e4m3fn)

        def body(k, _):
            into, out = [], []
            for i in range(chunk):
                code = graph_ref[side_block, pl.ds(first + k * chunk + i, 1), :]
                into.append(ones(code >> CODE_BITS, rows))
                out.append(ones(code & ((1 << CODE_BITS) - 1), columns))
            total[area] += right_dot(jnp.concatenate(into, axis=1), jnp.concatenate(out, axis=1))
            return 0

        total[area] = jnp.zeros((rows, columns), jnp.float32)
        lax.fori_loop(0, edges // (128 * chunk), body, 0)
        if len(outs) >= 2:
            outs[-2].wait()
        side = len(outs) % 2
        whole[(side,) + area] = total[area].astype(jnp.bfloat16)
        ref = (enc_ref, proc_ref, dec_ref)[n]
        copy = pltpu.make_async_copy(whole.at[(side,) + area], ref.at[side_block], out_sem.at[side])
        copy.start()
        outs.append(copy)

    work = [[], [(0, 0), (0, 1)], [(1, 0)], [(1, 1)], [(2, 0)], [(2, 1)]]
    twins = []
    for tick in range(MICRO + bits):
        for t in range(bits + 1):
            d = tick - t
            if d < 0 or d >= MICRO:
                continue
            if t == 0:
                if d == 0:
                    own.wait()
                else:
                    hops[3 * (d - 1) + 1].wait_recv()
                    hops[3 * (d - 1) + 2].wait_recv()
                spread(d)
            else:
                for g in range(groups):
                    planes[d, g, t - 1].wait_recv()
            if t < bits:
                for g in range(groups):
                    step(d, g, t)
            else:
                where = (slice(None),) + region(d, tuple(range(bits)))
                copy = remote(
                    all_ref.at[where], all_ref.at[where], twin_send.at[d], twin_recv.at[d], spot.sibling()
                )
                copy.start()
                twins.append(copy)
        if tick == 1:
            for n in range(4):
                dst = graph_ref.at[n // 2, pl.ds((n % 2) * code_rows, code_rows)]
                pltpu.make_async_copy(dst, dst, move_recv.at[0, n]).wait()
        for kind, block in work[tick] if tick < len(work) else []:
            build(kind, block)
    for copy in outs[-2:]:
        copy.wait()
    for copy in hops + list(planes.values()):
        copy.wait_send()
    for copy in twins:
        copy.wait()
    for here, copy in moves:

        @pl.when(jnp.logical_not(here))
        def _():
            copy.wait_send()

    for n in range(4):
        half, side = n % 2, n // 2
        for kind, dst in ((1, halo_ref.at[side, half]), (2, main_ref.at[side, half])):
            pltpu.make_async_copy(dst, dst, move_recv.at[kind, n]).wait()


def gather_all(plan, shapes, pack, cells, codes):
    mats, rows, width = pack.shape
    micro, half, lanes = cells.shape
    bits = plan.bits
    most_rows = max(shape[2] for shape in shapes)
    most_columns = max(shape[3] for shape in shapes)
    any_space = pl.BlockSpec(memory_space=pl.ANY)
    dma = pltpu.SemaphoreType.DMA
    return pl.pallas_call(
        functools.partial(gather_kernel, plan, shapes),
        out_shape=(
            jax.ShapeDtypeStruct((mats, MICRO) + (2,) * bits + (2, rows, width), pack.dtype),
            jax.ShapeDtypeStruct((2, 2, half, lanes), cells.dtype),
            jax.ShapeDtypeStruct((2, 2, half, lanes // 2), cells.dtype),
            *(jax.ShapeDtypeStruct((2,) + shape[2:], jnp.bfloat16) for shape in shapes),
        ),
        in_specs=[any_space] * 3,
        out_specs=(any_space,) * 6,
        scratch_shapes=[
            pltpu.VMEM((2,) + codes.shape, codes.dtype),
            pltpu.VMEM((most_rows, most_columns), jnp.float32),
            pltpu.VMEM((2, most_rows, most_columns), jnp.bfloat16),
            pltpu.VMEM((MICRO - 1, half, lanes), cells.dtype),
            pltpu.VMEM((MICRO - 1, codes.shape[0] // 2, codes.shape[1]), codes.dtype),
            dma,
            dma((2,)),
            dma((MICRO - 1, 3)),
            dma((MICRO - 1, 3)),
            dma((MICRO, bits, bits)),
            dma((MICRO, bits, bits)),
            dma((MICRO,)),
            dma((MICRO,)),
            dma((MICRO, 3)),
            dma((3, 4)),
        ],
        compiler_params=pltpu.CompilerParams(
            collective_id=0, has_side_effects=True, vmem_limit_bytes=48 << 20
        ),
        name="gather_all",
    )(pack, cells, codes)


def reduce_kernel(
    plan,
    grads_ref,
    low_ref,
    stats_ref,
    share_ref,
    total_ref,
    acc,
    twin_in,
    plane_out,
    plane_in,
    hop_out,
    hop_in,
    z_stats,
    plane_stats,
    twin_stats,
    own_sem,
    twin_send,
    twin_recv,
    plane_send,
    plane_recv,
    hop_send,
    hop_recv,
    stat_send,
    stat_recv,
):
    spot = Spot(plan)
    z, p, core = spot.z, spot.p, spot.core
    chips, bits = plan.chips, plan.bits
    groups = bits
    mats = grads_ref.shape[0]
    part = mats // groups
    every = (slice(None),) * bits
    order = [1, 2, 3, 0]
    owns = {}
    for d in order:
        item = (z + d) % MICRO
        owns[d] = pltpu.make_async_copy(
            grads_ref.at[(slice(None), item) + every + (core,)], acc.at[d], own_sem.at[d]
        )
        owns[d].start()
    spot.meet()
    twins = {}
    for d in order:
        item = (z + d) % MICRO
        twins[d] = remote(
            low_ref.at[(slice(None), item) + every + (1 - core,)],
            twin_in.at[d],
            twin_send.at[d],
            twin_recv.at[d],
            spot.sibling(),
        )
        twins[d].start()

    def starts(t):
        return sum(1 << (bits - 1 - s) for s in range(t))

    planes, hops = {}, []

    def send_step(d, g, t):
        done = tuple((g + s) % bits for s in range(t))
        b = (g + t) % bits
        count = 1 << (bits - 1 - t)
        at = starts(t)
        theirs = tuple(
            spot.bit(n) if n in done else (1 - spot.bit(n) if n == b else slice(None))
            for n in range(bits - 1, -1, -1)
        )

        def body(n, _):
            mat = g * part + n
            value = acc[(d, mat) + theirs]
            plane_out[d, mat, at : at + count] = value.reshape((count,) + value.shape[-2:]).astype(
                plane_out.dtype
            )
            return 0

        lax.fori_loop(0, part, body, 0)
        where = (d, pl.ds(g * part, part), pl.ds(at, count))
        planes[d, g, t] = remote(
            plane_out.at[where],
            plane_in.at[where],
            plane_send.at[d, g, t],
            plane_recv.at[d, g, t],
            spot.peer_bit(b),
        )
        planes[d, g, t].start()

    def add_step(d, g, t):
        planes[d, g, t].wait_recv()
        done = tuple((g + s) % bits for s in range(t + 1))
        count = 1 << (bits - 1 - t)
        at = starts(t)
        mine = tuple(spot.bit(n) if n in done else slice(None) for n in range(bits - 1, -1, -1))

        def body(n, _):
            mat = g * part + n
            where = (d, mat) + mine
            value = acc[where]
            came = plane_in[d, mat, at : at + count].astype(jnp.float32)
            acc[where] = value + came.reshape(value.shape)
            return 0

        lax.fori_loop(0, part, body, 0)

    for tick in range(MICRO + bits):
        for t in range(bits + 1):
            n = tick - t
            if n < 0 or n >= MICRO:
                continue
            d = order[n]
            if t == 0:
                owns[d].wait()
                twins[d].wait_recv()

                def body(mat, _):
                    acc[d, mat] = acc[d, mat] + twin_in[d, mat].astype(jnp.float32)
                    return 0

                lax.fori_loop(0, mats, body, 0)
            else:
                for g in range(groups):
                    add_step(d, g, t - 1)
            if t < bits:
                for g in range(groups):
                    send_step(d, g, t)
            elif d:

                def body(mat, _):
                    hop_out[d - 1, mat] = acc[(d, mat) + spot.held(())].astype(hop_out.dtype)
                    return 0

                lax.fori_loop(0, mats, body, 0)
                copy = remote(
                    hop_out.at[d - 1], hop_in.at[d - 1], hop_send.at[d - 1], hop_recv.at[d - 1], spot.peer_z(d)
                )
                copy.start()
                hops.append(copy)
    for copy in hops:
        copy.wait_recv()

    def body(mat, square):
        value = acc[(0, mat) + spot.held(())]
        for d in range(MICRO - 1):
            value = value + hop_in[d, mat].astype(jnp.float32)
        share_ref[mat] = value
        return square + value * value

    square = lax.fori_loop(0, mats, body, jnp.zeros(share_ref.shape[1:], jnp.float32))
    square = jnp.sum(square, axis=0, keepdims=True)
    lanes = total_ref.shape[1]
    square = sum(square[:, n : n + lanes] for n in range(0, square.shape[1], lanes))
    row = lax.broadcasted_iota(jnp.int32, total_ref.shape, 0)
    tile = jnp.where(row == 0, square, stats_ref[...])
    sends = []

    def exchange(buffer, index, targets, at):
        buffer[index] = tile
        copies = []
        for n, to in enumerate(targets):
            copy = remote(
                buffer.at[index], buffer.at[index], stat_send.at[at + n], stat_recv.at[at + n], to
            )
            copy.start()
            copies.append(copy)
        for copy in copies:
            copy.wait()
        total = buffer[0]
        for n in range(1, buffer.shape[0]):
            total = total + buffer[n]
        return total

    tile = exchange(z_stats, z, [spot.peer_z(d) for d in range(1, MICRO)], 0)
    tile = exchange(
        plane_stats, p, [spot.in_plane((p + d) % chips, core) for d in range(1, chips)], MICRO - 1
    )
    tile = exchange(twin_stats, core, [spot.sibling()], MICRO + chips - 2)
    total_ref[...] = tile
    for copy in list(twins.values()) + list(planes.values()) + hops:
        copy.wait_send()


def reduce_all(plan, grads, low, stats):
    mats, rows, width = grads.shape[0], grads.shape[-2], grads.shape[-1]
    bits, chips = plan.bits, plan.chips
    shards = (2,) * bits
    steps = chips - 1
    any_space = pl.BlockSpec(memory_space=pl.ANY)
    vmem = pl.BlockSpec(memory_space=pltpu.VMEM)
    dma = pltpu.SemaphoreType.DMA
    return pl.pallas_call(
        functools.partial(reduce_kernel, plan),
        out_shape=(
            jax.ShapeDtypeStruct((mats, rows, width), jnp.float32),
            jax.ShapeDtypeStruct(stats.shape, jnp.float32),
        ),
        in_specs=[any_space, any_space, vmem],
        out_specs=(vmem, vmem),
        scratch_shapes=[
            pltpu.VMEM((MICRO, mats) + shards + (rows, width), jnp.float32),
            pltpu.VMEM((MICRO, mats) + shards + (rows, width), low.dtype),
            pltpu.VMEM((MICRO, mats, steps, rows, width), jnp.bfloat16),
            pltpu.VMEM((MICRO, mats, steps, rows, width), jnp.bfloat16),
            pltpu.VMEM((MICRO - 1, mats, rows, width), jnp.bfloat16),
            pltpu.VMEM((MICRO - 1, mats, rows, width), jnp.bfloat16),
            pltpu.VMEM((MICRO,) + stats.shape, jnp.float32),
            pltpu.VMEM((chips,) + stats.shape, jnp.float32),
            pltpu.VMEM((2,) + stats.shape, jnp.float32),
            dma((MICRO,)),
            dma((MICRO,)),
            dma((MICRO,)),
            dma((MICRO, bits, bits)),
            dma((MICRO, bits, bits)),
            dma((MICRO - 1,)),
            dma((MICRO - 1,)),
            dma((MICRO + chips - 1,)),
            dma((MICRO + chips - 1,)),
        ],
        compiler_params=pltpu.CompilerParams(
            collective_id=1, has_side_effects=True, vmem_limit_bytes=56 << 20
        ),
        name="reduce_all",
    )(grads, low, stats)


class Matrices:
    def __init__(self, ref):
        self.ref = ref
        self.width = ref.shape[-1]
        self.shape = (ref.shape[0], self.width, self.width)

    def __getitem__(self, index):
        index = index if isinstance(index, tuple) else (index,)
        where = (SLOTS[index[0]],) + (slice(None),) * (len(self.ref.shape) - 2) + index[2:3]
        value = self.ref[where]
        return value.reshape(self.width, value.shape[-1])


def sigmoid(value):
    return 1.0 / (1.0 + jnp.exp(-value))


def centred(z):
    mean = jnp.mean(z, axis=-1, keepdims=True)
    away = z - mean
    spread = jnp.mean(away * away, axis=-1, keepdims=True)
    scale = lax.rsqrt(spread + EPS_NORM)
    return away * scale, scale


def network(
    plan,
    spot,
    variables,
    hooks,
    stats_ref,
    wts,
    cells,
    halo,
    enc,
    proc,
    dec,
    grid_low,
    grid_hid,
    ext,
    hid,
    pre,
    aggs,
    head_grad,
    act,
    d_inner,
    d_pre,
    d_agg,
    parcel,
    gains,
    gain_grads,
    ex_send,
    ex_recv,
):
    core = spot.core
    outer, inner = core, 1 - core
    lanes = halo.shape[-1]
    last = wts.shape[0] - 1
    mesh_rows, width = hid.shape[1:]
    grid_rows = grid_hid.shape[1]
    ring = 2 * walk(spot.p, plan.width) + core

    def near(blk):
        q = (ring + 2 * blk - 1 + 2 * plan.chips) % (2 * plan.chips)
        return spot.in_plane(walk(q // 2, plan.width), q % 2)

    def exchange(turn, blk, src):
        dst = ext.at[turn % 3, 3 * (1 - blk)]
        return remote(src, dst, ex_send.at[turn, blk], ex_recv.at[turn, blk], near(blk))

    def arrived(turn, blk):
        dst = ext.at[turn % 3, 3 * blk]
        pltpu.make_async_copy(dst, dst, ex_recv.at[turn, 1 - blk]).wait()

    def sent(turn, blk, src):
        pltpu.make_async_copy(src, src, ex_send.at[turn, blk]).wait()

    def tiles(rows, body):
        size = rows // (2 if rows == mesh_rows else 4)

        def one(n, _):
            body(pl.ds(pl.multiple_of(n * size, 16), size))
            return 0

        lax.fori_loop(0, rows // size, one, 0)

    hooks.need("last", "halo", "cells")
    group = (lanes + variables) // 128 * 128
    first_gain = lanes + variables - group
    gains[...] = wts[last, :, group : group + 128].astype(jnp.float32).T

    def gain(k):
        return gains[first_gain + k : first_gain + k + 1, :]

    gain_grads[...] = jnp.zeros_like(gain_grads)
    head_grad[...] = jnp.zeros_like(head_grad)
    stats_ref[...] = jnp.zeros_like(stats_ref)

    for b in range(4):
        if b in (0, 3):
            rows = halo[b // 3]
        else:
            rows = cells[(b - 1) * grid_rows : b * grid_rows, :lanes]
        hidden = right_dot(rows, wts[last, :, :lanes])
        if b in (1, 2):
            grid_hid[b - 1] = hidden
        grid_low[b] = hidden.astype(jnp.bfloat16)

    def forward(k, low_agg, base):
        value = matmul(low_agg, wts[k])
        if base is not None:
            value = value + matmul(base, wts[3 + k])
        active = (value * sigmoid(value)).astype(jnp.bfloat16)
        return value, active, matmul(active, wts[7 + k])

    def mesh_forward(k, blk):
        def body(rows):
            base = None if k == 0 else ext[k - 1, 1 + blk, rows]
            value, _, inside = forward(k, aggs[k, blk, rows], base)
            if k:
                pre[k - 1, blk, rows] = value
            result = centred(inside)[0] * gain(k)
            if k:
                result = hid[blk, rows] + result
            hid[blk, rows] = result
            ext[k, 1 + blk, rows] = result.astype(jnp.bfloat16)

        tiles(mesh_rows, body)
        exchange(k, blk, ext.at[k, 1 + blk]).start()
        hooks.pump()

    def collect(graph, blk, turn):
        size = mesh_rows
        own = pl.ds(pl.multiple_of(size * (1 - blk), 128), 2 * size)
        rest = pl.ds(pl.multiple_of(2 * size * blk, 128), size)
        total = matmul(graph[blk, :, own], ext[turn, 1:3].reshape(2 * size, width))
        arrived(turn, blk)
        total = total + matmul(graph[blk, :, rest], ext[turn, 3 * blk])
        return total.astype(jnp.bfloat16)

    hooks.need("enc")
    for blk in (outer, inner):
        senders = grid_low[pl.ds(blk, 3)].reshape(3 * grid_rows, width)
        aggs[0, blk] = matmul(enc[blk], senders).astype(jnp.bfloat16)
        if blk is outer:
            hooks.need(0, 7)
        mesh_forward(0, blk)
    hooks.need("proc")
    for k in (1, 2):
        hooks.between(k)
        hooks.need(k, 3 + k, 7 + k)
        for blk in (outer, inner):
            aggs[k, blk] = collect(proc, blk, k - 1)
            mesh_forward(k, blk)

    def through_norm(k, inside, grad):
        along, scale = centred(inside)
        gain_grads[k : k + 1, :] += jnp.sum(along * grad, axis=0, keepdims=True)
        grad = grad * gain(k)
        grad = grad - jnp.mean(grad, axis=-1, keepdims=True)
        grad = scale * (grad - along * jnp.mean(grad * along, axis=-1, keepdims=True))
        return grad.astype(jnp.bfloat16)

    def through_silu(k, value, low):
        back = right_dot(low, wts[7 + k])
        sig = sigmoid(value)
        return (back * sig * (1.0 + value * (1.0 - sig))).astype(jnp.bfloat16)

    def backward(k, value, inside, grad):
        low = through_norm(k, inside, grad)
        pre_low = through_silu(k, value, low)
        return low, pre_low, right_dot(pre_low, wts[k]).astype(jnp.bfloat16)

    def send_back(graph, blk, turn, rows):
        cols = pl.ds(pl.multiple_of(2 * mesh_rows * blk, 128), mesh_rows)
        if turn > 3:
            sent(turn - 1, blk, parcel.at[blk])
        parcel[blk] = left_dot(graph[blk, :, cols], d_agg[blk, pl.ds(0, rows)]).astype(jnp.bfloat16)
        exchange(turn, blk, parcel.at[blk]).start()

    def own_back(graph, b, rows):
        total = None
        for blk in range(2):
            region = b - blk + 1
            cols = pl.ds(pl.multiple_of(region * mesh_rows, 128), mesh_rows)
            part = left_dot(graph[blk, :, cols], d_agg[blk, pl.ds(0, rows)])
            total = part if total is None else total + part
        return total

    def flat(value):
        return value.reshape(value.shape[0] * value.shape[1], value.shape[2])

    used = pl.ds(0, grid_rows)
    hooks.between(3)
    hooks.need("targets", "dec", 3, 6, 10)
    for blk in (outer, inner):
        hid[blk, used] = collect(dec, blk, 2).astype(jnp.float32)

        def body(rows):
            base = grid_low[1 + blk, rows]
            value, active, inside = forward(3, hid[blk, rows].astype(jnp.bfloat16), base)
            out = grid_hid[blk, rows] + centred(inside)[0] * gain(3)
            low = out.astype(jnp.bfloat16)
            size = low.shape[0]
            cell = pl.ds(pl.multiple_of(blk * grid_rows + rows.start, 16), size)
            lane = lax.broadcasted_iota(jnp.int32, (size, 128), 1)
            tail = cells[cell, group : group + 128].astype(jnp.float32)
            piece = (lane >= first_gain) & (lane < first_gain + 3)
            weight = jnp.sum(jnp.where(piece, tail, 0.0), axis=1, keepdims=True)
            error = matmul(low, wts[last, :, lanes : 2 * lanes])
            error = error - cells[cell, lanes : 2 * lanes].astype(jnp.float32)
            place = lax.broadcasted_iota(jnp.int32, error.shape, 1)
            error = jnp.where(place < variables, error, 0.0)
            weighted = weight * error
            loss = jnp.sum(weighted * error, axis=0, keepdims=True)
            stats_ref[1:2, :] += sum(loss[:, n : n + 128] for n in range(0, lanes, 128))
            stats_ref[2:3, :] += jnp.sum(jnp.where(lane == 0, weight, 0.0), axis=0, keepdims=True)
            pred_low = (2.0 * weighted).astype(jnp.bfloat16)
            head_grad[...] += left_dot(low, pred_low)
            grad = right_dot(pred_low, wts[last, :, lanes : 2 * lanes])
            inner_low, pre_low, from_agg = backward(3, value, inside, grad)
            act[blk, rows] = active
            d_inner[blk, rows] = inner_low
            d_pre[blk, rows] = pre_low
            d_agg[blk, rows] = from_agg
            grid_hid[blk, rows] = grad + right_dot(pre_low, wts[6])

        tiles(grid_rows, body)
        send_back(dec, blk, 3, grid_rows)
    hooks.put(10, left_dot(flat(act[:, used]), flat(d_inner[:, used])))
    hooks.put(3, left_dot(flat(hid[:, used]).astype(jnp.bfloat16), flat(d_pre[:, used])))
    hooks.put(6, left_dot(flat(grid_low[1:3]), flat(d_pre[:, used])))
    for b in range(2):
        hid[b] = own_back(dec, b, grid_rows)

    def finish(turn, blk, total_ref, add):
        arrived(turn, blk)

        def body(rows):
            total = total_ref[blk, rows] + ext[turn % 3, 3 * blk, rows].astype(jnp.float32)
            total = total.astype(jnp.bfloat16).astype(jnp.float32)
            hid[blk, rows] = hid[blk, rows] + total if add else total

        tiles(mesh_rows, body)

    def mesh_backward(k, blk):
        def pre_of(rows):
            return pre[k - 1, blk, rows] if k else matmul(aggs[0, blk, rows], wts[0])

        def upper(rows):
            value = pre_of(rows)
            active = (value * sigmoid(value)).astype(jnp.bfloat16)
            act[blk, rows] = active
            d_inner[blk, rows] = through_norm(k, matmul(active, wts[7 + k]), hid[blk, rows])

        def lower(rows):
            pre_low = through_silu(k, pre_of(rows), d_inner[blk, rows])
            d_pre[blk, rows] = pre_low
            d_agg[blk, rows] = right_dot(pre_low, wts[k]).astype(jnp.bfloat16)
            if k:
                hid[blk, rows] += right_dot(pre_low, wts[3 + k])

        tiles(mesh_rows, upper)
        tiles(mesh_rows, lower)

    turn = 3
    for k in (2, 1):
        for blk in (outer, inner):
            finish(turn, blk, hid if k == 2 else pre.at[1], k < 2)
            hooks.pause()
            mesh_backward(k, blk)
            send_back(proc, blk, turn + 1, mesh_rows)
        turn += 1
        for b in range(2):
            pre[k - 1, b] = own_back(proc, b, mesh_rows)
        hooks.pause()
        hooks.put(7 + k, left_dot(flat(act[...]), flat(d_inner[...])))
        hooks.put(k, left_dot(flat(aggs[k]), flat(d_pre[...])))
        hooks.put(3 + k, left_dot(flat(ext[k - 1, 1:3]), flat(d_pre[...])))
    for blk in (outer, inner):
        finish(turn, blk, pre.at[0], True)
        hooks.pause()
        mesh_backward(0, blk)
    hooks.pause()
    hooks.put(7, left_dot(flat(act[...]), flat(d_inner[...])))
    hooks.put(0, left_dot(flat(aggs[0]), flat(d_pre[...])))
    embed_grad = None
    for b in range(4):
        total = None
        for blk in range(2):
            region = b - blk
            if 0 <= region < 3:
                cols = slice(region * grid_rows, (region + 1) * grid_rows)
                part = left_dot(enc[blk, :, cols], d_agg[blk])
                total = part if total is None else total + part
        low = total.astype(jnp.bfloat16)
        if b in (1, 2):
            low = (grid_hid[b - 1] + low.astype(jnp.float32)).astype(jnp.bfloat16)
            rows = cells[(b - 1) * grid_rows : b * grid_rows, :lanes]
        else:
            rows = halo[b // 3]
        part = left_dot(low, rows)
        embed_grad = part if embed_grad is None else embed_grad + part
    gains[...] = jnp.zeros_like(gains)
    gains[first_gain : first_gain + 4, :] = gain_grads[0:4, :]
    across = gains[...].T
    split = group - lanes
    hooks.put(
        last,
        jnp.concatenate([embed_grad, head_grad[:, :split], head_grad[:, split:] + across], axis=1),
    )
    for blk in range(2):
        for n in range(3):
            sent(n, blk, ext.at[n, 1 + blk])
        sent(5, blk, parcel.at[blk])


class Loads:
    def __init__(self, sem, pairs):
        self.copies = {}
        for n, (name, (src, dst)) in enumerate(pairs.items()):
            self.copies[name] = pltpu.make_async_copy(src, dst, sem.at[n])
            self.copies[name].start()

    def need(self, *names):
        for name in names:
            if name != "targets":
                self.copies[name].wait()

    def pump(self):
        pass

    def between(self, k):
        pass


class Store:
    def __init__(self, grads_ref, low_ref, stage, stage_low, sem):
        self.refs = (grads_ref, low_ref)
        self.stages = (stage, stage_low)
        self.sem = sem
        self.copies = []

    def put(self, mat, value):
        side = len(self.copies) % 2
        if len(self.copies) >= 2:
            for copy in self.copies[-2]:
                copy.wait()
        copies = []
        for n, (ref, stage) in enumerate(zip(self.refs, self.stages)):
            stage[side] = value.astype(stage.dtype)
            copies.append(pltpu.make_async_copy(stage.at[side], ref.at[mat], self.sem.at[side, n]))
            copies[-1].start()
        self.copies.append(copies)

    def pause(self):
        pass

    def finish(self):
        for copies in self.copies[-2:]:
            for copy in copies:
                copy.wait()


class Reduce:
    def __init__(self, plan, spot, refs, sems):
        self.plan, self.spot = plan, spot
        self.acc, self.low, self.twin_in, self.plane_out, self.plane_in = refs[:5]
        self.hop_out, self.hop_in, self.own = refs[5:]
        self.twin_send, self.twin_recv, self.plane_send, self.plane_recv = sems[:4]
        self.hop_send, self.hop_recv = sems[4:]
        self.batch, self.phase = -1, 0
        self.batches = []
        self.twins, self.planes, self.hops = {}, {}, {}

    def follow(self, source):
        self.need, self.pump, self.between = source.need, source.pump, source.between

    def put(self, mat, value):
        size = self.acc.shape[0]
        if not self.batches or len(self.batches[-1]) == size:
            self.batches.append([])
            self.batch, self.phase = len(self.batches) - 1, 0
            if self.batch:
                for copy in self.twins[self.batch - 1]:
                    copy.wait_send()
            self.twins[self.batch] = []
        slot = len(self.batches[-1])
        self.batches[-1].append(mat)
        rows, width = self.acc.shape[-2:]
        halves = value.reshape(-1, 2, rows, width)
        first = self.spot.core == 0
        shape = self.acc.shape[1:]
        self.acc[slot] = jnp.where(first, halves[:, 0], halves[:, 1]).reshape(shape)
        theirs = jnp.where(first, halves[:, 1], halves[:, 0]).reshape(shape)
        self.low[slot] = theirs.astype(self.low.dtype)
        side = self.batch % 2
        copy = remote(
            self.low.at[slot],
            self.twin_in.at[side, slot],
            self.twin_send.at[slot],
            self.twin_recv.at[side, slot],
            self.spot.sibling(),
        )
        copy.start()
        self.twins[self.batch].append(copy)

    def pause(self):
        self.phase += 1
        self.advance(self.phase)

    def index(self, fixed):
        return tuple(fixed.get(b, slice(None)) for b in range(self.plan.bits - 1, -1, -1))

    def advance(self, phase):
        spot, bits = self.spot, self.plan.bits
        size = self.acc.shape[0]
        batch = self.batch
        rows, width = self.acc.shape[-2:]
        if phase == 1:
            for copy in self.twins[batch]:
                copy.wait_recv()
            side = batch % 2

            def body(n, _):
                slot, item = n // MICRO, n % MICRO
                self.acc[slot, item] += self.twin_in[side, slot, item].astype(jnp.float32)
                return 0

            lax.fori_loop(0, size * MICRO, body, 0)
        elif phase <= bits + 1:
            self.add(batch, phase - 2)
        if phase <= bits:
            self.send(batch, phase - 1)
        elif phase == bits + 1:
            if batch:
                for copy in self.hops[batch - 1]:
                    copy.wait_send()
            self.hops[batch] = []
            mine = self.index({b: spot.bit(b) for b in range(bits)})
            for slot, mat in enumerate(self.batches[batch]):
                self.own[mat] = self.acc[(slot, spot.z) + mine]
                for d in range(1, MICRO):
                    value = self.acc[(slot, (spot.z + d) % MICRO) + mine]
                    self.hop_out[d - 1, slot] = value.astype(self.hop_out.dtype)
            for d in range(1, MICRO):
                copy = remote(
                    self.hop_out.at[d - 1],
                    self.hop_in.at[batch, d - 1],
                    self.hop_send.at[d - 1],
                    self.hop_recv.at[batch, d - 1],
                    spot.peer_z(d),
                )
                copy.start()
                self.hops[batch].append(copy)

    def steps(self, t, d):
        bits = self.plan.bits
        count = 1 << (bits - 1 - t)
        at = sum(1 << (bits - 1 - s) for s in range(t))
        done = [(d + s) % bits for s in range(t)]
        return (d + t) % bits, done, at, count

    def send(self, batch, t):
        spot = self.spot
        size = self.acc.shape[0]
        rows, width = self.acc.shape[-2:]
        for d in range(MICRO):
            b, done, at, count = self.steps(t, d)
            if batch:
                self.planes[batch - 1, t, d].wait_send()
            item = (spot.z + d) % MICRO
            fixed = {n: spot.bit(n) for n in done}
            fixed[b] = 1 - spot.bit(b)
            theirs = self.index(fixed)

            def body(slot, _):
                value = self.acc[(slot, item) + theirs].reshape(count, rows, width)
                self.plane_out[d, slot, at : at + count] = value.astype(self.plane_out.dtype)
                return 0

            lax.fori_loop(0, size, body, 0)
            where = (d, slice(None), pl.ds(at, count))
            copy = remote(
                self.plane_out.at[where],
                self.plane_in.at[(batch,) + where],
                self.plane_send.at[t, d],
                self.plane_recv.at[batch, t, d],
                spot.peer_bit(b),
            )
            copy.start()
            self.planes[batch, t, d] = copy

    def add(self, batch, t):
        spot = self.spot
        size = self.acc.shape[0]
        for d in range(MICRO):
            b, done, at, count = self.steps(t, d)
            self.planes[batch, t, d].wait_recv()
            item = (spot.z + d) % MICRO
            mine = self.index({n: spot.bit(n) for n in done + [b]})

            def body(slot, _):
                where = (slot, item) + mine
                value = self.acc[where]
                came = self.plane_in[batch, d, slot, at : at + count].astype(jnp.float32)
                self.acc[where] = value + came.reshape(value.shape)
                return 0

            lax.fori_loop(0, size, body, 0)

    def finish(self):
        for phase in range(self.phase + 1, self.plan.bits + 2):
            self.advance(phase)
        square = None
        for batch, mats in enumerate(self.batches):
            for copy in self.hops[batch]:
                copy.wait_recv()
            for slot, mat in enumerate(mats):
                value = self.own[mat]
                for d in range(MICRO - 1):
                    value = value + self.hop_in[batch, d, slot].astype(jnp.float32)
                self.own[mat] = value
                square = value * value if square is None else square + value * value
        last = len(self.batches) - 1
        for copy in self.twins[last] + self.hops[last]:
            copy.wait_send()
        for t in range(self.plan.bits):
            for d in range(MICRO):
                self.planes[last, t, d].wait_send()
        return square


def add_up(plan, spot, tile, refs, sems):
    send, recv = sems

    def exchange(tile, buffer, index, targets, at):
        buffer[index] = tile
        copies = []
        for n, to in enumerate(targets):
            copies.append(remote(buffer.at[index], buffer.at[index], send.at[at + n], recv.at[at + n], to))
            copies[-1].start()
        for copy in copies:
            copy.wait()
        total = buffer[0]
        for n in range(1, buffer.shape[0]):
            total = total + buffer[n]
        return total

    chips = plan.chips
    plane = [spot.in_plane((spot.p + d) % chips, spot.core) for d in range(1, chips)]
    plane += [spot.in_plane((spot.p + d) % chips, 1 - spot.core) for d in range(chips)]
    tile = exchange(tile, refs[0], 2 * spot.p + spot.core, plane, 0)
    return exchange(tile, refs[1], spot.z, [spot.peer_z(d) for d in range(1, MICRO)], 2 * chips - 1)


def fold_rows(square, lanes):
    square = jnp.sum(square, axis=0, keepdims=True)
    return sum(square[:, n : n + lanes] for n in range(0, square.shape[1], lanes))


def network_scratch(shapes):
    low, full = jnp.bfloat16, jnp.float32
    mesh_rows, grid_rows, width, lanes = shapes
    mesh_pair, grid_pair = (2, mesh_rows, width), (2, grid_rows, width)
    return [
        pltpu.VMEM((4,) + grid_pair[1:], low),
        pltpu.VMEM(grid_pair, full),
        pltpu.VMEM((3, 4) + mesh_pair[1:], low),
        pltpu.VMEM(mesh_pair, full),
        pltpu.VMEM((2,) + mesh_pair, full),
        pltpu.VMEM((3,) + mesh_pair, low),
        pltpu.VMEM((width, lanes), full),
        pltpu.VMEM(mesh_pair, low),
        pltpu.VMEM(mesh_pair, low),
        pltpu.VMEM(mesh_pair, low),
        pltpu.VMEM(mesh_pair, low),
        pltpu.VMEM(mesh_pair, low),
        pltpu.VMEM((128, width), full),
        pltpu.VMEM((8, width), full),
        pltpu.SemaphoreType.DMA((6, 2)),
        pltpu.SemaphoreType.DMA((6, 2)),
    ]


def reduce_scratch(plan, mats, rows, width):
    low, full = jnp.bfloat16, jnp.float32
    dma = pltpu.SemaphoreType.DMA
    batches, size = mats // 3, 3
    piece = (MICRO,) + (2,) * plan.bits + (rows, width)
    steps = (1 << plan.bits) - 1
    return [
        pltpu.VMEM((size,) + piece, full),
        pltpu.VMEM((size,) + piece, low),
        pltpu.VMEM((2, size) + piece, low),
        pltpu.VMEM((MICRO, size, steps, rows, width), low),
        pltpu.VMEM((batches, MICRO, size, steps, rows, width), low),
        pltpu.VMEM((MICRO - 1, size, rows, width), low),
        pltpu.VMEM((batches, MICRO - 1, size, rows, width), low),
    ], [
        dma((size,)),
        dma((2, size)),
        dma((plan.bits, MICRO)),
        dma((batches, plan.bits, MICRO)),
        dma((MICRO - 1,)),
        dma((batches, MICRO - 1)),
    ]


def load_pairs(ins, wts, cells, halo, graphs):
    pack_ref, cells_ref, halo_ref, *graph_refs = ins
    last = wts.shape[0] - 1
    pairs = {"last": (pack_ref.at[SLOTS[last]], wts.at[SLOTS[last]]), "halo": (halo_ref, halo), "cells": (cells_ref, cells)}

    def mats(*names):
        for n in names:
            pairs[n] = (pack_ref.at[SLOTS[n]], wts.at[SLOTS[n]])

    pairs["enc"] = (graph_refs[0], graphs[0])
    mats(0, 7)
    pairs["proc"] = (graph_refs[1], graphs[1])
    mats(1, 4, 8, 2, 5, 9)
    pairs["dec"] = (graph_refs[2], graphs[2])
    mats(3, 6, 10)
    return pairs


def train_kernel(plan, variables, *refs):
    ins, refs = refs[:6], refs[6:]
    outs, refs = refs[:3], refs[3:]
    data, refs = refs[:6], refs[6:]
    work, refs = refs[:16], refs[16:]
    load_sem, refs = refs[0], refs[1:]
    wts, cells, halo, *graphs = data
    spot = Spot(plan)
    loads = Loads(load_sem, load_pairs(ins, wts, cells, halo, graphs))
    spot.meet()
    hooks = Store(outs[0], outs[1], *refs)
    hooks.need, hooks.pump, hooks.between = loads.need, loads.pump, loads.between
    network(plan, spot, variables, hooks, outs[2], Matrices(wts), *data[1:], *work)
    hooks.finish()


def train(plan, variables, pack, cells, halo, encoder, processor, decoder):
    mats, width = pack.shape[0], pack.shape[2]
    lanes = halo.shape[-1]
    any_space = pl.BlockSpec(memory_space=pl.ANY)
    vmem = pl.BlockSpec(memory_space=pltpu.VMEM)
    dma = pltpu.SemaphoreType.DMA
    low, full = jnp.bfloat16, jnp.float32
    stats = jax.ShapeDtypeStruct((8, 128), full)
    out_shape = (jax.ShapeDtypeStruct(pack.shape, full), jax.ShapeDtypeStruct(pack.shape, low), stats)
    out_specs = (any_space, any_space, vmem)
    more = [pltpu.VMEM((2, width, width), full), pltpu.VMEM((2, width, width), low), dma((2, 2))]
    ins = (pack, cells, halo, encoder, processor, decoder)
    shapes = (encoder.shape[1], decoder.shape[1], width, lanes)
    return pl.pallas_call(
        functools.partial(train_kernel, plan, variables),
        out_shape=out_shape,
        in_specs=[any_space] * 6,
        out_specs=out_specs,
        scratch_shapes=[pltpu.VMEM(value.shape, low) for value in ins]
        + network_scratch(shapes)
        + [dma((mats + 5,))]
        + more,
        compiler_params=pltpu.CompilerParams(
            collective_id=2, has_side_effects=True, vmem_limit_bytes=63 << 20
        ),
        name="train",
    )(*ins)


PLAN = (
    (("cells", 0),),
    (("hop", 1), ("cells", 1),),
    (("cells", 2), ("cells", 3), ("stage", 0, 0), ("hop", 2)),
    (("stage", 0, 1), ("stage", 1, 0)),
    (("stage", 0, 2), ("stage", 1, 1), ("hop", 3)),
    (("stage", 2, 0), ("stage", 1, 2), ("hop", "targets")),
    (("stage", 2, 1), ("stage", 3, 0)),
    (("stage", 2, 2), ("stage", 3, 1)),
    (("stage", 3, 2), ("targets", 0)),
    (("targets", 1), ("targets", 2), ("targets", 3)),
)


class Gather:
    def __init__(self, plan, spot, shapes, ins, data, bufs, sems):
        self.plan, self.spot, self.shapes = plan, spot, shapes
        self.pack, self.cells_in, self.codes_in = ins
        self.wts, self.cells, self.halo, *self.graphs = data
        self.codes, self.code_hop, self.cell_hop, self.sums = bufs
        self.own_sem, self.hop_send, self.hop_recv, self.plane_send, self.plane_recv = sems[:5]
        self.twin_send, self.twin_recv, self.move_send, self.move_recv = sems[5:]
        self.size = 3
        self.parts = self.wts.shape[0] // self.size
        self.half = self.cells_in.shape[1]
        self.lanes = self.halo.shape[-1]
        self.sent, self.hops, self.planes, self.twins, self.moves = [], {}, {}, {}, []
        self.todo, self.done = [], set()
        z, p, core = spot.z, spot.p, spot.core
        block = p % 4
        self.bb, self.to_core = block % 2, block // 2

    def mats(self, part):
        return pl.ds(part * self.size, self.size)

    def region(self, part, z, done):
        return (self.mats(part), z) + self.spot.held(done) + (self.spot.core,)

    def wide(self, n):
        return pl.ds(n * self.lanes, self.lanes)

    def hop_slot(self, d, n):
        ref, first = self.cell_hop[d - 1]
        return ref.at[pl.ds(first, self.half), self.wide(n)]

    def code_part(self):
        size = self.code_hop.shape[1]
        return pl.ds(pl.multiple_of(self.spot.core * size, 8), size)

    def start(self):
        spot = self.spot
        every = self.region(0, spot.z, ())[1:]
        self.own = pltpu.make_async_copy(self.pack, self.wts.at[(slice(None),) + every], self.own_sem)
        self.own.start()
        spot.meet()
        self.jobs = ["codes", "cells", 0, 1, 2, 3, "targets"]
        for job in self.jobs[:3]:
            self.hop(job)
        for d in range(MICRO):
            if d:
                self.hops["codes", d].wait_recv()
                codes = self.code_hop.at[d - 1]
            else:
                codes = self.codes_in.at[self.code_part()]
            chip, _ = self.places(d)
            dst = self.codes.at[self.bb, self.code_part()]
            self.move(0, d, codes, dst, self.bb * 2 + spot.core, chip, self.to_core)
        self.own.wait()
        for group in PLAN:
            actions = []
            for kind, *more in group:
                action = {"cells": self.move_cells, "targets": self.move_targets, "hop": self.hop}.get(kind, self.stage)
                actions.append(((kind, *more), functools.partial(action, *more)))
            self.todo.append(actions)

    def hop(self, job):
        spot = self.spot
        every = self.region(0, spot.z, ())[1:]
        n = self.jobs.index(job)
        for d in range(1, MICRO):
            m = (spot.z + d) % MICRO
            if job == "codes":
                pair = self.codes_in.at[self.code_part()], self.code_hop.at[d - 1]
            elif job == "cells":
                pair = self.cells_in.at[m, :, self.wide(0)], self.hop_slot(d, 0)
            elif job == "targets":
                pair = self.cells_in.at[m, :, self.wide(1)], self.hop_slot(d, 1)
            else:
                pair = self.pack.at[self.mats(job)], self.wts.at[(self.mats(job),) + every]
            copy = remote(*pair, self.hop_send.at[d - 1, n], self.hop_recv.at[d - 1, n], spot.peer_z(d))
            copy.start()
            self.hops[job, d] = copy
            self.sent.append(copy)

    def places(self, d):
        chips = self.plan.chips
        j = (((self.spot.z - d) % MICRO) * chips + self.spot.p) // 4
        q = (2 * j + self.to_core + 2 * self.bb - 1) % (2 * chips)
        return walk(j, self.plan.width), (walk(q // 2, self.plan.width), q % 2)

    def move(self, kind, d, src, dst, slot, chip, to_core):
        spot = self.spot
        here = jnp.logical_and(chip == spot.p, to_core == spot.core)
        sem = self.move_recv.at[kind, slot]
        copy = remote(src, dst, self.move_send.at[kind, d], sem, spot.in_plane(chip, to_core))

        @pl.when(here)
        def _():
            pltpu.make_async_copy(src, dst, sem).start()

        @pl.when(jnp.logical_not(here))
        def _():
            copy.start()

        self.moves.append((here, copy))

    def rows(self, bb, core):
        return pl.ds(pl.multiple_of((bb * 2 + core) * self.half, 16), self.half)

    def move_cells(self, d):
        if d:
            self.hops["cells", d].wait_recv()
            src = self.hop_slot(d, 0)
        else:
            src = self.cells_in.at[self.spot.z, :, self.wide(0)]
        core = self.spot.core
        chip, near = self.places(d)
        side = 1 - self.bb
        dst = self.halo.at[side, pl.ds(pl.multiple_of(core * self.half, 16), self.half)]
        self.move(1, d, src, dst, side * 2 + core, *near)
        dst = self.cells.at[self.rows(self.bb, core), self.wide(0)]
        self.move(2, d, src, dst, self.bb * 2 + core, chip, self.to_core)

    def move_targets(self, d):
        if d:
            self.hops["targets", d].wait_recv()
            src = self.hop_slot(d, 1)
        else:
            src = self.cells_in.at[self.spot.z, :, self.wide(1)]
        core = self.spot.core
        chip, _ = self.places(d)
        dst = self.cells.at[self.rows(self.bb, core), self.wide(1)]
        self.move(3, d, src, dst, self.bb * 2 + core, chip, self.to_core)

    def moved(self, kind):
        for n in range(4):
            side, core = n // 2, n % 2
            if kind == 0:
                size = self.code_hop.shape[1]
                dst = self.codes.at[side, pl.ds(core * size, size)]
            elif kind == 1:
                dst = self.halo.at[side, pl.ds(core * self.half, self.half)]
            else:
                dst = self.cells.at[pl.ds(n * self.half, self.half), self.wide(kind - 2)]
            pltpu.make_async_copy(dst, dst, self.move_recv.at[kind, n]).wait()

    def stage(self, part, t):
        bits, spot = self.plan.bits, self.spot
        for d in range(MICRO):
            u = part * MICRO + d
            if t:
                self.planes[u, t - 1].wait_recv()
            elif d:
                self.hops[part, d].wait_recv()
            order = [(part + d + s) % bits for s in range(bits)]
            where = self.wts.at[self.region(part, (spot.z - d) % MICRO, order[:t])]
            if t < bits:
                to = spot.peer_bit(order[t])
                copy = remote(where, where, self.plane_send.at[u, t], self.plane_recv.at[u, t], to)
                self.planes[u, t] = copy
            else:
                copy = remote(where, where, self.twin_send.at[u], self.twin_recv.at[u], spot.sibling())
                self.twins[u] = copy
            copy.start()
            self.sent.append(copy)

    def pump(self):
        if self.todo:
            for name, action in self.todo.pop(0):
                action()
                self.done.add(name)

    def until(self, name):
        while name not in self.done:
            self.pump()

    def need(self, *names):
        for name in names:
            if name in ("enc", "proc", "dec"):
                continue
            if name == "cells":
                self.until(("cells", MICRO - 1))
                self.moved(2)
            elif name == "halo":
                self.until(("cells", MICRO - 1))
                self.moved(1)
            elif name == "targets":
                pass
            else:
                mat = self.wts.shape[0] - 1 if name == "last" else name
                part = SLOTS[mat] // self.size
                if ("part", part) in self.done:
                    continue
                self.until(("stage", part, self.plan.bits))
                for d in range(MICRO):
                    self.twins[part * MICRO + d].wait_recv()
                self.done.add(("part", part))

    def build(self, n, block, tiles, sums):
        first, edges, rows, columns = self.shapes[n]
        chunk = math.gcd(edges, 1024) // 128
        width = self.sums.shape[-1]
        spans = [(tile * width, min(width, columns - tile * width)) for tile in tiles]

        def ones(row, count):
            place = lax.broadcasted_iota(jnp.int32, (count, 128), 0).astype(jnp.int16)
            hit = place == row.astype(jnp.int16)
            return jnp.where(hit, jnp.bfloat16(1), jnp.bfloat16(0)).astype(jnp.float8_e4m3fn)

        def area(at, size):
            return at + (pl.ds(0, rows), pl.ds(0, size))

        for at, (_, size) in zip(sums, spans):
            self.sums[area(at, size)] = jnp.zeros((rows, size), jnp.float32)

        def body(k, _):
            codes = [self.codes[block, pl.ds(first + k * chunk + i, 1), :] for i in range(chunk)]
            into = jnp.concatenate([ones(code >> CODE_BITS, rows) for code in codes], axis=1)
            for at, (start, size) in zip(sums, spans):
                out = [ones((code & ((1 << CODE_BITS) - 1)) - start, size) for code in codes]
                self.sums[area(at, size)] += right_dot(into, jnp.concatenate(out, axis=1))
            return 0

        lax.fori_loop(0, edges // (128 * chunk), body, 0)
        for at, (start, size) in zip(sums, spans):
            self.graphs[n][block, :, start : start + size] = self.sums[area(at, size)].astype(jnp.bfloat16)

    def prepare(self):
        self.moved(0)
        width = self.sums.shape[-1]
        every = [(0, 0), (0, 1), (1, 0), (1, 1)]
        for n, block in ((0, 0), (0, 1), (1, 0), (1, 1)):
            tiles = list(range(-(-self.shapes[n][3] // width)))
            for turn in range(0, len(tiles), 4 - 2 * n):
                some = tiles[turn : turn + 4 - 2 * n]
                self.build(n, block, some, every[: len(some)])
                self.pump()

    def between(self, k):
        if k == 2:
            self.until(("targets", MICRO - 1))
            for here, copy in self.moves:

                @pl.when(jnp.logical_not(here))
                def _():
                    copy.wait_send()

            self.moves = []
            self.moved(3)
        if k in (1, 2):
            width = self.sums.shape[-1]
            tiles = list(range(-(-self.shapes[2][3] // width)))
            for n in range(0, len(tiles), 2):
                self.build(2, k - 1, tiles[n : n + 2], [(1, 0), (1, 1)])
                self.pump()

    def finish(self):
        for copy in self.sent:
            copy.wait_send()


def step_kernel(plan, variables, shapes, *refs):
    ins, refs = refs[:3], refs[3:]
    share_ref, total_ref, refs = refs[0], refs[1], refs[2:]
    data, refs = refs[:6], refs[6:]
    work, refs = refs[:16], refs[16:]
    reduce_refs, reduce_sems, refs = refs[:7], refs[7:13], refs[13:]
    tiles, tile_sems, refs = refs[:2], refs[2:4], refs[4:]
    codes, code_hop, stats, *sems = refs
    wts, cells, halo, *graphs = data
    ext, pre = work[2], work[4]
    half = ins[1].shape[1]
    cell_hop = [(ext.at[2, 1], 0), (ext.at[2, 1], half), (ext.at[2, 2], 0)]
    spot = Spot(plan)
    gather = Gather(plan, spot, shapes, ins, data, (codes, code_hop, cell_hop, pre), sems)
    gather.start()
    gather.prepare()
    hooks = Reduce(plan, spot, (*reduce_refs, share_ref), reduce_sems)
    hooks.follow(gather)
    network(plan, spot, variables, hooks, stats, Matrices(wts), *data[1:], *work)
    square = fold_rows(hooks.finish(), stats.shape[1])
    row = lax.broadcasted_iota(jnp.int32, stats.shape, 0)
    tile = jnp.where(row == 0, square, stats[...])
    total_ref[...] = add_up(plan, spot, tile, tiles, tile_sems)
    gather.finish()


def step(plan, variables, shapes, pack, cells, codes):
    mats, rows, width = pack.shape
    _, half, lanes = cells.shape
    lanes //= 2
    chips, bits = plan.chips, plan.bits
    low, full = jnp.bfloat16, jnp.float32
    any_space = pl.BlockSpec(memory_space=pl.ANY)
    vmem = pl.BlockSpec(memory_space=pltpu.VMEM)
    dma = pltpu.SemaphoreType.DMA
    stats = jax.ShapeDtypeStruct((8, 128), full)
    buffers, sems = reduce_scratch(plan, mats, rows, width)
    mesh_rows, grid_rows = shapes[0][2], shapes[2][2]
    units = mats // 3 * MICRO
    return pl.pallas_call(
        functools.partial(step_kernel, plan, variables, shapes),
        out_shape=(jax.ShapeDtypeStruct((mats, rows, width), full), stats),
        in_specs=[any_space] * 3,
        out_specs=(vmem, vmem),
        scratch_shapes=[
            pltpu.VMEM((mats, MICRO) + (2,) * bits + (2, rows, width), low),
            pltpu.VMEM((4 * half, 2 * lanes), low),
            pltpu.VMEM((2, 2 * half, lanes), low),
        ]
        + [pltpu.VMEM((2,) + shape[2:], low) for shape in shapes]
        + network_scratch((mesh_rows, grid_rows, width, lanes))
        + buffers
        + sems
        + [pltpu.VMEM((n,) + stats.shape, full) for n in (2 * chips, MICRO)]
        + [dma((MICRO + 2 * chips - 2,))] * 2
        + [
            pltpu.VMEM((2,) + codes.shape, codes.dtype),
            pltpu.VMEM((MICRO - 1, codes.shape[0] // 2, codes.shape[1]), codes.dtype),
            pltpu.VMEM(stats.shape, full),
            dma,
            dma((MICRO - 1, 7)),
            dma((MICRO - 1, 7)),
            dma((units, bits)),
            dma((units, bits)),
            dma((units,)),
            dma((units,)),
            dma((4, MICRO)),
            dma((4, 4)),
        ],
        compiler_params=pltpu.CompilerParams(
            collective_id=3, has_side_effects=True, vmem_limit_bytes=63 << 20
        ),
        name="step",
    )(pack, cells, codes)


def adamw(param, first, second, grad, scale, rate):
    clipped = grad * scale
    moment = BETA_ONE * first + (1.0 - BETA_ONE) * clipped
    square = BETA_TWO * second + (1.0 - BETA_TWO) * clipped * clipped
    fixed_one = moment / (1.0 - BETA_ONE**STEP)
    fixed_two = square / (1.0 - BETA_TWO**STEP)
    fresh = param - rate * (fixed_one / (jnp.sqrt(fixed_two) + EPS_ADAM) + DECAY * param)
    return (fresh, moment, square, fresh.astype(jnp.bfloat16))


def on_device(
    plan,
    grid_in,
    targets,
    area_weight,
    grid_count,
    g2m_edges,
    mesh_edges,
    m2g_edges,
    edge_count,
    embed_weight,
    embed_first,
    embed_second,
    node_mats,
    mats_first,
    mats_second,
    head_weight,
    head_first,
    head_second,
    norm_gains,
    gains_first,
    gains_second,
):
    half, variables = grid_in.shape[1:]
    grid_rows = 2 * half
    mesh_rows = M_DEV
    lanes = -(-variables // 128) * 128
    core = lax.axis_index("feat")

    position = core * half + jnp.arange(half, dtype=jnp.int32)
    weights = jnp.where(position[None, :] < grid_count, area_weight, 0.0)
    pieces = []
    rest = weights
    for _ in range(3):
        piece = lax.reduce_precision(rest, 8, 7)
        pieces.append(piece.astype(jnp.bfloat16))
        rest = rest - piece
    cells = jnp.concatenate(
        [
            jnp.pad(grid_in, ((0, 0), (0, 0), (0, lanes - variables))),
            targets,
            jnp.pad(jnp.stack(pieces, axis=-1), ((0, 0), (0, 0), (0, lanes - variables - 3))),
        ],
        axis=-1,
    )
    last = jnp.concatenate(
        [
            jnp.pad(embed_weight.T, ((0, 0), (0, lanes - variables))),
            head_weight,
            jnp.pad(norm_gains.T, ((0, 0), (0, lanes - variables - 4))),
        ],
        axis=-1,
    )
    order = sorted(SLOTS, key=SLOTS.get)
    mats = [last if n == len(order) - 1 else node_mats[n] for n in order]
    pack = jnp.stack(mats).astype(jnp.bfloat16)
    graphs = ((g2m_edges, grid_rows, mesh_rows), (mesh_edges, mesh_rows, mesh_rows), (m2g_edges, mesh_rows, grid_rows))
    codes, shapes = [], []
    first = 0
    for n, (edges, columns, rows) in enumerate(graphs):
        per = edges.shape[1]
        alive = jnp.arange(per, dtype=jnp.int32) < edge_count[n, 0]
        codes.append(jnp.where(alive, edges[1] * (1 << CODE_BITS) + edges[0], -1))
        shapes.append((first // 128, per, rows, 3 * columns))
        first += per
    codes = jnp.concatenate(codes).reshape(-1, 128)
    rows, width = pack.shape[1:]
    if rows % 16 == 0 and plan.bits == 2:
        share, total = step(plan, variables, shapes, pack, cells, codes)
    else:
        gathered, main, halo, *counts = gather_all(plan, shapes, pack, cells, codes)
        full = gathered.reshape(-1, width, width)
        main = main.reshape(-1, 2 * lanes)
        halo = halo.reshape(2, grid_rows, lanes)
        grads, low, stats = train(plan, variables, full, main, halo, *counts)
        share, total = reduce_all(plan, grads.reshape(gathered.shape), low.reshape(gathered.shape), stats)
    square_sum, loss_sum, weight_sum = (jnp.sum(total[n]) for n in range(3))
    shares = (
        share[-1, :, :variables].T,
        share[:-1],
        share[-1, :, lanes : lanes + variables],
        share[-1, :, lanes + variables : lanes + variables + 4].T,
    )
    grad_norm = jnp.sqrt(square_sum)
    scale = jnp.minimum(1.0, CLIP / (grad_norm + 1e-06))
    return (
        loss_sum,
        weight_sum,
        grad_norm,
        *adamw(embed_weight, embed_first, embed_second, shares[0], scale, RATE),
        *adamw(node_mats, mats_first, mats_second, shares[1], scale, RATE),
        *adamw(head_weight, head_first, head_second, shares[2], scale, RATE),
        *adamw(norm_gains, gains_first, gains_second, shares[3], scale, GAIN_RATE),
    )


def solution(mesh):
    plan = Plan(mesh.shape["nodes"])
    cells = P(None, BOTH, None)
    columns = P(None, BOTH)
    rows = P(BOTH, None)
    blocks = P(None, "nodes")
    return jax.shard_map(
        lambda *args: on_device(plan, *args),
        mesh=mesh,
        in_specs=(
            (cells, cells, columns, blocks, blocks, blocks, blocks, blocks)
            + (columns,) * 3
            + (cells,) * 3
            + (rows,) * 3
            + (columns,) * 3
        ),
        out_specs=(P(), P(), P()) + (columns,) * 4 + (cells,) * 4 + (rows,) * 4 + (columns,) * 4,
        check_vma=False,
    )
```
